256 devices in a mesh: gx: 8 (over y, core), gy: 8 (over z_lo, x), gz: 4 (over z_hi).
Axes of the slice: x: 4, y: 4, z: 8 (z_hi: 4, z_lo: 2; z = z_hi * 2 + z_lo), core: 2. Of those that a mesh axis runs over, the one named last changes fastest.
Arguments:
- distribution_functions: float32 [27, 64, 64, 512], P(None, 'gx', 'gy', 'gz'), as said below
- gaseous_thermal_state: float32 [64, 64, 512], P('gx', 'gy', 'gz'), may hold values from 0.8 to 1.2
- moisture_fraction: float32 [64, 64, 512], P('gx', 'gy', 'gz'), may hold values from 0 to 0.2
- parcel_lowest_node: int32 [3, 8, 8, 4, 2048], P(None, 'gx', 'gy', 'gz'), may hold values from -1 to 127, as said below
- parcel_fractional_shift: float32 [3, 8, 8, 4, 2048], P(None, 'gx', 'gy', 'gz'), may hold values from 0 to 1
- parcel_motion: float32 [3, 8, 8, 4, 2048], P(None, 'gx', 'gy', 'gz'), may hold values from -0.8 to 0.8
- parcel_thermal_state: float32 [8, 8, 4, 2048], P('gx', 'gy', 'gz'), may hold values from 0.3 to 0.7
- parcel_relaxation_factor: float32 [8, 8, 4, 2048], P('gx', 'gy', 'gz'), may hold values from 0.05 to 0.5
- parcel_live_number: int32 [8, 8, 4], P('gx', 'gy', 'gz'), may hold values from 128 to 2048, as said below
Outputs:
- distribution_functions_next: float32 [27, 64, 64, 512], P(None, 'gx', 'gy', 'gz')
- temperature_out: float32 [64, 64, 512], P('gx', 'gy', 'gz')
- vapour_out: float32 [64, 64, 512], P('gx', 'gy', 'gz')
- parcel_motion_after_drag: float32 [3, 8, 8, 4, 2048], P(None, 'gx', 'gy', 'gz')
The draws below stay inside these ranges and needn't reach their ends.
Inputs may be any that keep to these rules, and one draw needn't show every extreme that they name: `parcel_lowest_node`: row 0 lies in -1 to 7, row 1 in -1 to 7, row 2 in -1 to 127. `parcel_live_number`: every count is a multiple of 128 and at least 128; some block holds exactly 2048 live droplets. `distribution_functions`: every population is positive.
All inputs are finite; a program needn't handle non-finite values.
Results may differ from the reference program's by a relative error of at most 0.000078.
Values sent between devices are 32-bit elements; how exact they have to be, the bound alone decides.
A program may use at most 64 MiB of HBM per device.

```python
import math
import jax
import jax.numpy as jnp

CX = 8
CY = 8
CZ = 128
TILE = 128
DROP_TILES = 16
PARCEL_LIMIT = 2048
PATCHES_FIRST = 8
PATCHES_SECOND = 8
PATCHES_THIRD = 4
MESH_NODES_FIRST = 64
MESH_NODES_SECOND = 64
MESH_NODES_THIRD = 512


def draw_distribution_functions(key, part):
    labels = jnp.arange(27, dtype=jnp.int32)
    offsets = jnp.stack([labels // 9 - 1, labels // 3 % 3 - 1, labels % 3 - 1]).astype(jnp.float32)
    single = jnp.where(offsets == 0.0, 2.0 / 3.0, 1.0 / 6.0)
    weights = (single[0] * single[1] * single[2]).reshape(27, 1, 1, 1)
    ratio = 1.0 + 0.25 * jnp.clip(jax.random.normal(key, (27, MESH_NODES_FIRST, MESH_NODES_SECOND, MESH_NODES_THIRD), jnp.float32), -2.0, 2.0)
    return (weights * ratio).astype(jnp.float32)


def draw_parcel_lowest_node(key, part):
    grid_shape = (PATCHES_FIRST, PATCHES_SECOND, PATCHES_THIRD, PARCEL_LIMIT)
    first = jax.random.randint(jax.random.fold_in(key, 11), grid_shape, -1, CX)
    second = jax.random.randint(jax.random.fold_in(key, 12), grid_shape, -1, CY)
    third = jax.random.randint(jax.random.fold_in(key, 13), grid_shape, -1, CZ)
    return jnp.stack([first, second, third]).astype(jnp.int32)


def draw_parcel_live_number(key, part):
    blocks = PATCHES_FIRST * PATCHES_SECOND * PATCHES_THIRD
    spread = max(DROP_TILES - 1, 1)
    draws = jax.random.randint(jax.random.fold_in(key, 21), (blocks,), 0, DROP_TILES)
    tiles = 1 + draws * draws * (DROP_TILES - 1) // (spread * spread)
    fullest = jax.random.randint(jax.random.fold_in(key, 22), (), 0, blocks)
    tiles = jnp.where(jnp.arange(blocks, dtype=jnp.int32) == fullest, DROP_TILES, tiles)
    return (tiles * TILE).reshape(PATCHES_FIRST, PATCHES_SECOND, PATCHES_THIRD).astype(jnp.int32)


def levels(stream_key, extent, split, low, high):
    loudness = 1.0
    for axis_at, shards_of in split:
        heights = jax.random.uniform(jax.random.fold_in(jax.random.fold_in(stream_key, 6), axis_at), (shards_of,), jnp.float32, low / len(split), high / len(split))
        loudness = loudness * jnp.repeat(jnp.exp(heights), extent[axis_at] // shards_of).reshape((-1,) + (1,) * (len(extent) - 1 - axis_at))
    return loudness


def bell_draw(rng, shape, scale, bound, cuts=(), kind=jnp.bfloat16):
    values = jax.random.normal(rng, shape, jnp.float32) * scale
    if len(cuts) > 0:
        values = levels(rng, shape, cuts, -0.22, 0.18) * values
    return jnp.clip(values, min=-bound, max=bound).astype(kind)


def setup_inputs(seed: int = 0) -> dict:
    seeds = jax.random.split(jax.random.key(seed), 10)
    distribution_functions = draw_distribution_functions(jax.random.fold_in(seeds[9], 71), 0)
    gaseous_thermal_state = jnp.clip(0.8 + 0.40000004 * jax.random.uniform(seeds[1], (MESH_NODES_FIRST, MESH_NODES_SECOND, MESH_NODES_THIRD), jnp.float32) ** levels(seeds[1], (MESH_NODES_FIRST, MESH_NODES_SECOND, MESH_NODES_THIRD), ((0, 8), (1, 8), (2, 4)), -0.2, 0.2), 0.8, 1.2)
    moisture_fraction = jnp.clip(0.2 * jax.random.uniform(seeds[2], (MESH_NODES_FIRST, MESH_NODES_SECOND, MESH_NODES_THIRD), jnp.float32) ** levels(seeds[2], (MESH_NODES_FIRST, MESH_NODES_SECOND, MESH_NODES_THIRD), ((0, 8), (1, 8), (2, 4)), -0.2, 0.2), 0.0, 0.2)
    parcel_lowest_node = draw_parcel_lowest_node(jax.random.fold_in(seeds[9], 71), 0)
    parcel_fractional_shift = jnp.clip(1.0 * jax.random.uniform(seeds[4], (3, PATCHES_FIRST, PATCHES_SECOND, PATCHES_THIRD, PARCEL_LIMIT), jnp.float32) ** levels(seeds[4], (3, PATCHES_FIRST, PATCHES_SECOND, PATCHES_THIRD, PARCEL_LIMIT), ((1, 8), (2, 8), (3, 4)), -0.2, 0.2), 0.0, 1.0)
    parcel_motion = bell_draw(seeds[5], (3, PATCHES_FIRST, PATCHES_SECOND, PATCHES_THIRD, PARCEL_LIMIT), 0.2, 0.8, ((1, 8), (2, 8), (3, 4)), jnp.float32)
    parcel_thermal_state = jnp.clip(0.3 + 0.39999998 * jax.random.uniform(seeds[6], (PATCHES_FIRST, PATCHES_SECOND, PATCHES_THIRD, PARCEL_LIMIT), jnp.float32) ** levels(seeds[6], (PATCHES_FIRST, PATCHES_SECOND, PATCHES_THIRD, PARCEL_LIMIT), ((0, 8), (1, 8), (2, 4)), -0.2, 0.2), 0.3, 0.7)
    parcel_relaxation_factor = jnp.clip(jnp.exp(math.log(0.5) - 2.3025851 * jax.random.uniform(seeds[7], (PATCHES_FIRST, PATCHES_SECOND, PATCHES_THIRD, PARCEL_LIMIT), jnp.float32) ** levels(seeds[7], (PATCHES_FIRST, PATCHES_SECOND, PATCHES_THIRD, PARCEL_LIMIT), ((0, 8), (1, 8), (2, 4)), -0.2, 0.2)), 0.05, 0.5)
    parcel_live_number = draw_parcel_live_number(jax.random.fold_in(seeds[9], 71), 0)
    return {"distribution_functions": distribution_functions, "gaseous_thermal_state": gaseous_thermal_state, "moisture_fraction": moisture_fraction, "parcel_lowest_node": parcel_lowest_node, "parcel_fractional_shift": parcel_fractional_shift, "parcel_motion": parcel_motion, "parcel_thermal_state": parcel_thermal_state, "parcel_relaxation_factor": parcel_relaxation_factor, "parcel_live_number": parcel_live_number}


relax_time = 0.8
load_ratio = 2.0
thermal_exchange_factor = 1.0
equilibrium_vapor_factor = 0.05


def lattice_table():
    return [(label // 9 - 1, (label // 3) % 3 - 1, label % 3 - 1) for label in range(27)]


def lattice_weight(label):
    value = 1.0
    for step in lattice_table()[label]:
        value = value * (2.0 / 3.0 if step == 0 else 1.0 / 6.0)
    return value


def moments(distribution_functions):
    table = lattice_table()
    density = distribution_functions[0]
    for label in range(1, 27):
        density = density + distribution_functions[label]
    gaseous_motion = []
    for axis_num in range(3):
        total = jnp.zeros_like(density)
        for label in range(27):
            if table[label][axis_num] == 1:
                total = total + distribution_functions[label]
            elif table[label][axis_num] == -1:
                total = total - distribution_functions[label]
        gaseous_motion.append(total / density)
    return density, gaseous_motion


def relax_one(population, label, density, gaseous_motion, speed, feedback_terms_mesh):
    step_x, step_y, step_z = lattice_table()[label]
    weight = lattice_weight(label)
    along = float(step_x) * gaseous_motion[0] + float(step_y) * gaseous_motion[1] + float(step_z) * gaseous_motion[2]
    equil = weight * density * (1.0 + 3.0 * along + 4.5 * along * along - 1.5 * speed)
    push = float(step_x) * feedback_terms_mesh[0] + float(step_y) * feedback_terms_mesh[1] + float(step_z) * feedback_terms_mesh[2]
    return population - (population - equil) / relax_time + weight * (feedback_terms_mesh[4] + 3.0 * push)


def parcel_exchange_parts(interpolated, parcel_motion, parcel_thermal_state, parcel_relaxation_factor):
    increment = parcel_relaxation_factor[None] * (interpolated[0:3] - parcel_motion)
    thermal_exchange = thermal_exchange_factor * parcel_relaxation_factor * (parcel_thermal_state - interpolated[3])
    equilibrium_vapor = equilibrium_vapor_factor * jnp.exp(3.0 * (parcel_thermal_state - 0.5))
    mass = parcel_relaxation_factor * (equilibrium_vapor - interpolated[4])
    exchange_parts = jnp.concatenate([-load_ratio * increment, thermal_exchange[None], mass[None]], axis=0)
    return increment, exchange_parts


def tri_weight(frac, shift):
    return frac if shift == 1 else 1.0 - frac


def reference(distribution_functions, gaseous_thermal_state, moisture_fraction, parcel_lowest_node, parcel_fractional_shift, parcel_motion, parcel_thermal_state, parcel_relaxation_factor, parcel_live_number):
    density, gaseous_motion = moments(distribution_functions)
    moment_quantities = jnp.stack(gaseous_motion + [gaseous_thermal_state, moisture_fraction])
    slots = jnp.arange(PARCEL_LIMIT, dtype=jnp.int32).reshape(1, 1, 1, PARCEL_LIMIT)
    live = (slots < parcel_live_number[..., None]).astype(jnp.float32)
    anchor_x = jnp.arange(PATCHES_FIRST, dtype=jnp.int32).reshape(PATCHES_FIRST, 1, 1, 1) * CX + parcel_lowest_node[0]
    anchor_y = jnp.arange(PATCHES_SECOND, dtype=jnp.int32).reshape(1, PATCHES_SECOND, 1, 1) * CY + parcel_lowest_node[1]
    anchor_z = jnp.arange(PATCHES_THIRD, dtype=jnp.int32).reshape(1, 1, PATCHES_THIRD, 1) * CZ + parcel_lowest_node[2]
    interpolated = jnp.zeros((5,) + live.shape, jnp.float32)
    spots = []
    for corner in range(8):
        shift_x, shift_y, shift_z = corner // 4, (corner // 2) % 2, corner % 2
        cell_x = ((anchor_x + shift_x) % MESH_NODES_FIRST).astype(jnp.int32)
        cell_y = ((anchor_y + shift_y) % MESH_NODES_SECOND).astype(jnp.int32)
        cell_z = ((anchor_z + shift_z) % MESH_NODES_THIRD).astype(jnp.int32)
        weight = tri_weight(parcel_fractional_shift[0], shift_x) * tri_weight(parcel_fractional_shift[1], shift_y) * tri_weight(parcel_fractional_shift[2], shift_z)
        interpolated = interpolated + weight[None] * moment_quantities[:, cell_x, cell_y, cell_z]
        spots.append((cell_x, cell_y, cell_z, weight))
    increment, exchange_parts = parcel_exchange_parts(interpolated, parcel_motion, parcel_thermal_state, parcel_relaxation_factor)
    exchange_parts = exchange_parts * live[None]
    parcel_motion_after_drag = parcel_motion + increment * live[None]
    feedback_terms_mesh = jnp.zeros((5, MESH_NODES_FIRST, MESH_NODES_SECOND, MESH_NODES_THIRD), jnp.float32)
    for cell_x, cell_y, cell_z, weight in spots:
        feedback_terms_mesh = feedback_terms_mesh.at[:, cell_x, cell_y, cell_z].add(weight[None] * exchange_parts)
    speed = gaseous_motion[0] * gaseous_motion[0] + gaseous_motion[1] * gaseous_motion[1] + gaseous_motion[2] * gaseous_motion[2]
    table = lattice_table()
    outputs = []
    for label in range(27):
        relaxed = relax_one(distribution_functions[label], label, density, gaseous_motion, speed, feedback_terms_mesh)
        outputs.append(jnp.roll(relaxed, table[label], axis=(0, 1, 2)))
    distribution_functions_next = jnp.stack(outputs)
    return distribution_functions_next, gaseous_thermal_state + feedback_terms_mesh[3], moisture_fraction + feedback_terms_mesh[4], parcel_motion_after_drag
```

```python
import functools

import jax
import jax.numpy as jnp
from jax import lax
from jax.experimental import pallas as pl
from jax.experimental.pallas import tpu as pltpu
from jax.sharding import PartitionSpec as P

AXES = ("gx", "gy", "gz")
CHUNK = 256
PARCELS = 2048
PITCH = 24
F32 = jnp.float32
BF16 = jnp.bfloat16


def step_of(q):
    return q // 9 - 1, q // 3 % 3 - 1, q % 3 - 1


def weight_of(q):
    value = 1.0
    for step in step_of(q):
        value = value * (2.0 / 3.0 if step == 0 else 1.0 / 6.0)
    return value


def roll(v, k):
    k = k % 128
    return pltpu.roll(v, k, 1) if k else v


def split(v):
    hi = v.astype(BF16)
    lo = (v - hi.astype(F32)).astype(BF16)
    return hi, lo


def side_index(dx, dy):
    return 3 * (dx + 1) + dy + 1


Y_UP = [9 * a + 6 + b for a in range(3) for b in range(3)]
Y_DOWN = [9 * a + b for a in range(3) for b in range(3)]


def kernel(
    f, gt, gv, base, frac, vel, temp, rate, live,
    fo, to, vo, mo,
    ext, rho, ysend, csend, crecv, zsend, zrecv,
    a4, amat, bmat, dep, rim,
    dxr, dyr, c2send, c2recv, z2send, z2recv,
    pop, y3send, y3recv, c3send, c3recv, z3send, z3recv, zcol,
    send_sem, recv_sem,
):
    me = [lax.axis_index(a) for a in AXES]
    size = [lax.axis_size(a) for a in AXES]

    def device(d):
        return tuple(
            me[i] if d[i] == 0 else lax.rem(me[i] + (d[i] + size[i]), size[i]) for i in range(3)
        )

    around = [
        (dx, dy, dz)
        for dz in (-1, 1, 0)
        for dx in (-1, 0, 1)
        for dy in (-1, 0, 1)
        if (dx, dy, dz) != (0, 0, 0)
    ]
    barrier = pltpu.get_barrier_semaphore()
    for d in around:
        pl.semaphore_signal(
            barrier, inc=1, device_id=device(d), device_id_type=pl.DeviceIdType.MESH
        )

    def exchange(phase, moves):
        copies = []
        for n, (src, dst, d) in enumerate(moves):
            copy = pltpu.make_async_remote_copy(
                src_ref=src,
                dst_ref=dst,
                send_sem=send_sem.at[phase, n],
                recv_sem=recv_sem.at[phase, n],
                device_id=device(d),
                device_id_type=pl.DeviceIdType.MESH,
            )
            copy.start()
            copies.append(copy)
        return copies

    lane = lax.broadcasted_iota(jnp.int32, (8, 128), 1)
    sub = lax.broadcasted_iota(jnp.int32, (8, 128), 0)

    def skew(v, amount):
        for bit in range(3):
            v = jnp.where((sub >> bit) & 1 == 1, roll(v, amount << bit), v)
        return v

    def spread_row(v, row):
        return jnp.broadcast_to(v[row : row + 1], (8, 128))

    def moment_step(x, _):
        at = pl.multiple_of(x * 40, 8)
        pops = [f[q, x] for q in range(27)]
        total = pops[0]
        for q in range(1, 27):
            total = total + pops[q]
        rho[x] = total
        for axis in range(3):
            up = None
            for q in range(27):
                e = step_of(q)[axis]
                if e == 1:
                    up = pops[q] if up is None else up + pops[q]
                elif e == -1:
                    up = -pops[q] if up is None else up - pops[q]
            ext[pl.ds(at + 8 * axis, 8), :] = up / total
        ext[pl.ds(at + 24, 8), :] = gt[x]
        ext[pl.ds(at + 32, 8), :] = gv[x]
        return 0

    lax.fori_loop(0, 8, moment_step, 0)
    ext[pl.ds(520, 8), :] = jnp.zeros((8, 128), F32)

    for c in range(5):
        for side in range(2):
            ysend[side, pl.ds(8 * c, 8), :] = ext[pl.ds(8 * c + 7 * side, 8, stride=40), :]
    for j in range(4):
        x, y = (7, 0)[j // 2], (7, 0)[j % 2]
        csend[j, pl.ds(0, 5), :] = ext[pl.ds(40 * x + y, 5, stride=8), :]
        csend[j, pl.ds(5, 3), :] = jnp.zeros((3, 128), F32)
    low = jnp.zeros((8, 128), F32)
    high = jnp.zeros((8, 128), F32)
    for x in range(8):
        for c in range(5):
            at = 8 * x + c
            turned = roll(ext[pl.ds(8 * (5 * x + c), 8), :], at + 1)
            high = jnp.where(lane == at, turned, high)
            low = jnp.where(lane == at + 1, turned, low)
    zsend[0] = low
    zsend[1] = high

    pl.semaphore_wait(barrier, 26)

    def z_moves(send, recv):
        return [
            (
                send.at[(1 + dz) // 2],
                recv.at[(1 - dz) // 2, side_index(-dx, -dy)],
                (dx, dy, dz),
            )
            for (dx, dy, dz) in around
            if dz != 0
        ]

    def corner_moves(send, recv):
        return [
            (send.at[j], recv.at[j], ((1, -1)[j // 2], (1, -1)[j % 2], 0)) for j in range(4)
        ]

    copies1 = exchange(
        0,
        z_moves(zsend, zrecv)
        + [
            (ext.at[pl.ds(280, 40)], ext.at[pl.ds(320, 40)], (1, 0, 0)),
            (ext.at[pl.ds(0, 40)], ext.at[pl.ds(360, 40)], (-1, 0, 0)),
            (ysend.at[1], ext.at[pl.ds(400, 40)], (0, 1, 0)),
            (ysend.at[0], ext.at[pl.ds(440, 40)], (0, -1, 0)),
        ]
        + corner_moves(csend, crecv),
    )

    def collide_step(x, _):
        at = pl.multiple_of(x * 40, 8)
        to_row = pl.multiple_of(PITCH * (x + 1) + 8, 8)
        u = [ext[pl.ds(at + 8 * axis, 8), :] for axis in range(3)]
        speed = u[0] * u[0] + u[1] * u[1] + u[2] * u[2]
        total = rho[x]
        rest = 1.0 - 1.5 * speed
        for q in range(27):
            e = step_of(q)
            along = None
            for axis in range(3):
                if e[axis] != 0:
                    term = u[axis] if e[axis] == 1 else -u[axis]
                    along = term if along is None else along + term
            inner = rest if along is None else rest + along * (3.0 + 4.5 * along)
            equil = (1.25 * weight_of(q)) * total * inner
            pop[q, pl.ds(to_row, 8), :] = equil - 0.25 * f[q, x]
        return 0

    lax.fori_loop(0, 8, collide_step, 0)
    dep[...] = jnp.zeros_like(dep)
    rim[...] = jnp.zeros_like(rim)
    bmat[pl.ds(432, 80), :] = jnp.zeros((80, CHUNK), BF16)

    for copy in copies1:
        copy.wait_recv()

    for j in range(4):
        ext[pl.ds(480 + j, 5, stride=8), :] = crecv[j, pl.ds(0, 5), :]
    for c in range(5):
        ext[pl.ds(480 + 8 * c + 4, 4), :] = jnp.zeros((4, 128), F32)

    columns = []
    for s in range(13):
        sides = []
        for side in range(2):
            to_lane = 8 * side - side
            if s < 8:
                t = roll(zrecv[side, side_index(0, 0)], to_lane - 8 * s)
            elif s < 10:
                dx = (-1, 1)[s - 8]
                t = roll(zrecv[side, side_index(dx, 0)], to_lane - (56, 0)[s - 8])
            elif s < 12:
                dy = (-1, 1)[s - 10]
                t = spread_row(zrecv[side, side_index(0, dy)], (7, 0)[s - 10])
                t = skew(roll(t, to_lane), -8)
            else:
                t = jnp.zeros((8, 128), F32)
                for j in range(4):
                    got = zrecv[side, side_index((-1, 1)[j // 2], (-1, 1)[j % 2])]
                    got = roll(got, to_lane - (56, 0)[j // 2])
                    t = jnp.where(sub == j, spread_row(got, (7, 0)[j % 2]), t)
            sides.append(t)
        both = jnp.where(lane < 8, sides[0], jnp.where(lane < 16, sides[1], 0.0))
        hi = both.astype(BF16).astype(F32)
        both = hi + roll(both - hi, 16) + roll(hi, 32)
        for c in range(5):
            a4[pl.ds(8 * (5 * s + c), 8), :] = jnp.where(
                ((lane & 7) == c) & (lane < 48), both, 0.0
            )
    a4[pl.ds(520, 8), :] = jnp.zeros((8, 128), F32)

    def matrix_step(n, _):
        at = pl.multiple_of(n * 16, 16)
        hi, lo = split(ext[pl.ds(at, 16), :])
        amat[pl.ds(at, 16), pl.ds(0, 128)] = hi
        amat[pl.ds(at, 16), pl.ds(128, 128)] = hi
        amat[pl.ds(at, 16), pl.ds(256, 128)] = lo
        amat[pl.ds(at, 16), pl.ds(384, 128)] = a4[pl.ds(at, 16), :].astype(BF16)
        return 0

    lax.fori_loop(0, 33, matrix_step, 0)

    alive = live[0]

    def chunk_step(n, _):
        first = pl.multiple_of(n * CHUNK, CHUNK)
        here = pl.ds(first, CHUNK)
        bx, by, bz = (base[d : d + 1, here] for d in range(3))
        fx, fy, fz = (frac[d : d + 1, here] for d in range(3))
        rows8 = lax.broadcasted_iota(jnp.int32, (8, CHUNK), 0)

        def hat(cells, b, fr):
            return jnp.where(cells == b, 1.0 - fr, jnp.where(cells == b + 1, fr, 0.0))

        wz = hat(lax.broadcasted_iota(jnp.int32, (128, CHUNK), 0), bz, fz)
        wz_hi, wz_lo = split(wz)
        bmat[pl.ds(0, 128), :] = wz_hi
        bmat[pl.ds(128, 128), :] = wz_lo
        bmat[pl.ds(256, 128), :] = wz_hi
        below = jnp.where(bz == -1, 1.0 - fz, 0.0)
        above = jnp.where(bz == 127, fz, 0.0)
        rows16 = lax.broadcasted_iota(jnp.int32, (16, CHUNK), 0)
        rim_hi, rim_lo = split(jnp.where(rows16 < 8, below, above))
        bmat[pl.ds(384, 16), :] = rim_hi
        bmat[pl.ds(400, 16), :] = rim_hi
        bmat[pl.ds(416, 16), :] = rim_lo

        wx8 = hat(rows8, bx, fx)
        wy8 = hat(rows8, by, fy)
        x_low = jnp.where(bx == -1, 1.0 - fx, 0.0)
        x_high = jnp.where(bx == 7, fx, 0.0)
        y_low = jnp.where(by == -1, 1.0 - fy, 0.0)
        y_high = jnp.where(by == 7, fy, 0.0)
        plane = [wx8[x : x + 1] * wy8 for x in range(8)]
        plane += [x_low * wy8, x_high * wy8, y_low * wx8, y_high * wx8]
        edge = jnp.where(rows8 < 2, x_low, x_high) * jnp.where((rows8 & 1) == 0, y_low, y_high)
        plane.append(jnp.where(rows8 < 4, edge, 0.0))

        along = jnp.dot(amat[...], bmat[...], preferred_element_type=F32)
        sampled = []
        for c in range(5):
            total = None
            for s in range(13):
                at = 8 * (5 * s + c)
                term = along[at : at + 8] * plane[s]
                total = term if total is None else total + term
            sampled.append(jnp.sum(total, axis=0, keepdims=True))

        slot = lax.broadcasted_iota(jnp.int32, (1, CHUNK), 1) + first
        alive_here = slot < alive
        factor = jnp.where(alive_here, rate[0:1, here], 0.0)
        own_temp = temp[0:1, here]
        terms = []
        for d in range(3):
            motion = vel[d : d + 1, here]
            change = factor * (sampled[d] - motion)
            mo[d : d + 1, here] = motion + change
            terms.append(-2.0 * change)
        terms.append(factor * (own_temp - sampled[3]))
        terms.append(factor * (0.05 * jnp.exp(3.0 * (own_temp - 0.5)) - sampled[4]))

        load = [plane[s] * terms[c] for s in range(13) for c in range(5)]
        load.append(jnp.zeros((8, CHUNK), F32))
        load_hi, load_lo = split(jnp.concatenate(load, axis=0))
        nt = (((1,), (1,)), ((), ()))
        wz_both = bmat[pl.ds(0, 256), :]
        got_hi = lax.dot_general(load_hi, wz_both, nt, preferred_element_type=F32)
        got_lo = lax.dot_general(load_lo, wz_hi, nt, preferred_element_type=F32)
        dep[...] += got_hi[:, :128] + got_hi[:, 128:] + got_lo

        plane_hi, plane_lo = split(
            jnp.concatenate(plane + [jnp.zeros((24, CHUNK), F32)], axis=0)
        )
        rows = []
        zero3 = jnp.zeros((3, CHUNK), F32)
        stacked = jnp.concatenate(terms + [zero3], axis=0)
        side_hi, side_lo = split(jnp.concatenate([stacked * below, stacked * above], axis=0))
        plane_both = jnp.concatenate([plane_hi, plane_lo], axis=0)
        edge_hi = lax.dot_general(side_hi, plane_both, nt, preferred_element_type=F32)
        edge_lo = lax.dot_general(side_lo, plane_hi, nt, preferred_element_type=F32)
        rim[pl.ds(0, 16), :] += edge_hi[:, :128] + edge_hi[:, 128:] + edge_lo
        return 0

    lax.fori_loop(0, PARCELS // CHUNK, chunk_step, 0)

    by_row = jnp.transpose(rim[...])
    low = jnp.zeros((8, 128), F32)
    high = jnp.zeros((8, 128), F32)
    for s in range(13):
        v = by_row[8 * s : 8 * s + 8]
        mine = (lane >> 3) == s
        low = jnp.where(mine, roll(v, 8 * s), low)
        high = jnp.where(mine, roll(v, 8 * s - 8), high)
    z2send[0] = low
    z2send[1] = high
    for j in range(4):
        c2send[j, pl.ds(0, 5), :] = dep[pl.ds(480 + 3 - j, 5, stride=8), :]
        c2send[j, pl.ds(5, 3), :] = jnp.zeros((3, 128), F32)
    copies2 = exchange(
        1,
        z_moves(z2send, z2recv)
        + [
            (dep.at[pl.ds(360, 40)], dxr.at[0], (1, 0, 0)),
            (dep.at[pl.ds(320, 40)], dxr.at[1], (-1, 0, 0)),
            (dep.at[pl.ds(440, 40)], dyr.at[0], (0, 1, 0)),
            (dep.at[pl.ds(400, 40)], dyr.at[1], (0, -1, 0)),
        ]
        + corner_moves(c2send, c2recv),
    )
    for copy in copies2:
        copy.wait_recv()

    ends = []
    for side in range(2):
        acc = jnp.where(lane < 64, z2recv[side, side_index(0, 0)], 0.0)
        acc += jnp.where(lane < 8, roll(z2recv[side, side_index(-1, 0)], -72), 0.0)
        acc += jnp.where((lane >> 3) == 7, roll(z2recv[side, side_index(1, 0)], -8), 0.0)
        for dy, from_slot, row in ((-1, 11, 0), (1, 10, 7)):
            t = roll(z2recv[side, side_index(0, dy)], -8 * from_slot)
            t = skew(jnp.where(lane < 8, t, 0.0), 8)
            acc += jnp.where(sub == row, jnp.sum(t, axis=0, keepdims=True), 0.0)
        for j in range(4):
            dx, dy = (-1, 1)[j // 2], (-1, 1)[j % 2]
            to_x, row = (0, 7)[j // 2], (0, 7)[j % 2]
            t = roll(z2recv[side, side_index(dx, dy)], 8 * to_x - 96)
            t = spread_row(t, 3 - j)
            acc += jnp.where((sub == row) & ((lane >> 3) == to_x), t, 0.0)
        ends.append(acc)

    for x in range(8):
        for c in range(5):
            at = 8 * (5 * x + c)
            k = 8 * x + c
            v = dep[pl.ds(at, 8), :]
            v += jnp.where(lane == 0, roll(ends[0], -k), 0.0)
            v += jnp.where(lane == 127, roll(ends[1], 127 - k), 0.0)
            top = dyr[0, pl.ds(8 * c + x, 1), :]
            bottom = dyr[1, pl.ds(8 * c + x, 1), :]
            if x == 0:
                v += dxr[0, pl.ds(8 * c, 8), :]
                top += c2recv[0, pl.ds(c, 1), :]
                bottom += c2recv[1, pl.ds(c, 1), :]
            if x == 7:
                v += dxr[1, pl.ds(8 * c, 8), :]
                top += c2recv[2, pl.ds(c, 1), :]
                bottom += c2recv[3, pl.ds(c, 1), :]
            v += jnp.where(sub == 0, top, 0.0) + jnp.where(sub == 7, bottom, 0.0)
            rho_at = v
            a4[pl.ds(at, 8), :] = rho_at

    def push_step(x, _):
        at = pl.multiple_of(x * 40, 8)
        to_row = pl.multiple_of(PITCH * (x + 1) + 8, 8)
        s = [a4[pl.ds(at + 8 * c, 8), :] for c in range(5)]
        to[x] = gt[x] + s[3]
        vo[x] = gv[x] + s[4]
        for q in range(27):
            e = step_of(q)
            push = s[4]
            for axis in range(3):
                if e[axis] == 1:
                    push = push + 3.0 * s[axis]
                elif e[axis] == -1:
                    push = push - 3.0 * s[axis]
            pop[q, pl.ds(to_row, 8), :] += weight_of(q) * push
        return 0

    lax.fori_loop(0, 8, push_step, 0)

    for k in range(9):
        y3send[0, pl.ds(8 * k, 8), :] = pop[Y_DOWN[k], pl.ds(PITCH + 8, 8, stride=PITCH), :]
        y3send[1, pl.ds(8 * k, 8), :] = pop[Y_UP[k], pl.ds(PITCH + 15, 8, stride=PITCH), :]
    for j in range(4):
        sx, sy = (1, -1)[j // 2], (1, -1)[j % 2]
        row = PITCH * ((7, 0)[j // 2] + 1) + 8 + (7, 0)[j % 2]
        for k in range(3):
            q = 9 * (sx + 1) + 3 * (sy + 1) + k
            c3send[j, pl.ds(k, 1), :] = pop[q, pl.ds(row, 1), :]
        c3send[j, pl.ds(3, 5), :] = jnp.zeros((5, 128), F32)
    low = jnp.zeros((8, 128), F32)
    high = jnp.zeros((8, 128), F32)
    for x in range(8):
        for m in range(9):
            at = 16 * x + m
            row = PITCH * (x + 1) + 8
            low = jnp.where(lane == at, roll(pop[3 * m, pl.ds(row, 8), :], at), low)
            high = jnp.where(lane == at, roll(pop[3 * m + 2, pl.ds(row, 8), :], at + 1), high)
    z3send[0] = low
    z3send[1] = high
    copies3 = exchange(
        2,
        z_moves(z3send, z3recv)
        + [
            (
                pop.at[pl.ds(18, 9), pl.ds(PITCH * 8 + 8, 8)],
                pop.at[pl.ds(18, 9), pl.ds(8, 8)],
                (1, 0, 0),
            ),
            (
                pop.at[pl.ds(0, 9), pl.ds(PITCH + 8, 8)],
                pop.at[pl.ds(0, 9), pl.ds(PITCH * 9 + 8, 8)],
                (-1, 0, 0),
            ),
            (y3send.at[1], y3recv.at[0], (0, 1, 0)),
            (y3send.at[0], y3recv.at[1], (0, -1, 0)),
        ]
        + corner_moves(c3send, c3recv),
    )
    for copy in copies3:
        copy.wait_recv()

    for k in range(9):
        pop[Y_UP[k], pl.ds(PITCH + 7, 8, stride=PITCH), :] = y3recv[0, pl.ds(8 * k, 8), :]
        pop[Y_DOWN[k], pl.ds(PITCH + 16, 8, stride=PITCH), :] = y3recv[1, pl.ds(8 * k, 8), :]
    for j in range(4):
        sx, sy = (1, -1)[j // 2], (1, -1)[j % 2]
        row = PITCH * (0, 9)[j // 2] + (7, 16)[j % 2]
        for k in range(3):
            q = 9 * (sx + 1) + 3 * (sy + 1) + k
            pop[q, pl.ds(row, 1), :] = c3recv[j, pl.ds(k, 1), :]
    for side in range(2):
        face = z3recv[side, side_index(0, 0)]
        for x in range(8):
            zcol[side, pl.ds(PITCH * (x + 1) + 8, 8), :] = roll(face, -16 * x)
        left = z3recv[side, side_index(-1, 0)]
        zcol[side, pl.ds(8, 8), :] = roll(left, -112)
        zcol[side, pl.ds(PITCH * 9 + 8, 8), :] = z3recv[side, side_index(1, 0)]
        t = skew(spread_row(z3recv[side, side_index(0, -1)], 7), -16)
        zcol[side, pl.ds(PITCH + 7, 8, stride=PITCH), :] = t
        t = skew(spread_row(z3recv[side, side_index(0, 1)], 0), -16)
        zcol[side, pl.ds(PITCH + 16, 8, stride=PITCH), :] = t
        for j in range(4):
            t = z3recv[side, side_index((-1, 1)[j // 2], (-1, 1)[j % 2])]
            t = roll(t, (-112, 0)[j // 2])
            row = (7, 0)[j % 2]
            to_row = PITCH * (0, 9)[j // 2] + (7, 16)[j % 2]
            zcol[side, pl.ds(to_row, 1), :] = t[row : row + 1]

    for q in range(27):
        ex, ey, ez = step_of(q)
        m = q // 3
        for x in range(8):
            row = PITCH * (x - ex + 1) + 8 - ey
            v = pop[q, pl.ds(row, 8), :]
            if ez == 1:
                v = jnp.where(lane == 0, roll(zcol[0, pl.ds(row, 8), :], -m), roll(v, 1))
            elif ez == -1:
                v = jnp.where(lane == 127, roll(zcol[1, pl.ds(row, 8), :], 127 - m), roll(v, -1))
            fo[q, x] = v

    for copies in (copies1, copies2, copies3):
        for copy in copies:
            copy.wait_send()


def on_device(f, gt, gv, base, frac, vel, temp, rate, live):
    vmem = pl.BlockSpec(memory_space=pltpu.VMEM)
    fo, to, vo, mo = pl.pallas_call(
        kernel,
        out_shape=(
            jax.ShapeDtypeStruct(f.shape, F32),
            jax.ShapeDtypeStruct(gt.shape, F32),
            jax.ShapeDtypeStruct(gv.shape, F32),
            jax.ShapeDtypeStruct((3, PARCELS), F32),
        ),
        in_specs=[vmem] * 8 + [pl.BlockSpec(memory_space=pltpu.SMEM)],
        out_specs=[vmem] * 4,
        scratch_shapes=[
            pltpu.VMEM((528, 128), F32),
            pltpu.VMEM((8, 8, 128), F32),
            pltpu.VMEM((2, 40, 128), F32),
            pltpu.VMEM((4, 8, 128), F32),
            pltpu.VMEM((4, 8, 128), F32),
            pltpu.VMEM((2, 8, 128), F32),
            pltpu.VMEM((2, 9, 8, 128), F32),
            pltpu.VMEM((528, 128), F32),
            pltpu.VMEM((528, 512), BF16),
            pltpu.VMEM((512, CHUNK), BF16),
            pltpu.VMEM((528, 128), F32),
            pltpu.VMEM((128, 128), F32),
            pltpu.VMEM((2, 40, 128), F32),
            pltpu.VMEM((2, 40, 128), F32),
            pltpu.VMEM((4, 8, 128), F32),
            pltpu.VMEM((4, 8, 128), F32),
            pltpu.VMEM((2, 8, 128), F32),
            pltpu.VMEM((2, 9, 8, 128), F32),
            pltpu.VMEM((27, 10 * PITCH, 128), F32),
            pltpu.VMEM((2, 72, 128), F32),
            pltpu.VMEM((2, 72, 128), F32),
            pltpu.VMEM((4, 8, 128), F32),
            pltpu.VMEM((4, 8, 128), F32),
            pltpu.VMEM((2, 8, 128), F32),
            pltpu.VMEM((2, 9, 8, 128), F32),
            pltpu.VMEM((2, 10 * PITCH, 128), F32),
            pltpu.SemaphoreType.DMA((3, 26)),
            pltpu.SemaphoreType.DMA((3, 26)),
        ],
        compiler_params=pltpu.CompilerParams(
            collective_id=0, has_side_effects=True, vmem_limit_bytes=40 * 1024 * 1024
        ),
    )(
        f,
        gt,
        gv,
        base.reshape(3, PARCELS),
        frac.reshape(3, PARCELS),
        vel.reshape(3, PARCELS),
        temp.reshape(1, PARCELS),
        rate.reshape(1, PARCELS),
        live.reshape(1),
    )
    return fo, to, vo, mo.reshape(vel.shape)


def solution(mesh):
    placed = (
        P(None, "gx", "gy", "gz"),
        P("gx", "gy", "gz"),
        P("gx", "gy", "gz"),
        P(None, "gx", "gy", "gz", None),
        P(None, "gx", "gy", "gz", None),
        P(None, "gx", "gy", "gz", None),
        P("gx", "gy", "gz", None),
        P("gx", "gy", "gz", None),
        P("gx", "gy", "gz"),
    )
    return jax.shard_map(
        on_device,
        mesh=mesh,
        in_specs=placed,
        out_specs=(
            P(None, "gx", "gy", "gz"),
            P("gx", "gy", "gz"),
            P("gx", "gy", "gz"),
            P(None, "gx", "gy", "gz", None),
        ),
        check_vma=False,
    )
```

```python
import jax
import jax.numpy as jnp
from jax import lax
from jax.experimental import pallas as pl
from jax.experimental.pallas import tpu as pltpu
from jax.sharding import PartitionSpec as P

AXES = ("gx", "gy", "gz")
CHUNK = 256
PARCELS = 2048
PITCH = 24
F32 = jnp.float32
BF16 = jnp.bfloat16
MESH = pl.DeviceIdType.MESH
NT = (((1,), (1,)), ((), ()))


def step_of(q):
    return q // 9 - 1, q // 3 % 3 - 1, q % 3 - 1


def weight_of(q):
    value = 1.0
    for step in step_of(q):
        value = value * (2.0 / 3.0 if step == 0 else 1.0 / 6.0)
    return value


def roll(v, k):
    k = k % 128
    return pltpu.roll(v, k, 1) if k else v


def split(v):
    hi = v.astype(BF16)
    lo = (v - hi.astype(F32)).astype(BF16)
    return hi, lo


def side_index(dx, dy):
    return 3 * (dx + 1) + dy + 1


def place_of(x, y):
    if 0 <= x < 8:
        return (x, y) if 0 <= y < 8 else (10 if y < 0 else 11, x)
    if 0 <= y < 8:
        return 8 if x < 0 else 9, y
    return 12, 2 * (x > 0) + (y > 0)


SIGNS = [(1, 1), (1, -1), (-1, 1), (-1, -1)]
Y_UP = [9 * a + 6 + b for a in range(3) for b in range(3)]
Y_DOWN = [9 * a + b for a in range(3) for b in range(3)]


def push_of(q, s):
    push = s[4]
    e = step_of(q)
    for axis in range(3):
        if e[axis] == 1:
            push = push + 3.0 * s[axis]
        elif e[axis] == -1:
            push = push - 3.0 * s[axis]
    return weight_of(q) * push


def gather_kernel(
    f_in, gt_in, gv_in, base_in, frac_in, vel_in, temp_in, rate_in, live,
    fo, to_out, vo_out, mo_out,
    pop, zcol, to, vo, mo, staged,
    f, gt, gv, base, frac, vel, temp, rate,
    ext, ysend, csend, crecv, zsend, zrecv, ybsend, ybrecv, xbrecv,
    amat, wmat, pmat, plane_of, target, factor, sampled, edges,
    dep, rim, zslot, rimf,
    x2send, x2recv, y2send, y2recv, c2send, c2recv, z2send, z2recv, src,
    in_sem, out_sem, send_sem, recv_sem,
):
    me = [lax.axis_index(a) for a in AXES]
    size = [lax.axis_size(a) for a in AXES]

    def device(d):
        return tuple(
            me[i] if d[i] == 0 else lax.rem(me[i] + (d[i] + size[i]), size[i]) for i in range(3)
        )

    around = [
        (dx, dy, dz)
        for dz in (-1, 1, 0)
        for dx in (-1, 1, 0)
        for dy in (-1, 1, 0)
        if (dx, dy, dz) != (0, 0, 0)
    ]
    barrier = pltpu.get_barrier_semaphore()
    for d in around:
        pl.semaphore_signal(barrier, inc=1, device_id=device(d), device_id_type=MESH)

    fetches = []
    for n, (a, b) in enumerate(
        [
            (f_in, f), (gt_in, gt), (gv_in, gv), (base_in, base), (frac_in, frac),
            (vel_in, vel), (temp_in, temp), (rate_in, rate),
        ]
    ):
        fetch = pltpu.make_async_copy(a, b, in_sem.at[n])
        fetch.start()
        fetches.append(fetch)

    def write(pairs, at):
        copies = []
        for n, (a, b) in enumerate(pairs):
            copy = pltpu.make_async_copy(a, b, out_sem.at[at + n])
            copy.start()
            copies.append(copy)
        return copies

    def exchange(phase, moves):
        copies = []
        for n, (a, b, d) in enumerate(moves):
            copy = pltpu.make_async_remote_copy(
                src_ref=a,
                dst_ref=b,
                send_sem=send_sem.at[phase, n],
                recv_sem=recv_sem.at[phase, n],
                device_id=device(d),
                device_id_type=MESH,
            )
            copy.start()
            copies.append(copy)
        return copies

    lane = lax.broadcasted_iota(jnp.int32, (8, 128), 1)
    sub = lax.broadcasted_iota(jnp.int32, (8, 128), 0)
    low_lane = lane & 7
    group = lane >> 3

    def skew(v, amount):
        for bit in range(3):
            v = jnp.where((sub >> bit) & 1 == 1, roll(v, amount << bit), v)
        return v

    def spread_row(v, row):
        return jnp.broadcast_to(v[row : row + 1], (8, 128))

    for fetch in fetches[:3]:
        fetch.wait()

    def moment_step(x, _):
        at = pl.multiple_of(x * 40, 8)
        to_row = pl.multiple_of(PITCH * (x + 1) + 8, 8)
        pops = [f[q, x] for q in range(27)]
        total = pops[0]
        for q in range(1, 27):
            total = total + pops[q]
        u = []
        for axis in range(3):
            up = None
            for q in range(27):
                e = step_of(q)[axis]
                if e == 1:
                    up = pops[q] if up is None else up + pops[q]
                elif e == -1:
                    up = -pops[q] if up is None else up - pops[q]
            u.append(up / total)
            ext[pl.ds(at + 8 * axis, 8), :] = u[axis]
        ext[pl.ds(at + 24, 8), :] = gt[x]
        ext[pl.ds(at + 32, 8), :] = gv[x]
        rest = 1.0 - 1.5 * (u[0] * u[0] + u[1] * u[1] + u[2] * u[2])
        for q in range(27):
            e = step_of(q)
            along = None
            for axis in range(3):
                if e[axis] != 0:
                    term = u[axis] if e[axis] == 1 else -u[axis]
                    along = term if along is None else along + term
            inner = rest if along is None else rest + along * (3.0 + 4.5 * along)
            equil = (1.25 * weight_of(q)) * total * inner
            pop[q, pl.ds(to_row, 8), :] = equil - 0.25 * pops[q]
        return 0

    lax.fori_loop(0, 8, moment_step, 0)

    for c in range(5):
        for side in range(2):
            ysend[side, pl.ds(8 * c, 8), :] = ext[pl.ds(8 * c + 7 * side, 8, stride=40), :]
    for k in range(9):
        ybsend[0, pl.ds(8 * k, 8), :] = pop[Y_DOWN[k], pl.ds(PITCH + 8, 8, stride=PITCH), :]
        ybsend[1, pl.ds(8 * k, 8), :] = pop[Y_UP[k], pl.ds(PITCH + 15, 8, stride=PITCH), :]
    for j, (sx, sy) in enumerate(SIGNS):
        x, y = 7 if sx == 1 else 0, 7 if sy == 1 else 0
        csend[j, pl.ds(0, 5), :] = ext[pl.ds(40 * x + y, 5, stride=8), :]
        for k in range(3):
            q = 9 * (sx + 1) + 3 * (sy + 1) + k
            csend[j, pl.ds(5 + k, 1), :] = pop[q, pl.ds(PITCH * (x + 1) + 8 + y, 1), :]

    def z_pack(x, carry):
        low, high = carry
        at = pl.multiple_of(x * 40, 8)
        row = pl.multiple_of(PITCH * (x + 1) + 8, 8)
        near_low = jnp.zeros((8, 128), F32)
        near_high = jnp.zeros((8, 128), F32)
        for v in range(14):
            if v < 5:
                t_low = t_high = roll(ext[pl.ds(at + 8 * v, 8), :], v + 1)
            else:
                t_low = roll(pop[3 * (v - 5), pl.ds(row, 8), :], v + 1)
                t_high = roll(pop[3 * (v - 5) + 2, pl.ds(row, 8), :], v + 1)
            near_low = jnp.where(lane == v + 1, t_low, near_low)
            near_high = jnp.where(lane == v, t_high, near_high)
        return (
            low + pltpu.roll(near_low, 16 * x, 1),
            high + pltpu.roll(near_high, 16 * x, 1),
        )

    zero8 = jnp.zeros((8, 128), F32)
    low, high = lax.fori_loop(0, 8, z_pack, (zero8, zero8))
    zsend[0] = low
    zsend[1] = high

    for fetch in fetches[3:]:
        fetch.wait()
    alive = live[0]

    def weight_step(n, _):
        first = pl.multiple_of(n * CHUNK, CHUNK)
        here = pl.ds(first, CHUNK)
        bx, by, bz = (base[d, :, here] for d in range(3))
        fx, fy, fz = (frac[d, :, here] for d in range(3))
        rows8 = lax.broadcasted_iota(jnp.int32, (8, CHUNK), 0)

        def hat(cells, b, fr):
            return jnp.where(cells == b, 1.0 - fr, jnp.where(cells == b + 1, fr, 0.0))

        wz_hi, wz_lo = split(hat(lax.broadcasted_iota(jnp.int32, (128, CHUNK), 0), bz, fz))
        wmat[pl.ds(0, 128), here] = wz_hi
        wmat[pl.ds(128, 128), here] = wz_lo
        wmat[pl.ds(256, 128), here] = wz_hi
        edges[pl.ds(0, 1), here] = jnp.where(bz == -1, 1.0 - fz, 0.0)
        edges[pl.ds(1, 1), here] = jnp.where(bz == 127, fz, 0.0)

        wx8 = hat(rows8, bx, fx)
        wy8 = hat(rows8, by, fy)
        x_low = jnp.where(bx == -1, 1.0 - fx, 0.0)
        x_high = jnp.where(bx == 7, fx, 0.0)
        y_low = jnp.where(by == -1, 1.0 - fy, 0.0)
        y_high = jnp.where(by == 7, fy, 0.0)
        plane = [wx8[x : x + 1] * wy8 for x in range(8)]
        plane += [x_low * wy8, x_high * wy8, y_low * wx8, y_high * wx8]
        edge = jnp.where(rows8 < 2, x_low, x_high) * jnp.where((rows8 & 1) == 0, y_low, y_high)
        plane.append(jnp.where(rows8 < 4, edge, 0.0))
        plane = jnp.concatenate(plane + [jnp.zeros((24, CHUNK), F32)], axis=0)
        plane_of[:, here] = plane
        plane_hi, plane_lo = split(plane)
        pmat[pl.ds(0, 128), here] = plane_hi
        pmat[pl.ds(128, 128), here] = plane_lo

        slot = lax.broadcasted_iota(jnp.int32, (1, CHUNK), 1) + first
        own_temp = temp[:, here]
        target[:, here] = jnp.concatenate(
            [vel[d, :, here] for d in range(3)]
            + [own_temp, 0.05 * jnp.exp(3.0 * (own_temp - 0.5)), jnp.zeros((3, CHUNK), F32)],
            axis=0,
        )
        scale = jnp.where(rows8 < 3, 2.0, jnp.where(rows8 < 5, 1.0, 0.0))
        factor[:, here] = jnp.where(slot < alive, rate[:, here], 0.0) * scale
        return 0

    lax.fori_loop(0, PARCELS // CHUNK, weight_step, 0)

    def matrix_step(n, _):
        at = pl.multiple_of(n * 16, 16)
        hi, lo = split(ext[pl.ds(at, 16), :])
        amat[pl.ds(at, 16), pl.ds(0, 128)] = hi
        amat[pl.ds(at, 16), pl.ds(128, 128)] = hi
        amat[pl.ds(at, 16), pl.ds(256, 128)] = lo
        return 0

    pl.semaphore_wait(barrier, 26)

    def z_moves(send, recv):
        return [
            (
                send.at[(1 + dz) // 2],
                recv.at[(1 - dz) // 2, side_index(-dx, -dy)],
                (dx, dy, dz),
            )
            for (dx, dy, dz) in around
            if dz != 0
        ]

    def corner_moves(send, recv):
        return [(send.at[j], recv.at[j], (sx, sy, 0)) for j, (sx, sy) in enumerate(SIGNS)]

    copies1 = exchange(
        0,
        z_moves(zsend, zrecv)
        + corner_moves(csend, crecv)
        + [
            (ysend.at[1], ext.at[pl.ds(400, 40)], (0, 1, 0)),
            (ysend.at[0], ext.at[pl.ds(440, 40)], (0, -1, 0)),
            (ext.at[pl.ds(280, 40)], ext.at[pl.ds(320, 40)], (1, 0, 0)),
            (ext.at[pl.ds(0, 40)], ext.at[pl.ds(360, 40)], (-1, 0, 0)),
            (ybsend.at[1], ybrecv.at[0], (0, 1, 0)),
            (ybsend.at[0], ybrecv.at[1], (0, -1, 0)),
            (pop.at[pl.ds(18, 9), pl.ds(PITCH * 8 + 8, 8)], xbrecv.at[0], (1, 0, 0)),
            (pop.at[pl.ds(0, 9), pl.ds(PITCH + 8, 8)], xbrecv.at[1], (-1, 0, 0)),
        ],
    )

    lax.fori_loop(0, 20, matrix_step, 0)

    def sample(first_slot, last_slot, along, here, off):
        sums = []
        for c in range(5):
            total = None
            for s in range(first_slot, last_slot):
                at = 8 * (5 * s + c) - off
                term = along[at : at + 8] * plane_of[pl.ds(8 * s, 8), here]
                total = term if total is None else total + term
            sums.append(jnp.sum(total, axis=0, keepdims=True))
        return jnp.concatenate(sums + [jnp.zeros((3, CHUNK), F32)], axis=0)

    def own_step(n, _):
        here = pl.ds(pl.multiple_of(n * CHUNK, CHUNK), CHUNK)
        along = jnp.dot(amat[pl.ds(0, 320), :], wmat[:, here], preferred_element_type=F32)
        sampled[:, here] = sample(0, 8, along, here, 0)
        return 0

    lax.fori_loop(0, PARCELS // CHUNK, own_step, 0)
    dep[...] = jnp.zeros_like(dep)
    rim[...] = jnp.zeros_like(rim)

    for copy in copies1:
        copy.wait_recv()

    for j in range(4):
        ext[pl.ds(480 + j, 5, stride=8), :] = crecv[j, pl.ds(0, 5), :]
    for c in range(5):
        ext[pl.ds(480 + 8 * c + 4, 4), :] = jnp.zeros((4, 128), F32)
    ext[pl.ds(520, 8), :] = zero8

    rimf[pl.ds(104, 24), :] = jnp.zeros((24, 128), F32)
    for s in range(13):
        sides = []
        for side in range(2):
            if s < 8:
                t = roll(zrecv[side, side_index(0, 0)], -16 * s - side)
            elif s < 10:
                dx = (-1, 1)[s - 8]
                t = roll(zrecv[side, side_index(dx, 0)], -(112, 0)[s - 8] - side)
            elif s < 12:
                dy = (-1, 1)[s - 10]
                t = spread_row(zrecv[side, side_index(0, dy)], (7, 0)[s - 10])
                t = skew(roll(t, -side), -16)
            else:
                t = zero8
                for j in range(4):
                    got = zrecv[side, side_index((-1, 1)[j // 2], (-1, 1)[j % 2])]
                    got = roll(got, -(112, 0)[j // 2] - side)
                    t = jnp.where(sub == j, spread_row(got, (7, 0)[j % 2]), t)
            zslot[side, pl.ds(8 * s, 8), :] = t
            sides.append(t)
        both = jnp.where(lane < 8, sides[0], roll(sides[1], 8))
        rimf[pl.ds(8 * s, 8), :] = jnp.where((lane < 16) & (low_lane < 5), both, 0.0)
    fields_hi, fields_lo = split(jnp.transpose(rimf[...])[:16])
    rim_left = jnp.concatenate(
        [
            jnp.concatenate([fields_hi, fields_hi], axis=1),
            jnp.concatenate([fields_lo, fields_lo], axis=1),
        ],
        axis=0,
    )

    lax.fori_loop(20, 33, matrix_step, 0)

    def chunk_step(n, _):
        here = pl.ds(pl.multiple_of(n * CHUNK, CHUNK), CHUNK)
        below = edges[pl.ds(0, 1), here]
        above = edges[pl.ds(1, 1), here]
        along = jnp.dot(amat[pl.ds(320, 208), :], wmat[:, here], preferred_element_type=F32)
        got = sampled[:, here] + sample(8, 13, along, here, 320)
        ends = jnp.dot(rim_left, pmat[:, here], preferred_element_type=F32)
        ends = ends[:16] + ends[16:]
        got = got + below * ends[:8] + above * ends[8:]
        terms = factor[:, here] * (target[:, here] - got)
        for d in range(3):
            mo[d, :, here] = target[pl.ds(d, 1), here] - 0.5 * terms[d : d + 1]

        load = [
            plane_of[pl.ds(8 * s, 8), here] * terms[c : c + 1] for s in range(13) for c in range(5)
        ]
        load.append(jnp.zeros((8, CHUNK), F32))
        load_hi, load_lo = split(jnp.concatenate(load, axis=0))
        got_hi = lax.dot_general(
            load_hi, wmat[pl.ds(0, 256), here], NT, preferred_element_type=F32
        )
        got_lo = lax.dot_general(
            load_lo, wmat[pl.ds(0, 128), here], NT, preferred_element_type=F32
        )
        dep[...] += got_hi[:, :128] + got_hi[:, 128:] + got_lo

        side_hi, side_lo = split(jnp.concatenate([terms * below, terms * above], axis=0))
        edge_hi = lax.dot_general(side_hi, pmat[:, here], NT, preferred_element_type=F32)
        edge_lo = lax.dot_general(
            side_lo, pmat[pl.ds(0, 128), here], NT, preferred_element_type=F32
        )
        rim[pl.ds(0, 16), :] += edge_hi[:, :128] + edge_hi[:, 128:] + edge_lo
        return 0

    lax.fori_loop(0, PARCELS // CHUNK, chunk_step, 0)

    by_row = jnp.transpose(rim[...])
    low = zero8
    high = zero8
    for s in range(13):
        v = by_row[8 * s : 8 * s + 8]
        own = [dep[pl.ds(8 * (5 * s + c), 8), :] for c in range(5)]
        mine = group == s
        low = jnp.where(mine, roll(v, 8 * s), low)
        high = jnp.where(mine, roll(v, 8 * s - 8), high)
    ring = jnp.where(
        low_lane == 0,
        roll(low, -4) + 3.0 * roll(low, -2),
        jnp.where(
            low_lane < 3,
            roll(low, 1),
            jnp.where(low_lane == 4, high - 3.0 * roll(high, 2), roll(high, 5)),
        ),
    )
    for s in range(13):
        own = [dep[pl.ds(8 * (5 * s + c), 8), :] for c in range(5)]
        lean = 3.0 * own[2]
        for v, (a, b) in enumerate([(own[4] - lean, own[4] + lean), (own[0],) * 2, (own[1],) * 2]):
            at = 8 * s + 5 + v
            low = jnp.where(lane == at, roll(a, at), low)
            high = jnp.where(lane == at, roll(b, at + 1), high)
    z2send[0] = low
    z2send[1] = high

    def fill(send, blocks, singles, at):
        for n, block in enumerate(blocks):
            send[pl.ds(40 * n, 40), :] = block
        for n, (x, y) in enumerate(singles):
            s, r = place_of(x, y)
            send[pl.ds(at + 8 * n, 5), :] = dep[pl.ds(40 * s + r, 5, stride=8), :]
        send[pl.ds(at + 32, 8), :] = ring

    far = {1: (7, 8), -1: (0, -1)}
    for n, sign in enumerate((-1, 1)):
        a, b = far[sign]
        fill(
            x2send.at[n],
            [dep[pl.ds(40 * place_of(x, 0)[0], 40), :] for x in (a, b)],
            [(a, -1), (a, 8), (b, -1), (b, 8)],
            80,
        )
        for c in range(5):
            y2send[n, pl.ds(8 * c, 8), :] = dep[pl.ds(8 * c + a, 8, stride=40), :]
        y2send[n, pl.ds(40, 40), :] = dep[pl.ds(40 * place_of(0, b)[0], 40), :]
        fill(y2send.at[n], [], [(-1, a), (8, a), (-1, b), (8, b)], 80)
    for j, (sx, sy) in enumerate(SIGNS):
        fill(c2send.at[j], [], [(x, y) for x in far[sx] for y in far[sy]], 0)

    copies2 = exchange(
        1,
        z_moves(z2send, z2recv)
        + corner_moves(c2send, c2recv)
        + [
            (y2send.at[1], y2recv.at[0], (0, 1, 0)),
            (y2send.at[0], y2recv.at[1], (0, -1, 0)),
            (x2send.at[1], x2recv.at[0], (1, 0, 0)),
            (x2send.at[0], x2recv.at[1], (-1, 0, 0)),
        ],
    )
    for copy in copies1:
        copy.wait_send()
    for copy in copies2:
        copy.wait_recv()

    rings = {(0, 0): ring}
    for n, sign in enumerate((-1, 1)):
        rings[sign, 0] = x2recv[n, pl.ds(112, 8), :]
        rings[0, sign] = y2recv[n, pl.ds(112, 8), :]
    for j, (sx, sy) in enumerate(SIGNS):
        rings[-sx, -sy] = c2recv[j, pl.ds(32, 8), :]
    layers = []
    for side in range(2):
        acc = None
        for (dx, dy), ring_at in rings.items():
            t = z2recv[side, side_index(dx, dy)]
            t += jnp.where(low_lane >= 5, roll(ring_at, (5, 1)[side]), 0.0)
            xs = {0: range(-1, 9), -1: (-1, 0), 1: (7, 8)}[dx]
            ys = {0: range(-1, 9), -1: (-1, 0), 1: (7, 8)}[dy]
            singles = [(x, y) for x in xs for y in ys]
            if dx == 0 and dy == 0:
                acc = t
                continue
            if dy == 0:
                for x in xs:
                    s = place_of(x, 0)[0]
                    s_from = place_of(x - 8 * dx, 0)[0]
                    acc += jnp.where(group == s, roll(t, 8 * (s - s_from)), 0.0)
                singles = [(x, y) for (x, y) in singles if y in (-1, 8)]
            if dx == 0:
                row, s, s_from = (7, 10, 11) if dy == -1 else (0, 11, 10)
                rows = roll(skew(spread_row(t, row), -8), 8 * s)
                acc += jnp.where(group == s, rows, 0.0)
                rows = jnp.where(group == 0, roll(t, -8 * s_from), 0.0)
                rows = jnp.sum(skew(rows, 8), axis=0, keepdims=True)
                acc += jnp.where(sub == 7 - row, rows, 0.0)
                singles = [(x, y) for (x, y) in singles if x in (-1, 8)]
            for x, y in singles:
                s, r = place_of(x, y)
                s_from, r_from = place_of(x - 8 * dx, y - 8 * dy)
                got = spread_row(roll(t, 8 * (s - s_from)), r_from)
                acc += jnp.where((group == s) & (sub == r), got, 0.0)
        layers.append(acc)

    for s in range(13):
        for c in range(5):
            at = 8 * (5 * s + c)
            k = 8 * s + c
            v = dep[pl.ds(at, 8), :]
            v += jnp.where(lane == 0, roll(layers[0], -k), 0.0)
            v += jnp.where(lane == 127, roll(layers[1], 127 - k), 0.0)
            src[pl.ds(at, 8), :] = v
    def take(recv, singles, at):
        for n, (x, y) in enumerate(singles):
            s, r = place_of(x, y)
            src[pl.ds(40 * s + r, 5, stride=8), :] += recv[pl.ds(at + 8 * n, 5), :]

    near = {-1: (-1, 0), 1: (8, 7)}
    for n, sign in enumerate((-1, 1)):
        a, b = near[sign]
        for m, x in enumerate((a, b)):
            src[pl.ds(40 * place_of(x, 0)[0], 40), :] += x2recv[n, pl.ds(40 * m, 40), :]
        take(x2recv.at[n], [(a, -1), (a, 8), (b, -1), (b, 8)], 80)
        src[pl.ds(40 * place_of(0, a)[0], 40), :] += y2recv[n, pl.ds(0, 40), :]
        for c in range(5):
            src[pl.ds(8 * c + b, 8, stride=40), :] += y2recv[n, pl.ds(40 + 8 * c, 8), :]
        take(y2recv.at[n], [(-1, a), (8, a), (-1, b), (8, b)], 80)
    for j, (sx, sy) in enumerate(SIGNS):
        take(c2recv.at[j], [(x, y) for x in near[-sx] for y in near[-sy]], 0)

    def push_step(x, _):
        at = pl.multiple_of(x * 40, 8)
        to_row = pl.multiple_of(PITCH * (x + 1) + 8, 8)
        s = [src[pl.ds(at + 8 * c, 8), :] for c in range(5)]
        to[x] = gt[x] + s[3]
        vo[x] = gv[x] + s[4]
        for q in range(27):
            pop[q, pl.ds(to_row, 8), :] += push_of(q, s)
        return 0

    lax.fori_loop(0, 8, push_step, 0)
    s8, s9, s10, s11, s12 = (
        [src[pl.ds(8 * (5 * s + c), 8), :] for c in range(5)] for s in range(8, 13)
    )
    for k in range(9):
        pop[18 + k, pl.ds(8, 8), :] = xbrecv[0, k] + push_of(18 + k, s8)
        pop[k, pl.ds(PITCH * 9 + 8, 8), :] = xbrecv[1, k] + push_of(k, s9)
        q = Y_UP[k]
        pop[q, pl.ds(PITCH + 7, 8, stride=PITCH), :] = (
            ybrecv[0, pl.ds(8 * k, 8), :] + push_of(q, s10)
        )
        q = Y_DOWN[k]
        pop[q, pl.ds(PITCH + 16, 8, stride=PITCH), :] = (
            ybrecv[1, pl.ds(8 * k, 8), :] + push_of(q, s11)
        )
    for j, (sx, sy) in enumerate(SIGNS):
        row = PITCH * (0, 9)[j // 2] + (7, 16)[j % 2]
        for k in range(3):
            q = 9 * (sx + 1) + 3 * (sy + 1) + k
            total = crecv[j, pl.ds(5 + k, 1), :] + push_of(q, s12)[j : j + 1]
            pop[q, pl.ds(row, 1), :] = total

    number = lane - 5
    used = (number >= 0) & (number < 9)
    step_x = jnp.where(number < 3, -1.0, jnp.where(number < 6, 0.0, 1.0))
    third = jnp.where(number < 3, number, jnp.where(number < 6, number - 3, number - 6))
    step_y = jnp.where(third == 0, -1.0, jnp.where(third == 1, 0.0, 1.0))
    share = jnp.where(step_x == 0.0, 2.0 / 3.0, 1.0 / 6.0)
    share = share * jnp.where(step_y == 0.0, 2.0 / 3.0, 1.0 / 6.0)
    share = jnp.where(used, share * (1.0 / 6.0), 0.0)
    share_x = 3.0 * share * step_x
    share_y = 3.0 * share * step_y
    for side in range(2):
        for s in range(13):
            three = [
                jnp.broadcast_to(layers[side][:, 8 * s + v : 8 * s + v + 1], (8, 128))
                for v in (5, 6, 7)
            ]
            t = zslot[side, pl.ds(8 * s, 8), :]
            t = t + share * three[0] + share_x * three[1] + share_y * three[2]
            if s < 8:
                zcol[side, pl.ds(PITCH * (s + 1) + 8, 8), :] = t
            elif s < 10:
                zcol[side, pl.ds(PITCH * (0, 9)[s - 8] + 8, 8), :] = t
            elif s < 12:
                zcol[side, pl.ds(PITCH + (7, 16)[s - 10], 8, stride=PITCH), :] = t
            else:
                for j in range(4):
                    row = PITCH * (0, 9)[j // 2] + (7, 16)[j % 2]
                    zcol[side, pl.ds(row, 1), :] = t[j : j + 1]

    written = write([(to, to_out), (vo, vo_out), (mo, mo_out)], 0)
    for part in range(9):
        for q in range(3 * part, 3 * part + 3):
            ex, ey, ez = step_of(q)
            m = q // 3 + 5
            for x in range(8):
                row = PITCH * (x - ex + 1) + 8 - ey
                v = pop[q, pl.ds(row, 8), :]
                if ez == 1:
                    v = jnp.where(lane == 0, roll(zcol[0, pl.ds(row, 8), :], -m), roll(v, 1))
                elif ez == -1:
                    v = jnp.where(
                        lane == 127, roll(zcol[1, pl.ds(row, 8), :], 127 - m), roll(v, -1)
                    )
                staged[q, x] = v
        here = pl.ds(3 * part, 3)
        written += write([(staged.at[here], fo.at[here])], 3 + part)

    for copy in copies2:
        copy.wait_send()
    for copy in written:
        copy.wait()


def keep_kernel(a0, a1, a2, a3, b0, b1, b2, b3, t0, t1, t2, t3, sem):
    trips = []
    for part in range(3):
        here = pl.ds(9 * part, 9)
        trips.append((a0.at[here], t0.at[here], b0.at[here]))
    trips += [(a1, t1, b1), (a2, t2, b2), (a3, t3, b3)]
    copies = []
    for n, (a, t, _) in enumerate(trips):
        copy = pltpu.make_async_copy(a, t, sem.at[0, n])
        copy.start()
        copies.append(copy)
    outs = []
    for n, (_, t, b) in enumerate(trips):
        copies[n].wait()
        copy = pltpu.make_async_copy(t, b, sem.at[1, n])
        copy.start()
        outs.append(copy)
    for copy in outs:
        copy.wait()


def on_device(f, gt, gv, base, frac, vel, temp, rate, live):
    anywhere = pl.BlockSpec(memory_space=pl.ANY)

    def buffer(*shape, dtype=F32):
        return pltpu.VMEM(shape, dtype)

    results = (
        jax.ShapeDtypeStruct(f.shape, F32),
        jax.ShapeDtypeStruct(gt.shape, F32),
        jax.ShapeDtypeStruct(gv.shape, F32),
        jax.ShapeDtypeStruct((3, 1, PARCELS), F32),
    )
    inner = pl.pallas_call(
        gather_kernel,
        out_shape=results,
        in_specs=[anywhere] * 8 + [pl.BlockSpec(memory_space=pltpu.SMEM)],
        out_specs=[anywhere] * 4,
        scratch_shapes=[
            buffer(27, 10 * PITCH, 128),
            buffer(2, 10 * PITCH, 128),
            buffer(8, 8, 128),
            buffer(8, 8, 128),
            buffer(3, 1, PARCELS),
            buffer(27, 8, 8, 128),
            buffer(27, 8, 8, 128),
            buffer(8, 8, 128),
            buffer(8, 8, 128),
            buffer(3, 1, PARCELS, dtype=jnp.int32),
            buffer(3, 1, PARCELS),
            buffer(3, 1, PARCELS),
            buffer(1, PARCELS),
            buffer(1, PARCELS),
            buffer(528, 128),
            buffer(2, 40, 128),
            buffer(4, 8, 128),
            buffer(4, 8, 128),
            buffer(2, 8, 128),
            buffer(2, 9, 8, 128),
            buffer(2, 72, 128),
            buffer(2, 72, 128),
            buffer(2, 9, 8, 128),
            buffer(528, 384, dtype=BF16),
            buffer(384, PARCELS, dtype=BF16),
            buffer(256, PARCELS, dtype=BF16),
            buffer(128, PARCELS),
            buffer(8, PARCELS),
            buffer(8, PARCELS),
            buffer(8, PARCELS),
            buffer(8, PARCELS),
            buffer(528, 128),
            buffer(128, 128),
            buffer(2, 104, 128),
            buffer(128, 128),
            buffer(2, 120, 128),
            buffer(2, 120, 128),
            buffer(2, 120, 128),
            buffer(2, 120, 128),
            buffer(4, 40, 128),
            buffer(4, 40, 128),
            buffer(2, 8, 128),
            buffer(2, 9, 8, 128),
            buffer(528, 128),
            pltpu.SemaphoreType.DMA((8,)),
            pltpu.SemaphoreType.DMA((12,)),
            pltpu.SemaphoreType.DMA((2, 30)),
            pltpu.SemaphoreType.DMA((2, 30)),
        ],
        compiler_params=pltpu.CompilerParams(
            collective_id=0, has_side_effects=True, vmem_limit_bytes=56 * 1024 * 1024
        ),
    )(
        f,
        gt,
        gv,
        base.reshape(3, 1, PARCELS),
        frac.reshape(3, 1, PARCELS),
        vel.reshape(3, 1, PARCELS),
        temp.reshape(1, PARCELS),
        rate.reshape(1, PARCELS),
        live.reshape(1),
    )
    fo, to, vo, mo = pl.pallas_call(
        keep_kernel,
        out_shape=results,
        in_specs=[anywhere] * 4,
        out_specs=[anywhere] * 4,
        scratch_shapes=[
            buffer(*f.shape),
            buffer(*gt.shape),
            buffer(*gv.shape),
            buffer(3, 1, PARCELS),
            pltpu.SemaphoreType.DMA((2, 6)),
        ],
        compiler_params=pltpu.CompilerParams(vmem_limit_bytes=56 * 1024 * 1024),
    )(*inner)
    return fo, to, vo, mo.reshape(vel.shape)


def solution(mesh):
    placed = (
        P(None, "gx", "gy", "gz"),
        P("gx", "gy", "gz"),
        P("gx", "gy", "gz"),
        P(None, "gx", "gy", "gz", None),
        P(None, "gx", "gy", "gz", None),
        P(None, "gx", "gy", "gz", None),
        P("gx", "gy", "gz", None),
        P("gx", "gy", "gz", None),
        P("gx", "gy", "gz"),
    )
    return jax.shard_map(
        on_device,
        mesh=mesh,
        in_specs=placed,
        out_specs=(
            P(None, "gx", "gy", "gz"),
            P("gx", "gy", "gz"),
            P("gx", "gy", "gz"),
            P(None, "gx", "gy", "gz", None),
        ),
        check_vma=False,
    )
```

```python
import jax
import jax.numpy as jnp
from jax import lax
from jax.experimental import pallas as pl
from jax.experimental.pallas import tpu as pltpu
from jax.sharding import PartitionSpec as P

AXES = ("gx", "gy", "gz")
CHUNK = 1024
PARCELS = 2048
PITCH = 24
F32 = jnp.float32
BF16 = jnp.bfloat16
MESH = pl.DeviceIdType.MESH
NT = (((1,), (1,)), ((), ()))


def step_of(q):
    return q // 9 - 1, q // 3 % 3 - 1, q % 3 - 1


def weight_of(q):
    value = 1.0
    for step in step_of(q):
        value = value * (2.0 / 3.0 if step == 0 else 1.0 / 6.0)
    return value


def roll(v, k):
    k = k % 128
    return pltpu.roll(v, k, 1) if k else v


def split(v):
    hi = v.astype(BF16)
    lo = (v - hi.astype(F32)).astype(BF16)
    return hi, lo


def side_index(dx, dy):
    return 3 * (dx + 1) + dy + 1


def place_of(x, y):
    if 0 <= x < 8:
        return (x, y) if 0 <= y < 8 else (10 if y < 0 else 11, x)
    if 0 <= y < 8:
        return 8 if x < 0 else 9, y
    return 12, 2 * (x > 0) + (y > 0)


SIGNS = [(1, 1), (1, -1), (-1, 1), (-1, -1)]
Y_UP = [9 * a + 6 + b for a in range(3) for b in range(3)]
Y_DOWN = [9 * a + b for a in range(3) for b in range(3)]


def push_of(q, s):
    push = s[4]
    e = step_of(q)
    for axis in range(3):
        if e[axis] == 1:
            push = push + 3.0 * s[axis]
        elif e[axis] == -1:
            push = push - 3.0 * s[axis]
    return weight_of(q) * push


def gather_kernel(
    f_in, gt_in, gv_in, base_in, frac_in, vel_in, temp_in, rate_in, live,
    fo, to_out, vo_out, mo_out,
    pop, zcol, to, vo, mo, staged,
    f, gt, gv, base, frac, vel, temp, rate,
    ext, ysend, csend, crecv, zsend, zrecv, ybsend, ybrecv, xbrecv,
    amat, wmat, pmat, plane_of, target, factor, sampled, edges,
    dep, rim, zslot, rimf,
    x2send, x2recv, y2send, y2recv, c2send, c2recv, z2send, z2recv, src,
    in_sem, out_sem, send_sem, recv_sem,
):
    me = [lax.axis_index(a) for a in AXES]
    size = [lax.axis_size(a) for a in AXES]

    def device(d):
        return tuple(
            me[i] if d[i] == 0 else lax.rem(me[i] + (d[i] + size[i]), size[i]) for i in range(3)
        )

    around = [
        (dx, dy, dz)
        for dz in (-1, 1, 0)
        for dx in (-1, 1, 0)
        for dy in (-1, 1, 0)
        if (dx, dy, dz) != (0, 0, 0)
    ]
    barrier = pltpu.get_barrier_semaphore()
    for d in around:
        pl.semaphore_signal(barrier, inc=1, device_id=device(d), device_id_type=MESH)

    fetches = []
    for n, (a, b) in enumerate(
        [
            (f_in, f), (gt_in, gt), (gv_in, gv), (base_in, base), (frac_in, frac),
            (vel_in, vel), (temp_in, temp), (rate_in, rate),
        ]
    ):
        fetch = pltpu.make_async_copy(a, b, in_sem.at[n])
        fetch.start()
        fetches.append(fetch)

    def write(pairs, at):
        copies = []
        for n, (a, b) in enumerate(pairs):
            copy = pltpu.make_async_copy(a, b, out_sem.at[at + n])
            copy.start()
            copies.append(copy)
        return copies

    def exchange(phase, moves):
        copies = []
        for n, (a, b, d) in enumerate(moves):
            copy = pltpu.make_async_remote_copy(
                src_ref=a,
                dst_ref=b,
                send_sem=send_sem.at[phase, n],
                recv_sem=recv_sem.at[phase, n],
                device_id=device(d),
                device_id_type=MESH,
            )
            copy.start()
            copies.append(copy)
        return copies

    lane = lax.broadcasted_iota(jnp.int32, (8, 128), 1)
    sub = lax.broadcasted_iota(jnp.int32, (8, 128), 0)
    low_lane = lane & 7
    group = lane >> 3

    def skew(v, amount):
        for bit in range(3):
            v = jnp.where((sub >> bit) & 1 == 1, roll(v, amount << bit), v)
        return v

    def spread_row(v, row):
        return jnp.broadcast_to(v[row : row + 1], (8, 128))

    for fetch in fetches[:3]:
        fetch.wait()

    def moment_step(x, _):
        at = pl.multiple_of(x * 40, 8)
        to_row = pl.multiple_of(PITCH * (x + 1) + 8, 8)
        pops = [f[q, x] for q in range(27)]
        total = pops[0]
        for q in range(1, 27):
            total = total + pops[q]
        u = []
        for axis in range(3):
            up = None
            for q in range(27):
                e = step_of(q)[axis]
                if e == 1:
                    up = pops[q] if up is None else up + pops[q]
                elif e == -1:
                    up = -pops[q] if up is None else up - pops[q]
            u.append(up / total)
            ext[pl.ds(at + 8 * axis, 8), :] = u[axis]
        ext[pl.ds(at + 24, 8), :] = gt[x]
        ext[pl.ds(at + 32, 8), :] = gv[x]
        rest = 1.0 - 1.5 * (u[0] * u[0] + u[1] * u[1] + u[2] * u[2])
        for q in range(27):
            e = step_of(q)
            along = None
            for axis in range(3):
                if e[axis] != 0:
                    term = u[axis] if e[axis] == 1 else -u[axis]
                    along = term if along is None else along + term
            inner = rest if along is None else rest + along * (3.0 + 4.5 * along)
            equil = (1.25 * weight_of(q)) * total * inner
            pop[q, pl.ds(to_row, 8), :] = equil - 0.25 * pops[q]
        return 0

    lax.fori_loop(0, 8, moment_step, 0)

    for c in range(5):
        for side in range(2):
            ysend[side, pl.ds(8 * c, 8), :] = ext[pl.ds(8 * c + 7 * side, 8, stride=40), :]
    for k in range(9):
        ybsend[0, pl.ds(8 * k, 8), :] = pop[Y_DOWN[k], pl.ds(PITCH + 8, 8, stride=PITCH), :]
        ybsend[1, pl.ds(8 * k, 8), :] = pop[Y_UP[k], pl.ds(PITCH + 15, 8, stride=PITCH), :]
    for j, (sx, sy) in enumerate(SIGNS):
        x, y = 7 if sx == 1 else 0, 7 if sy == 1 else 0
        csend[j, pl.ds(0, 5), :] = ext[pl.ds(40 * x + y, 5, stride=8), :]
        for k in range(3):
            q = 9 * (sx + 1) + 3 * (sy + 1) + k
            csend[j, pl.ds(5 + k, 1), :] = pop[q, pl.ds(PITCH * (x + 1) + 8 + y, 1), :]

    def z_pack(x, carry):
        low, high = carry
        at = pl.multiple_of(x * 40, 8)
        row = pl.multiple_of(PITCH * (x + 1) + 8, 8)
        near_low = jnp.zeros((8, 128), F32)
        near_high = jnp.zeros((8, 128), F32)
        for v in range(14):
            if v < 5:
                t_low = t_high = roll(ext[pl.ds(at + 8 * v, 8), :], v + 1)
            else:
                t_low = roll(pop[3 * (v - 5), pl.ds(row, 8), :], v + 1)
                t_high = roll(pop[3 * (v - 5) + 2, pl.ds(row, 8), :], v + 1)
            near_low = jnp.where(lane == v + 1, t_low, near_low)
            near_high = jnp.where(lane == v, t_high, near_high)
        return (
            low + pltpu.roll(near_low, 16 * x, 1),
            high + pltpu.roll(near_high, 16 * x, 1),
        )

    zero8 = jnp.zeros((8, 128), F32)
    low, high = lax.fori_loop(0, 8, z_pack, (zero8, zero8))
    zsend[0] = low
    zsend[1] = high

    for fetch in fetches[3:]:
        fetch.wait()
    alive = live[0]

    def weight_step(n, _):
        first = pl.multiple_of(n * CHUNK, CHUNK)
        here = pl.ds(first, CHUNK)
        bx, by, bz = (base[d, :, here] for d in range(3))
        fx, fy, fz = (frac[d, :, here] for d in range(3))
        rows8 = lax.broadcasted_iota(jnp.int32, (8, CHUNK), 0)

        def hat(cells, b, fr):
            return jnp.where(cells == b, 1.0 - fr, jnp.where(cells == b + 1, fr, 0.0))

        wz_hi, wz_lo = split(hat(lax.broadcasted_iota(jnp.int32, (128, CHUNK), 0), bz, fz))
        wmat[pl.ds(0, 128), here] = wz_hi
        wmat[pl.ds(128, 128), here] = wz_lo
        wmat[pl.ds(256, 128), here] = wz_hi
        edges[pl.ds(0, 1), here] = jnp.where(bz == -1, 1.0 - fz, 0.0)
        edges[pl.ds(1, 1), here] = jnp.where(bz == 127, fz, 0.0)

        wx8 = hat(rows8, bx, fx)
        wy8 = hat(rows8, by, fy)
        x_low = jnp.where(bx == -1, 1.0 - fx, 0.0)
        x_high = jnp.where(bx == 7, fx, 0.0)
        y_low = jnp.where(by == -1, 1.0 - fy, 0.0)
        y_high = jnp.where(by == 7, fy, 0.0)
        plane = [wx8[x : x + 1] * wy8 for x in range(8)]
        plane += [x_low * wy8, x_high * wy8, y_low * wx8, y_high * wx8]
        edge = jnp.where(rows8 < 2, x_low, x_high) * jnp.where((rows8 & 1) == 0, y_low, y_high)
        plane.append(jnp.where(rows8 < 4, edge, 0.0))
        plane = jnp.concatenate(plane + [jnp.zeros((24, CHUNK), F32)], axis=0)
        plane_of[:, here] = plane
        plane_hi, plane_lo = split(plane)
        pmat[pl.ds(0, 128), here] = plane_hi
        pmat[pl.ds(128, 128), here] = plane_lo

        slot = lax.broadcasted_iota(jnp.int32, (1, CHUNK), 1) + first
        own_temp = temp[:, here]
        target[:, here] = jnp.concatenate(
            [vel[d, :, here] for d in range(3)]
            + [own_temp, 0.05 * jnp.exp(3.0 * (own_temp - 0.5)), jnp.zeros((3, CHUNK), F32)],
            axis=0,
        )
        scale = jnp.where(rows8 < 3, 2.0, jnp.where(rows8 < 5, 1.0, 0.0))
        factor[:, here] = jnp.where(slot < alive, rate[:, here], 0.0) * scale
        return 0

    lax.fori_loop(0, PARCELS // CHUNK, weight_step, 0)

    def matrix_step(n, _):
        at = pl.multiple_of(n * 16, 16)
        hi, lo = split(ext[pl.ds(at, 16), :])
        amat[pl.ds(at, 16), pl.ds(0, 128)] = hi
        amat[pl.ds(at, 16), pl.ds(128, 128)] = hi
        amat[pl.ds(at, 16), pl.ds(256, 128)] = lo
        return 0

    pl.semaphore_wait(barrier, 26)

    def z_moves(send, recv):
        return [
            (
                send.at[(1 + dz) // 2],
                recv.at[(1 - dz) // 2, side_index(-dx, -dy)],
                (dx, dy, dz),
            )
            for (dx, dy, dz) in around
            if dz != 0
        ]

    def corner_moves(send, recv):
        return [(send.at[j], recv.at[j], (sx, sy, 0)) for j, (sx, sy) in enumerate(SIGNS)]

    copies1 = exchange(
        0,
        z_moves(zsend, zrecv)
        + corner_moves(csend, crecv)
        + [
            (ysend.at[1], ext.at[pl.ds(400, 40)], (0, 1, 0)),
            (ysend.at[0], ext.at[pl.ds(440, 40)], (0, -1, 0)),
            (ext.at[pl.ds(280, 40)], ext.at[pl.ds(320, 40)], (1, 0, 0)),
            (ext.at[pl.ds(0, 40)], ext.at[pl.ds(360, 40)], (-1, 0, 0)),
            (ybsend.at[1], ybrecv.at[0], (0, 1, 0)),
            (ybsend.at[0], ybrecv.at[1], (0, -1, 0)),
            (pop.at[pl.ds(18, 9), pl.ds(PITCH * 8 + 8, 8)], xbrecv.at[0], (1, 0, 0)),
            (pop.at[pl.ds(0, 9), pl.ds(PITCH + 8, 8)], xbrecv.at[1], (-1, 0, 0)),
        ],
    )

    lax.fori_loop(0, 20, matrix_step, 0)

    def sample(first_slot, last_slot, along, here, off):
        sums = []
        for c in range(5):
            total = None
            for s in range(first_slot, last_slot):
                at = 8 * (5 * s + c) - off
                term = along[at : at + 8] * plane_of[pl.ds(8 * s, 8), here]
                total = term if total is None else total + term
            sums.append(jnp.sum(total, axis=0, keepdims=True))
        return jnp.concatenate(sums + [jnp.zeros((3, CHUNK), F32)], axis=0)

    def own_step(n, _):
        here = pl.ds(pl.multiple_of(n * CHUNK, CHUNK), CHUNK)
        along = jnp.dot(amat[pl.ds(0, 320), :], wmat[:, here], preferred_element_type=F32)
        sampled[:, here] = sample(0, 8, along, here, 0)
        return 0

    lax.fori_loop(0, PARCELS // CHUNK, own_step, 0)
    dep[...] = jnp.zeros_like(dep)
    rim[...] = jnp.zeros_like(rim)

    for copy in copies1:
        copy.wait_recv()

    for j in range(4):
        ext[pl.ds(480 + j, 5, stride=8), :] = crecv[j, pl.ds(0, 5), :]
    for c in range(5):
        ext[pl.ds(480 + 8 * c + 4, 4), :] = jnp.zeros((4, 128), F32)
    ext[pl.ds(520, 8), :] = zero8

    rimf[pl.ds(104, 24), :] = jnp.zeros((24, 128), F32)
    for s in range(13):
        sides = []
        for side in range(2):
            if s < 8:
                t = roll(zrecv[side, side_index(0, 0)], -16 * s - side)
            elif s < 10:
                dx = (-1, 1)[s - 8]
                t = roll(zrecv[side, side_index(dx, 0)], -(112, 0)[s - 8] - side)
            elif s < 12:
                dy = (-1, 1)[s - 10]
                t = spread_row(zrecv[side, side_index(0, dy)], (7, 0)[s - 10])
                t = skew(roll(t, -side), -16)
            else:
                t = zero8
                for j in range(4):
                    got = zrecv[side, side_index((-1, 1)[j // 2], (-1, 1)[j % 2])]
                    got = roll(got, -(112, 0)[j // 2] - side)
                    t = jnp.where(sub == j, spread_row(got, (7, 0)[j % 2]), t)
            zslot[side, pl.ds(8 * s, 8), :] = t
            sides.append(t)
        both = jnp.where(lane < 8, sides[0], roll(sides[1], 8))
        rimf[pl.ds(8 * s, 8), :] = jnp.where((lane < 16) & (low_lane < 5), both, 0.0)
    fields_hi, fields_lo = split(jnp.transpose(rimf[...])[:16])
    rim_left = jnp.concatenate(
        [
            jnp.concatenate([fields_hi, fields_hi], axis=1),
            jnp.concatenate([fields_lo, fields_lo], axis=1),
        ],
        axis=0,
    )

    lax.fori_loop(20, 33, matrix_step, 0)

    def chunk_step(n, _):
        here = pl.ds(pl.multiple_of(n * CHUNK, CHUNK), CHUNK)
        below = edges[pl.ds(0, 1), here]
        above = edges[pl.ds(1, 1), here]
        along = jnp.dot(amat[pl.ds(320, 208), :], wmat[:, here], preferred_element_type=F32)
        got = sampled[:, here] + sample(8, 13, along, here, 320)
        ends = jnp.dot(rim_left, pmat[:, here], preferred_element_type=F32)
        ends = ends[:16] + ends[16:]
        got = got + below * ends[:8] + above * ends[8:]
        terms = factor[:, here] * (target[:, here] - got)
        for d in range(3):
            mo[d, :, here] = target[pl.ds(d, 1), here] - 0.5 * terms[d : d + 1]

        load = [
            plane_of[pl.ds(8 * s, 8), here] * terms[c : c + 1] for s in range(13) for c in range(5)
        ]
        load.append(jnp.zeros((8, CHUNK), F32))
        load_hi, load_lo = split(jnp.concatenate(load, axis=0))
        got_hi = lax.dot_general(
            load_hi, wmat[pl.ds(0, 256), here], NT, preferred_element_type=F32
        )
        got_lo = lax.dot_general(
            load_lo, wmat[pl.ds(0, 128), here], NT, preferred_element_type=F32
        )
        dep[...] += got_hi[:, :128] + got_hi[:, 128:] + got_lo

        side_hi, side_lo = split(jnp.concatenate([terms * below, terms * above], axis=0))
        edge_hi = lax.dot_general(side_hi, pmat[:, here], NT, preferred_element_type=F32)
        edge_lo = lax.dot_general(
            side_lo, pmat[pl.ds(0, 128), here], NT, preferred_element_type=F32
        )
        rim[pl.ds(0, 16), :] += edge_hi[:, :128] + edge_hi[:, 128:] + edge_lo
        return 0

    lax.fori_loop(0, PARCELS // CHUNK, chunk_step, 0)

    by_row = jnp.transpose(rim[...])
    low = zero8
    high = zero8
    for s in range(13):
        v = by_row[8 * s : 8 * s + 8]
        own = [dep[pl.ds(8 * (5 * s + c), 8), :] for c in range(5)]
        mine = group == s
        low = jnp.where(mine, roll(v, 8 * s), low)
        high = jnp.where(mine, roll(v, 8 * s - 8), high)
    ring = jnp.where(
        low_lane == 0,
        roll(low, -4) + 3.0 * roll(low, -2),
        jnp.where(
            low_lane < 3,
            roll(low, 1),
            jnp.where(low_lane == 4, high - 3.0 * roll(high, 2), roll(high, 5)),
        ),
    )
    for s in range(13):
        own = [dep[pl.ds(8 * (5 * s + c), 8), :] for c in range(5)]
        lean = 3.0 * own[2]
        for v, (a, b) in enumerate([(own[4] - lean, own[4] + lean), (own[0],) * 2, (own[1],) * 2]):
            at = 8 * s + 5 + v
            low = jnp.where(lane == at, roll(a, at), low)
            high = jnp.where(lane == at, roll(b, at + 1), high)
    z2send[0] = low
    z2send[1] = high

    def fill(send, blocks, singles, at):
        for n, block in enumerate(blocks):
            send[pl.ds(40 * n, 40), :] = block
        for n, (x, y) in enumerate(singles):
            s, r = place_of(x, y)
            send[pl.ds(at + 8 * n, 5), :] = dep[pl.ds(40 * s + r, 5, stride=8), :]
        send[pl.ds(at + 32, 8), :] = ring

    far = {1: (7, 8), -1: (0, -1)}
    for n, sign in enumerate((-1, 1)):
        a, b = far[sign]
        fill(
            x2send.at[n],
            [dep[pl.ds(40 * place_of(x, 0)[0], 40), :] for x in (a, b)],
            [(a, -1), (a, 8), (b, -1), (b, 8)],
            80,
        )
        for c in range(5):
            y2send[n, pl.ds(8 * c, 8), :] = dep[pl.ds(8 * c + a, 8, stride=40), :]
        y2send[n, pl.ds(40, 40), :] = dep[pl.ds(40 * place_of(0, b)[0], 40), :]
        fill(y2send.at[n], [], [(-1, a), (8, a), (-1, b), (8, b)], 80)
    for j, (sx, sy) in enumerate(SIGNS):
        fill(c2send.at[j], [], [(x, y) for x in far[sx] for y in far[sy]], 0)

    copies2 = exchange(
        1,
        z_moves(z2send, z2recv)
        + corner_moves(c2send, c2recv)
        + [
            (y2send.at[1], y2recv.at[0], (0, 1, 0)),
            (y2send.at[0], y2recv.at[1], (0, -1, 0)),
            (x2send.at[1], x2recv.at[0], (1, 0, 0)),
            (x2send.at[0], x2recv.at[1], (-1, 0, 0)),
        ],
    )
    for copy in copies1:
        copy.wait_send()
    for copy in copies2:
        copy.wait_recv()

    rings = {(0, 0): ring}
    for n, sign in enumerate((-1, 1)):
        rings[sign, 0] = x2recv[n, pl.ds(112, 8), :]
        rings[0, sign] = y2recv[n, pl.ds(112, 8), :]
    for j, (sx, sy) in enumerate(SIGNS):
        rings[-sx, -sy] = c2recv[j, pl.ds(32, 8), :]
    layers = []
    for side in range(2):
        acc = None
        for (dx, dy), ring_at in rings.items():
            t = z2recv[side, side_index(dx, dy)]
            t += jnp.where(low_lane >= 5, roll(ring_at, (5, 1)[side]), 0.0)
            xs = {0: range(-1, 9), -1: (-1, 0), 1: (7, 8)}[dx]
            ys = {0: range(-1, 9), -1: (-1, 0), 1: (7, 8)}[dy]
            singles = [(x, y) for x in xs for y in ys]
            if dx == 0 and dy == 0:
                acc = t
                continue
            if dy == 0:
                for x in xs:
                    s = place_of(x, 0)[0]
                    s_from = place_of(x - 8 * dx, 0)[0]
                    acc += jnp.where(group == s, roll(t, 8 * (s - s_from)), 0.0)
                singles = [(x, y) for (x, y) in singles if y in (-1, 8)]
            if dx == 0:
                row, s, s_from = (7, 10, 11) if dy == -1 else (0, 11, 10)
                rows = roll(skew(spread_row(t, row), -8), 8 * s)
                acc += jnp.where(group == s, rows, 0.0)
                rows = jnp.where(group == 0, roll(t, -8 * s_from), 0.0)
                rows = jnp.sum(skew(rows, 8), axis=0, keepdims=True)
                acc += jnp.where(sub == 7 - row, rows, 0.0)
                singles = [(x, y) for (x, y) in singles if x in (-1, 8)]
            for x, y in singles:
                s, r = place_of(x, y)
                s_from, r_from = place_of(x - 8 * dx, y - 8 * dy)
                got = spread_row(roll(t, 8 * (s - s_from)), r_from)
                acc += jnp.where((group == s) & (sub == r), got, 0.0)
        layers.append(acc)

    for s in range(13):
        for c in range(5):
            at = 8 * (5 * s + c)
            k = 8 * s + c
            v = dep[pl.ds(at, 8), :]
            v += jnp.where(lane == 0, roll(layers[0], -k), 0.0)
            v += jnp.where(lane == 127, roll(layers[1], 127 - k), 0.0)
            src[pl.ds(at, 8), :] = v
    def take(recv, singles, at):
        for n, (x, y) in enumerate(singles):
            s, r = place_of(x, y)
            src[pl.ds(40 * s + r, 5, stride=8), :] += recv[pl.ds(at + 8 * n, 5), :]

    near = {-1: (-1, 0), 1: (8, 7)}
    for n, sign in enumerate((-1, 1)):
        a, b = near[sign]
        for m, x in enumerate((a, b)):
            src[pl.ds(40 * place_of(x, 0)[0], 40), :] += x2recv[n, pl.ds(40 * m, 40), :]
        take(x2recv.at[n], [(a, -1), (a, 8), (b, -1), (b, 8)], 80)
        src[pl.ds(40 * place_of(0, a)[0], 40), :] += y2recv[n, pl.ds(0, 40), :]
        for c in range(5):
            src[pl.ds(8 * c + b, 8, stride=40), :] += y2recv[n, pl.ds(40 + 8 * c, 8), :]
        take(y2recv.at[n], [(-1, a), (8, a), (-1, b), (8, b)], 80)
    for j, (sx, sy) in enumerate(SIGNS):
        take(c2recv.at[j], [(x, y) for x in near[-sx] for y in near[-sy]], 0)

    def push_step(x, _):
        at = pl.multiple_of(x * 40, 8)
        to_row = pl.multiple_of(PITCH * (x + 1) + 8, 8)
        s = [src[pl.ds(at + 8 * c, 8), :] for c in range(5)]
        to[x] = gt[x] + s[3]
        vo[x] = gv[x] + s[4]
        for q in range(27):
            pop[q, pl.ds(to_row, 8), :] += push_of(q, s)
        return 0

    lax.fori_loop(0, 8, push_step, 0)
    s8, s9, s10, s11, s12 = (
        [src[pl.ds(8 * (5 * s + c), 8), :] for c in range(5)] for s in range(8, 13)
    )
    for k in range(9):
        pop[18 + k, pl.ds(8, 8), :] = xbrecv[0, k] + push_of(18 + k, s8)
        pop[k, pl.ds(PITCH * 9 + 8, 8), :] = xbrecv[1, k] + push_of(k, s9)
        q = Y_UP[k]
        pop[q, pl.ds(PITCH + 7, 8, stride=PITCH), :] = (
            ybrecv[0, pl.ds(8 * k, 8), :] + push_of(q, s10)
        )
        q = Y_DOWN[k]
        pop[q, pl.ds(PITCH + 16, 8, stride=PITCH), :] = (
            ybrecv[1, pl.ds(8 * k, 8), :] + push_of(q, s11)
        )
    for j, (sx, sy) in enumerate(SIGNS):
        row = PITCH * (0, 9)[j // 2] + (7, 16)[j % 2]
        for k in range(3):
            q = 9 * (sx + 1) + 3 * (sy + 1) + k
            total = crecv[j, pl.ds(5 + k, 1), :] + push_of(q, s12)[j : j + 1]
            pop[q, pl.ds(row, 1), :] = total

    number = lane - 5
    used = (number >= 0) & (number < 9)
    step_x = jnp.where(number < 3, -1.0, jnp.where(number < 6, 0.0, 1.0))
    third = jnp.where(number < 3, number, jnp.where(number < 6, number - 3, number - 6))
    step_y = jnp.where(third == 0, -1.0, jnp.where(third == 1, 0.0, 1.0))
    share = jnp.where(step_x == 0.0, 2.0 / 3.0, 1.0 / 6.0)
    share = share * jnp.where(step_y == 0.0, 2.0 / 3.0, 1.0 / 6.0)
    share = jnp.where(used, share * (1.0 / 6.0), 0.0)
    share_x = 3.0 * share * step_x
    share_y = 3.0 * share * step_y
    for side in range(2):
        for s in range(13):
            three = [
                jnp.broadcast_to(layers[side][:, 8 * s + v : 8 * s + v + 1], (8, 128))
                for v in (5, 6, 7)
            ]
            t = zslot[side, pl.ds(8 * s, 8), :]
            t = t + share * three[0] + share_x * three[1] + share_y * three[2]
            if s < 8:
                zcol[side, pl.ds(PITCH * (s + 1) + 8, 8), :] = t
            elif s < 10:
                zcol[side, pl.ds(PITCH * (0, 9)[s - 8] + 8, 8), :] = t
            elif s < 12:
                zcol[side, pl.ds(PITCH + (7, 16)[s - 10], 8, stride=PITCH), :] = t
            else:
                for j in range(4):
                    row = PITCH * (0, 9)[j // 2] + (7, 16)[j % 2]
                    zcol[side, pl.ds(row, 1), :] = t[j : j + 1]

    written = write([(to, to_out), (vo, vo_out), (mo, mo_out)], 0)
    for part in range(9):
        for q in range(3 * part, 3 * part + 3):
            ex, ey, ez = step_of(q)
            m = q // 3 + 5
            for x in range(8):
                row = PITCH * (x - ex + 1) + 8 - ey
                v = pop[q, pl.ds(row, 8), :]
                if ez == 1:
                    v = jnp.where(lane == 0, roll(zcol[0, pl.ds(row, 8), :], -m), roll(v, 1))
                elif ez == -1:
                    v = jnp.where(
                        lane == 127, roll(zcol[1, pl.ds(row, 8), :], 127 - m), roll(v, -1)
                    )
                staged[q, x] = v
        here = pl.ds(3 * part, 3)
        written += write([(staged.at[here], fo.at[here])], 3 + part)

    for copy in copies2:
        copy.wait_send()
    for copy in written:
        copy.wait()


def keep_kernel(a0, a1, a2, a3, b0, b1, b2, b3, t0, t1, t2, t3, sem):
    trips = []
    for part in range(3):
        here = pl.ds(9 * part, 9)
        trips.append((a0.at[here], t0.at[here], b0.at[here]))
    trips += [(a1, t1, b1), (a2, t2, b2), (a3, t3, b3)]
    copies = []
    for n, (a, t, _) in enumerate(trips):
        copy = pltpu.make_async_copy(a, t, sem.at[0, n])
        copy.start()
        copies.append(copy)
    outs = []
    for n, (_, t, b) in enumerate(trips):
        copies[n].wait()
        copy = pltpu.make_async_copy(t, b, sem.at[1, n])
        copy.start()
        outs.append(copy)
    for copy in outs:
        copy.wait()


def on_device(f, gt, gv, base, frac, vel, temp, rate, live):
    anywhere = pl.BlockSpec(memory_space=pl.ANY)

    def buffer(*shape, dtype=F32):
        return pltpu.VMEM(shape, dtype)

    results = (
        jax.ShapeDtypeStruct(f.shape, F32),
        jax.ShapeDtypeStruct(gt.shape, F32),
        jax.ShapeDtypeStruct(gv.shape, F32),
        jax.ShapeDtypeStruct((3, 1, PARCELS), F32),
    )
    inner = pl.pallas_call(
        gather_kernel,
        out_shape=results,
        in_specs=[anywhere] * 8 + [pl.BlockSpec(memory_space=pltpu.SMEM)],
        out_specs=[anywhere] * 4,
        scratch_shapes=[
            buffer(27, 10 * PITCH, 128),
            buffer(2, 10 * PITCH, 128),
            buffer(8, 8, 128),
            buffer(8, 8, 128),
            buffer(3, 1, PARCELS),
            buffer(27, 8, 8, 128),
            buffer(27, 8, 8, 128),
            buffer(8, 8, 128),
            buffer(8, 8, 128),
            buffer(3, 1, PARCELS, dtype=jnp.int32),
            buffer(3, 1, PARCELS),
            buffer(3, 1, PARCELS),
            buffer(1, PARCELS),
            buffer(1, PARCELS),
            buffer(528, 128),
            buffer(2, 40, 128),
            buffer(4, 8, 128),
            buffer(4, 8, 128),
            buffer(2, 8, 128),
            buffer(2, 9, 8, 128),
            buffer(2, 72, 128),
            buffer(2, 72, 128),
            buffer(2, 9, 8, 128),
            buffer(528, 384, dtype=BF16),
            buffer(384, PARCELS, dtype=BF16),
            buffer(256, PARCELS, dtype=BF16),
            buffer(128, PARCELS),
            buffer(8, PARCELS),
            buffer(8, PARCELS),
            buffer(8, PARCELS),
            buffer(8, PARCELS),
            buffer(528, 128),
            buffer(128, 128),
            buffer(2, 104, 128),
            buffer(128, 128),
            buffer(2, 120, 128),
            buffer(2, 120, 128),
            buffer(2, 120, 128),
            buffer(2, 120, 128),
            buffer(4, 40, 128),
            buffer(4, 40, 128),
            buffer(2, 8, 128),
            buffer(2, 9, 8, 128),
            buffer(528, 128),
            pltpu.SemaphoreType.DMA((8,)),
            pltpu.SemaphoreType.DMA((12,)),
            pltpu.SemaphoreType.DMA((2, 30)),
            pltpu.SemaphoreType.DMA((2, 30)),
        ],
        compiler_params=pltpu.CompilerParams(
            collective_id=0, has_side_effects=True, vmem_limit_bytes=56 * 1024 * 1024
        ),
    )(
        f,
        gt,
        gv,
        base.reshape(3, 1, PARCELS),
        frac.reshape(3, 1, PARCELS),
        vel.reshape(3, 1, PARCELS),
        temp.reshape(1, PARCELS),
        rate.reshape(1, PARCELS),
        live.reshape(1),
    )
    fo, to, vo, mo = pl.pallas_call(
        keep_kernel,
        out_shape=results,
        in_specs=[anywhere] * 4,
        out_specs=[anywhere] * 4,
        scratch_shapes=[
            buffer(*f.shape),
            buffer(*gt.shape),
            buffer(*gv.shape),
            buffer(3, 1, PARCELS),
            pltpu.SemaphoreType.DMA((2, 6)),
        ],
        compiler_params=pltpu.CompilerParams(vmem_limit_bytes=56 * 1024 * 1024),
    )(*inner)
    return fo, to, vo, mo.reshape(vel.shape)


def solution(mesh):
    placed = (
        P(None, "gx", "gy", "gz"),
        P("gx", "gy", "gz"),
        P("gx", "gy", "gz"),
        P(None, "gx", "gy", "gz", None),
        P(None, "gx", "gy", "gz", None),
        P(None, "gx", "gy", "gz", None),
        P("gx", "gy", "gz", None),
        P("gx", "gy", "gz", None),
        P("gx", "gy", "gz"),
    )
    return jax.shard_map(
        on_device,
        mesh=mesh,
        in_specs=placed,
        out_specs=(
            P(None, "gx", "gy", "gz"),
            P("gx", "gy", "gz"),
            P("gx", "gy", "gz"),
            P(None, "gx", "gy", "gz", None),
        ),
        check_vma=False,
    )
```

```python
import jax
import jax.numpy as jnp
from jax import lax
from jax.experimental import pallas as pl
from jax.experimental.pallas import tpu as pltpu
from jax.sharding import PartitionSpec as P

AXES = ("gx", "gy", "gz")
CHUNK = 1024
PARCELS = 2048
PITCH = 24
F32 = jnp.float32
BF16 = jnp.bfloat16
MESH = pl.DeviceIdType.MESH
NT = (((1,), (1,)), ((), ()))


def step_of(q):
    return q // 9 - 1, q // 3 % 3 - 1, q % 3 - 1


def weight_of(q):
    value = 1.0
    for step in step_of(q):
        value = value * (2.0 / 3.0 if step == 0 else 1.0 / 6.0)
    return value


def roll(v, k):
    k = k % 128
    return pltpu.roll(v, k, 1) if k else v


def split(v):
    hi = v.astype(BF16)
    lo = (v - hi.astype(F32)).astype(BF16)
    return hi, lo


def side_index(dx, dy):
    return 3 * (dx + 1) + dy + 1


def place_of(x, y):
    if 0 <= x < 8:
        return (x, y) if 0 <= y < 8 else (10 if y < 0 else 11, x)
    if 0 <= y < 8:
        return 8 if x < 0 else 9, y
    return 12, 2 * (x > 0) + (y > 0)


SIGNS = [(1, 1), (1, -1), (-1, 1), (-1, -1)]
Y_UP = [9 * a + 6 + b for a in range(3) for b in range(3)]
Y_DOWN = [9 * a + b for a in range(3) for b in range(3)]


def push_of(q, s):
    push = s[4]
    e = step_of(q)
    for axis in range(3):
        if e[axis] == 1:
            push = push + 3.0 * s[axis]
        elif e[axis] == -1:
            push = push - 3.0 * s[axis]
    return weight_of(q) * push


def gather_kernel(
    f_in, gt_in, gv_in, base_in, frac_in, vel_in, temp_in, rate_in, live,
    fo, to_out, vo_out, mo_out,
    pop, zcol, to, vo, mo, staged,
    f, gt, gv, base, frac, vel, temp, rate,
    ext, ysend, csend, crecv, zsend, zrecv, ybsend, ybrecv, xbrecv,
    amat, wmat, pmat, plane_of, target, factor, sampled, edges,
    dep, rim, zslot, rimf,
    x2send, x2recv, y2send, y2recv, c2send, c2recv, z2send, z2recv, src,
    in_sem, out_sem, send_sem, recv_sem,
):
    me = [lax.axis_index(a) for a in AXES]
    size = [lax.axis_size(a) for a in AXES]

    def device(d):
        return tuple(
            me[i] if d[i] == 0 else lax.rem(me[i] + (d[i] + size[i]), size[i]) for i in range(3)
        )

    around = [
        (dx, dy, dz)
        for dz in (-1, 1, 0)
        for dx in (-1, 1, 0)
        for dy in (-1, 1, 0)
        if (dx, dy, dz) != (0, 0, 0)
    ]
    barrier = pltpu.get_barrier_semaphore()
    for d in around:
        pl.semaphore_signal(barrier, inc=1, device_id=device(d), device_id_type=MESH)

    fetches = []
    for n, (a, b) in enumerate(
        [
            (f_in, f), (gt_in, gt), (gv_in, gv), (base_in, base), (frac_in, frac),
            (vel_in, vel), (temp_in, temp), (rate_in, rate),
        ]
    ):
        fetch = pltpu.make_async_copy(a, b, in_sem.at[n])
        fetch.start()
        fetches.append(fetch)

    def write(pairs, at):
        copies = []
        for n, (a, b) in enumerate(pairs):
            copy = pltpu.make_async_copy(a, b, out_sem.at[at + n])
            copy.start()
            copies.append(copy)
        return copies

    def exchange(phase, moves, at=0):
        copies = []
        for n, (a, b, d) in enumerate(moves, start=at):
            copy = pltpu.make_async_remote_copy(
                src_ref=a,
                dst_ref=b,
                send_sem=send_sem.at[phase, n],
                recv_sem=recv_sem.at[phase, n],
                device_id=device(d),
                device_id_type=MESH,
            )
            copy.start()
            copies.append(copy)
        return copies

    lane = lax.broadcasted_iota(jnp.int32, (8, 128), 1)
    sub = lax.broadcasted_iota(jnp.int32, (8, 128), 0)
    low_lane = lane & 7
    group = lane >> 3

    def skew(v, amount):
        for bit in range(3):
            v = jnp.where((sub >> bit) & 1 == 1, roll(v, amount << bit), v)
        return v

    def spread_row(v, row):
        return jnp.broadcast_to(v[row : row + 1], (8, 128))

    for fetch in fetches[:3]:
        fetch.wait()

    def moment_step(x, _):
        at = pl.multiple_of(x * 40, 8)
        to_row = pl.multiple_of(PITCH * (x + 1) + 8, 8)
        pops = [f[q, x] for q in range(27)]
        total = pops[0]
        for q in range(1, 27):
            total = total + pops[q]
        u = []
        for axis in range(3):
            up = None
            for q in range(27):
                e = step_of(q)[axis]
                if e == 1:
                    up = pops[q] if up is None else up + pops[q]
                elif e == -1:
                    up = -pops[q] if up is None else up - pops[q]
            u.append(up / total)
            ext[pl.ds(at + 8 * axis, 8), :] = u[axis]
        ext[pl.ds(at + 24, 8), :] = gt[x]
        ext[pl.ds(at + 32, 8), :] = gv[x]
        rest = 1.0 - 1.5 * (u[0] * u[0] + u[1] * u[1] + u[2] * u[2])
        for q in range(27):
            e = step_of(q)
            along = None
            for axis in range(3):
                if e[axis] != 0:
                    term = u[axis] if e[axis] == 1 else -u[axis]
                    along = term if along is None else along + term
            inner = rest if along is None else rest + along * (3.0 + 4.5 * along)
            equil = (1.25 * weight_of(q)) * total * inner
            pop[q, pl.ds(to_row, 8), :] = equil - 0.25 * pops[q]
        return 0

    lax.fori_loop(0, 8, moment_step, 0)

    for c in range(5):
        for side in range(2):
            ysend[side, pl.ds(8 * c, 8), :] = ext[pl.ds(8 * c + 7 * side, 8, stride=40), :]
    for k in range(9):
        ybsend[0, pl.ds(8 * k, 8), :] = pop[Y_DOWN[k], pl.ds(PITCH + 8, 8, stride=PITCH), :]
        ybsend[1, pl.ds(8 * k, 8), :] = pop[Y_UP[k], pl.ds(PITCH + 15, 8, stride=PITCH), :]
    for j, (sx, sy) in enumerate(SIGNS):
        x, y = 7 if sx == 1 else 0, 7 if sy == 1 else 0
        csend[j, pl.ds(0, 5), :] = ext[pl.ds(40 * x + y, 5, stride=8), :]
        for k in range(3):
            q = 9 * (sx + 1) + 3 * (sy + 1) + k
            csend[j, pl.ds(5 + k, 1), :] = pop[q, pl.ds(PITCH * (x + 1) + 8 + y, 1), :]

    def z_pack(x, carry):
        low, high = carry
        at = pl.multiple_of(x * 40, 8)
        row = pl.multiple_of(PITCH * (x + 1) + 8, 8)
        near_low = jnp.zeros((8, 128), F32)
        near_high = jnp.zeros((8, 128), F32)
        for v in range(14):
            if v < 5:
                t_low = t_high = roll(ext[pl.ds(at + 8 * v, 8), :], v + 1)
            else:
                t_low = roll(pop[3 * (v - 5), pl.ds(row, 8), :], v + 1)
                t_high = roll(pop[3 * (v - 5) + 2, pl.ds(row, 8), :], v + 1)
            near_low = jnp.where(lane == v + 1, t_low, near_low)
            near_high = jnp.where(lane == v, t_high, near_high)
        return (
            low + pltpu.roll(near_low, 16 * x, 1),
            high + pltpu.roll(near_high, 16 * x, 1),
        )

    zero8 = jnp.zeros((8, 128), F32)
    low, high = lax.fori_loop(0, 8, z_pack, (zero8, zero8))
    zsend[0] = low
    zsend[1] = high

    for fetch in fetches[3:]:
        fetch.wait()
    alive = live[0]

    def weight_step(n, _):
        first = pl.multiple_of(n * CHUNK, CHUNK)
        here = pl.ds(first, CHUNK)
        bx, by, bz = (base[d, :, here] for d in range(3))
        fx, fy, fz = (frac[d, :, here] for d in range(3))
        rows8 = lax.broadcasted_iota(jnp.int32, (8, CHUNK), 0)

        def hat(cells, b, fr):
            return jnp.where(cells == b, 1.0 - fr, jnp.where(cells == b + 1, fr, 0.0))

        wz_hi, wz_lo = split(hat(lax.broadcasted_iota(jnp.int32, (128, CHUNK), 0), bz, fz))
        wmat[pl.ds(0, 128), here] = wz_hi
        wmat[pl.ds(128, 128), here] = wz_lo
        wmat[pl.ds(256, 128), here] = wz_hi
        edges[pl.ds(0, 1), here] = jnp.where(bz == -1, 1.0 - fz, 0.0)
        edges[pl.ds(1, 1), here] = jnp.where(bz == 127, fz, 0.0)
        edges[pl.ds(2, 1), here] = jnp.where(bz == -1, fz, 0.0)
        edges[pl.ds(3, 1), here] = jnp.where(bz == 127, 1.0 - fz, 0.0)

        wx8 = hat(rows8, bx, fx)
        wy8 = hat(rows8, by, fy)
        x_low = jnp.where(bx == -1, 1.0 - fx, 0.0)
        x_high = jnp.where(bx == 7, fx, 0.0)
        y_low = jnp.where(by == -1, 1.0 - fy, 0.0)
        y_high = jnp.where(by == 7, fy, 0.0)
        plane = [wx8[x : x + 1] * wy8 for x in range(8)]
        plane += [x_low * wy8, x_high * wy8, y_low * wx8, y_high * wx8]
        edge = jnp.where(rows8 < 2, x_low, x_high) * jnp.where((rows8 & 1) == 0, y_low, y_high)
        plane.append(jnp.where(rows8 < 4, edge, 0.0))
        plane = jnp.concatenate(plane + [jnp.zeros((24, CHUNK), F32)], axis=0)
        plane_of[:, here] = plane
        plane_hi, plane_lo = split(plane)
        pmat[pl.ds(0, 128), here] = plane_hi
        pmat[pl.ds(128, 128), here] = plane_lo

        slot = lax.broadcasted_iota(jnp.int32, (1, CHUNK), 1) + first
        own_temp = temp[:, here]
        target[:, here] = jnp.concatenate(
            [vel[d, :, here] for d in range(3)]
            + [own_temp, 0.05 * jnp.exp(3.0 * (own_temp - 0.5)), jnp.zeros((3, CHUNK), F32)],
            axis=0,
        )
        scale = jnp.where(rows8 < 3, 2.0, jnp.where(rows8 < 5, 1.0, 0.0))
        factor[:, here] = jnp.where(slot < alive, rate[:, here], 0.0) * scale
        return 0

    lax.fori_loop(0, PARCELS // CHUNK, weight_step, 0)

    def matrix_step(n, _):
        at = pl.multiple_of(n * 16, 16)
        hi, lo = split(ext[pl.ds(at, 16), :])
        amat[pl.ds(at, 16), pl.ds(0, 128)] = hi
        amat[pl.ds(at, 16), pl.ds(128, 128)] = hi
        amat[pl.ds(at, 16), pl.ds(256, 128)] = lo
        return 0

    pl.semaphore_wait(barrier, 26)

    def z_moves(send, recv):
        return [
            (
                send.at[(1 + dz) // 2],
                recv.at[(1 - dz) // 2, side_index(-dx, -dy)],
                (dx, dy, dz),
            )
            for (dx, dy, dz) in around
            if dz != 0
        ]

    def corner_moves(send, recv):
        return [(send.at[j], recv.at[j], (sx, sy, 0)) for j, (sx, sy) in enumerate(SIGNS)]

    copies1 = exchange(
        0,
        corner_moves(csend, crecv)
        + [
            (ysend.at[1], ext.at[pl.ds(400, 40)], (0, 1, 0)),
            (ysend.at[0], ext.at[pl.ds(440, 40)], (0, -1, 0)),
            (ext.at[pl.ds(280, 40)], ext.at[pl.ds(320, 40)], (1, 0, 0)),
            (ext.at[pl.ds(0, 40)], ext.at[pl.ds(360, 40)], (-1, 0, 0)),
        ],
    )
    copies_z = exchange(0, z_moves(zsend, zrecv), 8)
    copies_b = exchange(
        0,
        [
            (ybsend.at[1], ybrecv.at[0], (0, 1, 0)),
            (ybsend.at[0], ybrecv.at[1], (0, -1, 0)),
            (pop.at[pl.ds(18, 9), pl.ds(PITCH * 8 + 8, 8)], xbrecv.at[0], (1, 0, 0)),
            (pop.at[pl.ds(0, 9), pl.ds(PITCH + 8, 8)], xbrecv.at[1], (-1, 0, 0)),
        ],
        26,
    )

    lax.fori_loop(0, 20, matrix_step, 0)

    def sample(first_slot, last_slot, along, here, off):
        sums = []
        for c in range(5):
            total = None
            for s in range(first_slot, last_slot):
                at = 8 * (5 * s + c) - off
                term = along[at : at + 8] * plane_of[pl.ds(8 * s, 8), here]
                total = term if total is None else total + term
            sums.append(jnp.sum(total, axis=0, keepdims=True))
        return jnp.concatenate(sums + [jnp.zeros((3, CHUNK), F32)], axis=0)

    def own_step(n, _):
        here = pl.ds(pl.multiple_of(n * CHUNK, CHUNK), CHUNK)
        along = jnp.dot(amat[pl.ds(0, 320), :], wmat[:, here], preferred_element_type=F32)
        sampled[:, here] = sample(0, 8, along, here, 0)
        return 0

    lax.fori_loop(0, PARCELS // CHUNK, own_step, 0)
    dep[...] = jnp.zeros_like(dep)
    rim[...] = jnp.zeros_like(rim)

    for copy in copies1:
        copy.wait_recv()

    for j in range(4):
        ext[pl.ds(480 + j, 5, stride=8), :] = crecv[j, pl.ds(0, 5), :]
    for c in range(5):
        ext[pl.ds(480 + 8 * c + 4, 4), :] = jnp.zeros((4, 128), F32)
    ext[pl.ds(520, 8), :] = zero8

    lax.fori_loop(20, 33, matrix_step, 0)

    def chunk_step(n, _):
        here = pl.ds(pl.multiple_of(n * CHUNK, CHUNK), CHUNK)
        below = edges[pl.ds(0, 1), here]
        above = edges[pl.ds(1, 1), here]
        along = jnp.dot(amat[pl.ds(320, 208), :], wmat[:, here], preferred_element_type=F32)
        got = sampled[:, here] + sample(8, 13, along, here, 320)
        terms = factor[:, here] * (target[:, here] - got)
        for d in range(3):
            mo[d, :, here] = target[pl.ds(d, 1), here] - 0.5 * terms[d : d + 1]

        load = [
            plane_of[pl.ds(8 * s, 8), here] * terms[c : c + 1] for s in range(13) for c in range(5)
        ]
        load.append(jnp.zeros((8, CHUNK), F32))
        load_hi, load_lo = split(jnp.concatenate(load, axis=0))
        got_hi = lax.dot_general(
            load_hi, wmat[pl.ds(0, 256), here], NT, preferred_element_type=F32
        )
        got_lo = lax.dot_general(
            load_lo, wmat[pl.ds(0, 128), here], NT, preferred_element_type=F32
        )
        dep[...] += got_hi[:, :128] + got_hi[:, 128:] + got_lo

        side_hi, side_lo = split(jnp.concatenate([terms * below, terms * above], axis=0))
        edge_hi = lax.dot_general(side_hi, pmat[:, here], NT, preferred_element_type=F32)
        edge_lo = lax.dot_general(
            side_lo, pmat[pl.ds(0, 128), here], NT, preferred_element_type=F32
        )
        rim[pl.ds(0, 16), :] += edge_hi[:, :128] + edge_hi[:, 128:] + edge_lo
        return 0

    lax.fori_loop(0, PARCELS // CHUNK, chunk_step, 0)

    for copy in copies_z:
        copy.wait_recv()
    rimf[pl.ds(104, 24), :] = jnp.zeros((24, 128), F32)
    for s in range(13):
        sides = []
        for side in range(2):
            if s < 8:
                t = roll(zrecv[side, side_index(0, 0)], -16 * s - side)
            elif s < 10:
                dx = (-1, 1)[s - 8]
                t = roll(zrecv[side, side_index(dx, 0)], -(112, 0)[s - 8] - side)
            elif s < 12:
                dy = (-1, 1)[s - 10]
                t = spread_row(zrecv[side, side_index(0, dy)], (7, 0)[s - 10])
                t = skew(roll(t, -side), -16)
            else:
                t = zero8
                for j in range(4):
                    got = zrecv[side, side_index((-1, 1)[j // 2], (-1, 1)[j % 2])]
                    got = roll(got, -(112, 0)[j // 2] - side)
                    t = jnp.where(sub == j, spread_row(got, (7, 0)[j % 2]), t)
            zslot[side, pl.ds(8 * s, 8), :] = t
            sides.append(t)
        both = jnp.where(lane < 8, sides[0], roll(sides[1], 8))
        rimf[pl.ds(8 * s, 8), :] = jnp.where((lane < 16) & (low_lane < 5), both, 0.0)
    fields_hi, fields_lo = split(jnp.transpose(rimf[...])[:16])
    rim_left = jnp.concatenate(
        [
            jnp.concatenate([fields_hi, fields_hi], axis=1),
            jnp.concatenate([fields_lo, fields_lo], axis=1),
        ],
        axis=0,
    )

    def layer_step(n, _):
        here = pl.ds(pl.multiple_of(n * CHUNK, CHUNK), CHUNK)
        below, above, first, last = (edges[pl.ds(k, 1), here] for k in range(4))
        ends = jnp.dot(rim_left, pmat[:, here], preferred_element_type=F32)
        ends = ends[:16] + ends[16:]
        terms = -factor[:, here] * (below * ends[:8] + above * ends[8:])
        for d in range(3):
            mo[d, :, here] -= 0.5 * terms[d : d + 1]
        inside = [t[c : c + 1] for c in range(5) for t in (terms * last, terms * first)]
        left = jnp.concatenate(
            [terms * below, terms * above] + inside + [jnp.zeros((6, CHUNK), F32)], axis=0
        )
        left_hi, left_lo = split(left)
        got_hi = lax.dot_general(left_hi, pmat[:, here], NT, preferred_element_type=F32)
        got_lo = lax.dot_general(
            left_lo, pmat[pl.ds(0, 128), here], NT, preferred_element_type=F32
        )
        rim[pl.ds(0, 32), :] += got_hi[:, :128] + got_hi[:, 128:] + got_lo
        return 0

    lax.fori_loop(0, PARCELS // CHUNK, layer_step, 0)

    by_row = jnp.transpose(rim[...])
    outer = (lane == 0) | (lane == 127)
    low = zero8
    high = zero8
    for s in range(13):
        v = by_row[8 * s : 8 * s + 8]
        for c in range(5):
            dep[pl.ds(8 * (5 * s + c), 8), :] += jnp.where(outer, roll(v, -17 - 2 * c), 0.0)
        mine = group == s
        low = jnp.where(mine, roll(v, 8 * s), low)
        high = jnp.where(mine, roll(v, 8 * s - 8), high)
    ring = jnp.where(
        low_lane == 0,
        roll(low, -4) + 3.0 * roll(low, -2),
        jnp.where(
            low_lane < 3,
            roll(low, 1),
            jnp.where(low_lane == 4, high - 3.0 * roll(high, 2), roll(high, 5)),
        ),
    )
    for s in range(13):
        own = [dep[pl.ds(8 * (5 * s + c), 8), :] for c in range(5)]
        lean = 3.0 * own[2]
        for v, (a, b) in enumerate([(own[4] - lean, own[4] + lean), (own[0],) * 2, (own[1],) * 2]):
            at = 8 * s + 5 + v
            low = jnp.where(lane == at, roll(a, at), low)
            high = jnp.where(lane == at, roll(b, at + 1), high)
    z2send[0] = low
    z2send[1] = high

    def fill(send, blocks, singles, at):
        for n, block in enumerate(blocks):
            send[pl.ds(40 * n, 40), :] = block
        for n, (x, y) in enumerate(singles):
            s, r = place_of(x, y)
            send[pl.ds(at + 8 * n, 5), :] = dep[pl.ds(40 * s + r, 5, stride=8), :]
        send[pl.ds(at + 32, 8), :] = ring

    far = {1: (7, 8), -1: (0, -1)}
    for n, sign in enumerate((-1, 1)):
        a, b = far[sign]
        fill(
            x2send.at[n],
            [dep[pl.ds(40 * place_of(x, 0)[0], 40), :] for x in (a, b)],
            [(a, -1), (a, 8), (b, -1), (b, 8)],
            80,
        )
        for c in range(5):
            y2send[n, pl.ds(8 * c, 8), :] = dep[pl.ds(8 * c + a, 8, stride=40), :]
        y2send[n, pl.ds(40, 40), :] = dep[pl.ds(40 * place_of(0, b)[0], 40), :]
        fill(y2send.at[n], [], [(-1, a), (8, a), (-1, b), (8, b)], 80)
    for j, (sx, sy) in enumerate(SIGNS):
        fill(c2send.at[j], [], [(x, y) for x in far[sx] for y in far[sy]], 0)

    copies2 = exchange(
        1,
        z_moves(z2send, z2recv)
        + corner_moves(c2send, c2recv)
        + [
            (y2send.at[1], y2recv.at[0], (0, 1, 0)),
            (y2send.at[0], y2recv.at[1], (0, -1, 0)),
            (x2send.at[1], x2recv.at[0], (1, 0, 0)),
            (x2send.at[0], x2recv.at[1], (-1, 0, 0)),
        ],
    )
    for copy in copies1 + copies_z + copies_b:
        copy.wait_send()
    for copy in copies_b:
        copy.wait_recv()
    for copy in copies2:
        copy.wait_recv()

    rings = {(0, 0): ring}
    for n, sign in enumerate((-1, 1)):
        rings[sign, 0] = x2recv[n, pl.ds(112, 8), :]
        rings[0, sign] = y2recv[n, pl.ds(112, 8), :]
    for j, (sx, sy) in enumerate(SIGNS):
        rings[-sx, -sy] = c2recv[j, pl.ds(32, 8), :]
    layers = []
    for side in range(2):
        acc = None
        for (dx, dy), ring_at in rings.items():
            t = z2recv[side, side_index(dx, dy)]
            t += jnp.where(low_lane >= 5, roll(ring_at, (5, 1)[side]), 0.0)
            xs = {0: range(-1, 9), -1: (-1, 0), 1: (7, 8)}[dx]
            ys = {0: range(-1, 9), -1: (-1, 0), 1: (7, 8)}[dy]
            singles = [(x, y) for x in xs for y in ys]
            if dx == 0 and dy == 0:
                acc = t
                continue
            if dy == 0:
                for x in xs:
                    s = place_of(x, 0)[0]
                    s_from = place_of(x - 8 * dx, 0)[0]
                    acc += jnp.where(group == s, roll(t, 8 * (s - s_from)), 0.0)
                singles = [(x, y) for (x, y) in singles if y in (-1, 8)]
            if dx == 0:
                row, s, s_from = (7, 10, 11) if dy == -1 else (0, 11, 10)
                rows = roll(skew(spread_row(t, row), -8), 8 * s)
                acc += jnp.where(group == s, rows, 0.0)
                rows = jnp.where(group == 0, roll(t, -8 * s_from), 0.0)
                rows = jnp.sum(skew(rows, 8), axis=0, keepdims=True)
                acc += jnp.where(sub == 7 - row, rows, 0.0)
                singles = [(x, y) for (x, y) in singles if x in (-1, 8)]
            for x, y in singles:
                s, r = place_of(x, y)
                s_from, r_from = place_of(x - 8 * dx, y - 8 * dy)
                got = spread_row(roll(t, 8 * (s - s_from)), r_from)
                acc += jnp.where((group == s) & (sub == r), got, 0.0)
        layers.append(acc)

    for s in range(13):
        for c in range(5):
            at = 8 * (5 * s + c)
            k = 8 * s + c
            v = dep[pl.ds(at, 8), :]
            v += jnp.where(lane == 0, roll(layers[0], -k), 0.0)
            v += jnp.where(lane == 127, roll(layers[1], 127 - k), 0.0)
            src[pl.ds(at, 8), :] = v
    def take(recv, singles, at):
        for n, (x, y) in enumerate(singles):
            s, r = place_of(x, y)
            src[pl.ds(40 * s + r, 5, stride=8), :] += recv[pl.ds(at + 8 * n, 5), :]

    near = {-1: (-1, 0), 1: (8, 7)}
    for n, sign in enumerate((-1, 1)):
        a, b = near[sign]
        for m, x in enumerate((a, b)):
            src[pl.ds(40 * place_of(x, 0)[0], 40), :] += x2recv[n, pl.ds(40 * m, 40), :]
        take(x2recv.at[n], [(a, -1), (a, 8), (b, -1), (b, 8)], 80)
        src[pl.ds(40 * place_of(0, a)[0], 40), :] += y2recv[n, pl.ds(0, 40), :]
        for c in range(5):
            src[pl.ds(8 * c + b, 8, stride=40), :] += y2recv[n, pl.ds(40 + 8 * c, 8), :]
        take(y2recv.at[n], [(-1, a), (8, a), (-1, b), (8, b)], 80)
    for j, (sx, sy) in enumerate(SIGNS):
        take(c2recv.at[j], [(x, y) for x in near[-sx] for y in near[-sy]], 0)

    def push_step(x, _):
        at = pl.multiple_of(x * 40, 8)
        to_row = pl.multiple_of(PITCH * (x + 1) + 8, 8)
        s = [src[pl.ds(at + 8 * c, 8), :] for c in range(5)]
        to[x] = gt[x] + s[3]
        vo[x] = gv[x] + s[4]
        for q in range(27):
            pop[q, pl.ds(to_row, 8), :] += push_of(q, s)
        return 0

    lax.fori_loop(0, 8, push_step, 0)
    s8, s9, s10, s11, s12 = (
        [src[pl.ds(8 * (5 * s + c), 8), :] for c in range(5)] for s in range(8, 13)
    )
    for k in range(9):
        pop[18 + k, pl.ds(8, 8), :] = xbrecv[0, k] + push_of(18 + k, s8)
        pop[k, pl.ds(PITCH * 9 + 8, 8), :] = xbrecv[1, k] + push_of(k, s9)
        q = Y_UP[k]
        pop[q, pl.ds(PITCH + 7, 8, stride=PITCH), :] = (
            ybrecv[0, pl.ds(8 * k, 8), :] + push_of(q, s10)
        )
        q = Y_DOWN[k]
        pop[q, pl.ds(PITCH + 16, 8, stride=PITCH), :] = (
            ybrecv[1, pl.ds(8 * k, 8), :] + push_of(q, s11)
        )
    for j, (sx, sy) in enumerate(SIGNS):
        row = PITCH * (0, 9)[j // 2] + (7, 16)[j % 2]
        for k in range(3):
            q = 9 * (sx + 1) + 3 * (sy + 1) + k
            total = crecv[j, pl.ds(5 + k, 1), :] + push_of(q, s12)[j : j + 1]
            pop[q, pl.ds(row, 1), :] = total

    number = lane - 5
    used = (number >= 0) & (number < 9)
    step_x = jnp.where(number < 3, -1.0, jnp.where(number < 6, 0.0, 1.0))
    third = jnp.where(number < 3, number, jnp.where(number < 6, number - 3, number - 6))
    step_y = jnp.where(third == 0, -1.0, jnp.where(third == 1, 0.0, 1.0))
    share = jnp.where(step_x == 0.0, 2.0 / 3.0, 1.0 / 6.0)
    share = share * jnp.where(step_y == 0.0, 2.0 / 3.0, 1.0 / 6.0)
    share = jnp.where(used, share * (1.0 / 6.0), 0.0)
    share_x = 3.0 * share * step_x
    share_y = 3.0 * share * step_y
    for side in range(2):
        for s in range(13):
            three = [
                jnp.broadcast_to(layers[side][:, 8 * s + v : 8 * s + v + 1], (8, 128))
                for v in (5, 6, 7)
            ]
            t = zslot[side, pl.ds(8 * s, 8), :]
            t = t + share * three[0] + share_x * three[1] + share_y * three[2]
            if s < 8:
                zcol[side, pl.ds(PITCH * (s + 1) + 8, 8), :] = t
            elif s < 10:
                zcol[side, pl.ds(PITCH * (0, 9)[s - 8] + 8, 8), :] = t
            elif s < 12:
                zcol[side, pl.ds(PITCH + (7, 16)[s - 10], 8, stride=PITCH), :] = t
            else:
                for j in range(4):
                    row = PITCH * (0, 9)[j // 2] + (7, 16)[j % 2]
                    zcol[side, pl.ds(row, 1), :] = t[j : j + 1]

    written = write([(to, to_out), (vo, vo_out), (mo, mo_out)], 0)
    for part in range(9):
        for q in range(3 * part, 3 * part + 3):
            ex, ey, ez = step_of(q)
            m = q // 3 + 5
            for x in range(8):
                row = PITCH * (x - ex + 1) + 8 - ey
                v = pop[q, pl.ds(row, 8), :]
                if ez == 1:
                    v = jnp.where(lane == 0, roll(zcol[0, pl.ds(row, 8), :], -m), roll(v, 1))
                elif ez == -1:
                    v = jnp.where(
                        lane == 127, roll(zcol[1, pl.ds(row, 8), :], 127 - m), roll(v, -1)
                    )
                staged[q, x] = v
        here = pl.ds(3 * part, 3)
        written += write([(staged.at[here], fo.at[here])], 3 + part)

    for copy in copies2:
        copy.wait_send()
    for copy in written:
        copy.wait()


def keep_kernel(a0, a1, a2, a3, b0, b1, b2, b3, t0, t1, t2, t3, sem):
    trips = []
    for part in range(3):
        here = pl.ds(9 * part, 9)
        trips.append((a0.at[here], t0.at[here], b0.at[here]))
    trips += [(a1, t1, b1), (a2, t2, b2), (a3, t3, b3)]
    copies = []
    for n, (a, t, _) in enumerate(trips):
        copy = pltpu.make_async_copy(a, t, sem.at[0, n])
        copy.start()
        copies.append(copy)
    outs = []
    for n, (_, t, b) in enumerate(trips):
        copies[n].wait()
        copy = pltpu.make_async_copy(t, b, sem.at[1, n])
        copy.start()
        outs.append(copy)
    for copy in outs:
        copy.wait()


def on_device(f, gt, gv, base, frac, vel, temp, rate, live):
    anywhere = pl.BlockSpec(memory_space=pl.ANY)

    def buffer(*shape, dtype=F32):
        return pltpu.VMEM(shape, dtype)

    results = (
        jax.ShapeDtypeStruct(f.shape, F32),
        jax.ShapeDtypeStruct(gt.shape, F32),
        jax.ShapeDtypeStruct(gv.shape, F32),
        jax.ShapeDtypeStruct((3, 1, PARCELS), F32),
    )
    inner = pl.pallas_call(
        gather_kernel,
        out_shape=results,
        in_specs=[anywhere] * 8 + [pl.BlockSpec(memory_space=pltpu.SMEM)],
        out_specs=[anywhere] * 4,
        scratch_shapes=[
            buffer(27, 10 * PITCH, 128),
            buffer(2, 10 * PITCH, 128),
            buffer(8, 8, 128),
            buffer(8, 8, 128),
            buffer(3, 1, PARCELS),
            buffer(27, 8, 8, 128),
            buffer(27, 8, 8, 128),
            buffer(8, 8, 128),
            buffer(8, 8, 128),
            buffer(3, 1, PARCELS, dtype=jnp.int32),
            buffer(3, 1, PARCELS),
            buffer(3, 1, PARCELS),
            buffer(1, PARCELS),
            buffer(1, PARCELS),
            buffer(528, 128),
            buffer(2, 40, 128),
            buffer(4, 8, 128),
            buffer(4, 8, 128),
            buffer(2, 8, 128),
            buffer(2, 9, 8, 128),
            buffer(2, 72, 128),
            buffer(2, 72, 128),
            buffer(2, 9, 8, 128),
            buffer(528, 384, dtype=BF16),
            buffer(384, PARCELS, dtype=BF16),
            buffer(256, PARCELS, dtype=BF16),
            buffer(128, PARCELS),
            buffer(8, PARCELS),
            buffer(8, PARCELS),
            buffer(8, PARCELS),
            buffer(8, PARCELS),
            buffer(528, 128),
            buffer(128, 128),
            buffer(2, 104, 128),
            buffer(128, 128),
            buffer(2, 120, 128),
            buffer(2, 120, 128),
            buffer(2, 120, 128),
            buffer(2, 120, 128),
            buffer(4, 40, 128),
            buffer(4, 40, 128),
            buffer(2, 8, 128),
            buffer(2, 9, 8, 128),
            buffer(528, 128),
            pltpu.SemaphoreType.DMA((8,)),
            pltpu.SemaphoreType.DMA((12,)),
            pltpu.SemaphoreType.DMA((2, 30)),
            pltpu.SemaphoreType.DMA((2, 30)),
        ],
        compiler_params=pltpu.CompilerParams(
            collective_id=0, has_side_effects=True, vmem_limit_bytes=56 * 1024 * 1024
        ),
    )(
        f,
        gt,
        gv,
        base.reshape(3, 1, PARCELS),
        frac.reshape(3, 1, PARCELS),
        vel.reshape(3, 1, PARCELS),
        temp.reshape(1, PARCELS),
        rate.reshape(1, PARCELS),
        live.reshape(1),
    )
    fo, to, vo, mo = pl.pallas_call(
        keep_kernel,
        out_shape=results,
        in_specs=[anywhere] * 4,
        out_specs=[anywhere] * 4,
        scratch_shapes=[
            buffer(*f.shape),
            buffer(*gt.shape),
            buffer(*gv.shape),
            buffer(3, 1, PARCELS),
            pltpu.SemaphoreType.DMA((2, 6)),
        ],
        compiler_params=pltpu.CompilerParams(vmem_limit_bytes=56 * 1024 * 1024),
    )(*inner)
    return fo, to, vo, mo.reshape(vel.shape)


def solution(mesh):
    placed = (
        P(None, "gx", "gy", "gz"),
        P("gx", "gy", "gz"),
        P("gx", "gy", "gz"),
        P(None, "gx", "gy", "gz", None),
        P(None, "gx", "gy", "gz", None),
        P(None, "gx", "gy", "gz", None),
        P("gx", "gy", "gz", None),
        P("gx", "gy", "gz", None),
        P("gx", "gy", "gz"),
    )
    return jax.shard_map(
        on_device,
        mesh=mesh,
        in_specs=placed,
        out_specs=(
            P(None, "gx", "gy", "gz"),
            P("gx", "gy", "gz"),
            P("gx", "gy", "gz"),
            P(None, "gx", "gy", "gz", None),
        ),
        check_vma=False,
    )
```

```python
import jax
import jax.numpy as jnp
from jax import lax
from jax.experimental import pallas as pl
from jax.experimental.pallas import tpu as pltpu
from jax.sharding import PartitionSpec as P

AXES = ("gx", "gy", "gz")
CHUNK = 1024
PARCELS = 2048
PITCH = 24
F32 = jnp.float32
BF16 = jnp.bfloat16
MESH = pl.DeviceIdType.MESH
NT = (((1,), (1,)), ((), ()))


def step_of(q):
    return q // 9 - 1, q // 3 % 3 - 1, q % 3 - 1


def weight_of(q):
    value = 1.0
    for step in step_of(q):
        value = value * (2.0 / 3.0 if step == 0 else 1.0 / 6.0)
    return value


def roll(v, k):
    k = k % 128
    return pltpu.roll(v, k, 1) if k else v


def split(v):
    hi = v.astype(BF16)
    lo = (v - hi.astype(F32)).astype(BF16)
    return hi, lo


def side_index(dx, dy):
    return 3 * (dx + 1) + dy + 1


def place_of(x, y):
    if 0 <= x < 8:
        return (x, y) if 0 <= y < 8 else (10 if y < 0 else 11, x)
    if 0 <= y < 8:
        return 8 if x < 0 else 9, y
    return 12, 2 * (x > 0) + (y > 0)


SIGNS = [(1, 1), (1, -1), (-1, 1), (-1, -1)]
Y_UP = [9 * a + 6 + b for a in range(3) for b in range(3)]
Y_DOWN = [9 * a + b for a in range(3) for b in range(3)]


def push_of(q, s):
    push = s[4]
    e = step_of(q)
    for axis in range(3):
        if e[axis] == 1:
            push = push + 3.0 * s[axis]
        elif e[axis] == -1:
            push = push - 3.0 * s[axis]
    return weight_of(q) * push


def gather_kernel(
    f_in, gt_in, gv_in, base_in, frac_in, vel_in, temp_in, rate_in, live,
    fo, to_out, vo_out, mo_out,
    pop, zcol, to, vo, mo, staged,
    f, gt, gv, base, frac, vel, temp, rate,
    ext, ysend, csend, crecv, zsend, zrecv, ybsend, ybrecv, xbrecv,
    amat, wmat, pmat, plane_of, target, factor, sampled, edges, terms_of, left,
    dep, rim, zslot, rimf,
    x2send, x2recv, y2send, y2recv, c2send, c2recv, z2send, z2recv, src,
    in_sem, out_sem, send_sem, recv_sem,
):
    me = [lax.axis_index(a) for a in AXES]
    size = [lax.axis_size(a) for a in AXES]

    def device(d):
        return tuple(
            me[i] if d[i] == 0 else lax.rem(me[i] + (d[i] + size[i]), size[i]) for i in range(3)
        )

    around = [
        (dx, dy, dz)
        for dz in (-1, 1, 0)
        for dx in (-1, 1, 0)
        for dy in (-1, 1, 0)
        if (dx, dy, dz) != (0, 0, 0)
    ]
    barrier = pltpu.get_barrier_semaphore()
    for d in around:
        pl.semaphore_signal(barrier, inc=1, device_id=device(d), device_id_type=MESH)

    fetches = []
    for n, (a, b) in enumerate(
        [
            (f_in, f), (gt_in, gt), (gv_in, gv), (base_in, base), (frac_in, frac),
            (vel_in, vel), (temp_in, temp), (rate_in, rate),
        ]
    ):
        fetch = pltpu.make_async_copy(a, b, in_sem.at[n])
        fetch.start()
        fetches.append(fetch)

    def write(pairs, at):
        copies = []
        for n, (a, b) in enumerate(pairs):
            copy = pltpu.make_async_copy(a, b, out_sem.at[at + n])
            copy.start()
            copies.append(copy)
        return copies

    def exchange(phase, moves, at=0):
        copies = []
        for n, (a, b, d) in enumerate(moves, start=at):
            copy = pltpu.make_async_remote_copy(
                src_ref=a,
                dst_ref=b,
                send_sem=send_sem.at[phase, n],
                recv_sem=recv_sem.at[phase, n],
                device_id=device(d),
                device_id_type=MESH,
            )
            copy.start()
            copies.append(copy)
        return copies

    lane = lax.broadcasted_iota(jnp.int32, (8, 128), 1)
    sub = lax.broadcasted_iota(jnp.int32, (8, 128), 0)
    low_lane = lane & 7
    group = lane >> 3

    def skew(v, amount):
        for bit in range(3):
            v = jnp.where((sub >> bit) & 1 == 1, roll(v, amount << bit), v)
        return v

    def spread_row(v, row):
        return jnp.broadcast_to(v[row : row + 1], (8, 128))

    for fetch in fetches[:3]:
        fetch.wait()

    def moment_step(x, _):
        at = pl.multiple_of(x * 40, 8)
        to_row = pl.multiple_of(PITCH * (x + 1) + 8, 8)
        pops = [f[q, x] for q in range(27)]
        total = pops[0]
        for q in range(1, 27):
            total = total + pops[q]
        u = []
        for axis in range(3):
            up = None
            for q in range(27):
                e = step_of(q)[axis]
                if e == 1:
                    up = pops[q] if up is None else up + pops[q]
                elif e == -1:
                    up = -pops[q] if up is None else up - pops[q]
            u.append(up / total)
            ext[pl.ds(at + 8 * axis, 8), :] = u[axis]
        ext[pl.ds(at + 24, 8), :] = gt[x]
        ext[pl.ds(at + 32, 8), :] = gv[x]
        rest = 1.0 - 1.5 * (u[0] * u[0] + u[1] * u[1] + u[2] * u[2])
        for q in range(27):
            e = step_of(q)
            along = None
            for axis in range(3):
                if e[axis] != 0:
                    term = u[axis] if e[axis] == 1 else -u[axis]
                    along = term if along is None else along + term
            inner = rest if along is None else rest + along * (3.0 + 4.5 * along)
            equil = (1.25 * weight_of(q)) * total * inner
            pop[q, pl.ds(to_row, 8), :] = equil - 0.25 * pops[q]
        return 0

    lax.fori_loop(0, 8, moment_step, 0)

    for c in range(5):
        for side in range(2):
            ysend[side, pl.ds(8 * c, 8), :] = ext[pl.ds(8 * c + 7 * side, 8, stride=40), :]
    for k in range(9):
        ybsend[0, pl.ds(8 * k, 8), :] = pop[Y_DOWN[k], pl.ds(PITCH + 8, 8, stride=PITCH), :]
        ybsend[1, pl.ds(8 * k, 8), :] = pop[Y_UP[k], pl.ds(PITCH + 15, 8, stride=PITCH), :]
    for j, (sx, sy) in enumerate(SIGNS):
        x, y = 7 if sx == 1 else 0, 7 if sy == 1 else 0
        csend[j, pl.ds(0, 5), :] = ext[pl.ds(40 * x + y, 5, stride=8), :]
        for k in range(3):
            q = 9 * (sx + 1) + 3 * (sy + 1) + k
            csend[j, pl.ds(5 + k, 1), :] = pop[q, pl.ds(PITCH * (x + 1) + 8 + y, 1), :]

    def z_pack(x, carry):
        low, high = carry
        at = pl.multiple_of(x * 40, 8)
        row = pl.multiple_of(PITCH * (x + 1) + 8, 8)
        near_low = jnp.zeros((8, 128), F32)
        near_high = jnp.zeros((8, 128), F32)
        for v in range(14):
            if v < 5:
                t_low = t_high = roll(ext[pl.ds(at + 8 * v, 8), :], v + 1)
            else:
                t_low = roll(pop[3 * (v - 5), pl.ds(row, 8), :], v + 1)
                t_high = roll(pop[3 * (v - 5) + 2, pl.ds(row, 8), :], v + 1)
            near_low = jnp.where(lane == v + 1, t_low, near_low)
            near_high = jnp.where(lane == v, t_high, near_high)
        return (
            low + pltpu.roll(near_low, 16 * x, 1),
            high + pltpu.roll(near_high, 16 * x, 1),
        )

    zero8 = jnp.zeros((8, 128), F32)
    low, high = lax.fori_loop(0, 8, z_pack, (zero8, zero8))
    zsend[0] = low
    zsend[1] = high

    for fetch in fetches[3:]:
        fetch.wait()
    alive = live[0]

    def weight_step(n, _):
        first = pl.multiple_of(n * CHUNK, CHUNK)
        here = pl.ds(first, CHUNK)
        bx, by, bz = (base[d, :, here] for d in range(3))
        fx, fy, fz = (frac[d, :, here] for d in range(3))
        rows8 = lax.broadcasted_iota(jnp.int32, (8, CHUNK), 0)

        def hat(cells, b, fr):
            return jnp.where(cells == b, 1.0 - fr, jnp.where(cells == b + 1, fr, 0.0))

        wz_hi, wz_lo = split(hat(lax.broadcasted_iota(jnp.int32, (128, CHUNK), 0), bz, fz))
        wmat[pl.ds(0, 128), here] = wz_hi
        wmat[pl.ds(128, 128), here] = wz_lo
        wmat[pl.ds(256, 128), here] = wz_hi
        edges[pl.ds(0, 1), here] = jnp.where(bz == -1, 1.0 - fz, 0.0)
        edges[pl.ds(1, 1), here] = jnp.where(bz == 127, fz, 0.0)
        edges[pl.ds(2, 1), here] = hat(0, bz, fz)
        edges[pl.ds(3, 1), here] = hat(127, bz, fz)

        wx8 = hat(rows8, bx, fx)
        wy8 = hat(rows8, by, fy)
        x_low = jnp.where(bx == -1, 1.0 - fx, 0.0)
        x_high = jnp.where(bx == 7, fx, 0.0)
        y_low = jnp.where(by == -1, 1.0 - fy, 0.0)
        y_high = jnp.where(by == 7, fy, 0.0)
        plane = [wx8[x : x + 1] * wy8 for x in range(8)]
        plane += [x_low * wy8, x_high * wy8, y_low * wx8, y_high * wx8]
        edge = jnp.where(rows8 < 2, x_low, x_high) * jnp.where((rows8 & 1) == 0, y_low, y_high)
        plane.append(jnp.where(rows8 < 4, edge, 0.0))
        plane = jnp.concatenate(plane + [jnp.zeros((24, CHUNK), F32)], axis=0)
        plane_of[:, here] = plane
        plane_hi, plane_lo = split(plane)
        pmat[pl.ds(0, 128), here] = plane_hi
        pmat[pl.ds(128, 128), here] = plane_lo

        slot = lax.broadcasted_iota(jnp.int32, (1, CHUNK), 1) + first
        own_temp = temp[:, here]
        target[:, here] = jnp.concatenate(
            [vel[d, :, here] for d in range(3)]
            + [own_temp, 0.05 * jnp.exp(3.0 * (own_temp - 0.5)), jnp.zeros((3, CHUNK), F32)],
            axis=0,
        )
        scale = jnp.where(rows8 < 3, 2.0, jnp.where(rows8 < 5, 1.0, 0.0))
        factor[:, here] = jnp.where(slot < alive, rate[:, here], 0.0) * scale
        return 0

    lax.fori_loop(0, PARCELS // CHUNK, weight_step, 0)

    def matrix_step(n, _):
        at = pl.multiple_of(n * 16, 16)
        hi, lo = split(ext[pl.ds(at, 16), :])
        amat[pl.ds(at, 16), pl.ds(0, 128)] = hi
        amat[pl.ds(at, 16), pl.ds(128, 128)] = hi
        amat[pl.ds(at, 16), pl.ds(256, 128)] = lo
        return 0

    pl.semaphore_wait(barrier, 26)

    def z_moves(send, recv):
        return [
            (
                send.at[(1 + dz) // 2],
                recv.at[(1 - dz) // 2, side_index(-dx, -dy)],
                (dx, dy, dz),
            )
            for (dx, dy, dz) in around
            if dz != 0
        ]

    def corner_moves(send, recv):
        return [(send.at[j], recv.at[j], (sx, sy, 0)) for j, (sx, sy) in enumerate(SIGNS)]

    copies1 = exchange(
        0,
        corner_moves(csend, crecv)
        + [
            (ysend.at[1], ext.at[pl.ds(400, 40)], (0, 1, 0)),
            (ysend.at[0], ext.at[pl.ds(440, 40)], (0, -1, 0)),
            (ext.at[pl.ds(280, 40)], ext.at[pl.ds(320, 40)], (1, 0, 0)),
            (ext.at[pl.ds(0, 40)], ext.at[pl.ds(360, 40)], (-1, 0, 0)),
        ],
    )
    copies_z = exchange(0, z_moves(zsend, zrecv), 8)
    copies_b = exchange(
        0,
        [
            (ybsend.at[1], ybrecv.at[0], (0, 1, 0)),
            (ybsend.at[0], ybrecv.at[1], (0, -1, 0)),
            (pop.at[pl.ds(18, 9), pl.ds(PITCH * 8 + 8, 8)], xbrecv.at[0], (1, 0, 0)),
            (pop.at[pl.ds(0, 9), pl.ds(PITCH + 8, 8)], xbrecv.at[1], (-1, 0, 0)),
        ],
        26,
    )

    lax.fori_loop(0, 20, matrix_step, 0)

    def sample(first_slot, last_slot, along, here, off):
        sums = []
        for c in range(5):
            total = None
            for s in range(first_slot, last_slot):
                at = 8 * (5 * s + c) - off
                term = along[at : at + 8] * plane_of[pl.ds(8 * s, 8), here]
                total = term if total is None else total + term
            sums.append(jnp.sum(total, axis=0, keepdims=True))
        return jnp.concatenate(sums + [jnp.zeros((3, CHUNK), F32)], axis=0)

    def own_step(n, _):
        here = pl.ds(pl.multiple_of(n * CHUNK, CHUNK), CHUNK)
        along = jnp.dot(amat[pl.ds(0, 320), :], wmat[:, here], preferred_element_type=F32)
        sampled[:, here] = sample(0, 8, along, here, 0)
        return 0

    lax.fori_loop(0, PARCELS // CHUNK, own_step, 0)
    dep[...] = jnp.zeros_like(dep)
    rim[...] = jnp.zeros_like(rim)
    left[...] = jnp.zeros_like(left)

    for copy in copies1:
        copy.wait_recv()

    for j in range(4):
        ext[pl.ds(480 + j, 5, stride=8), :] = crecv[j, pl.ds(0, 5), :]
    for c in range(5):
        ext[pl.ds(480 + 8 * c + 4, 4), :] = jnp.zeros((4, 128), F32)
    ext[pl.ds(520, 8), :] = zero8

    lax.fori_loop(20, 33, matrix_step, 0)

    def term_step(n, _):
        here = pl.ds(pl.multiple_of(n * CHUNK, CHUNK), CHUNK)
        along = jnp.dot(amat[pl.ds(320, 208), :], wmat[:, here], preferred_element_type=F32)
        got = sampled[:, here] + sample(8, 13, along, here, 320)
        terms_of[:, here] = factor[:, here] * (target[:, here] - got)
        return 0

    def load_step(n, _):
        here = pl.ds(pl.multiple_of(n * CHUNK, CHUNK), CHUNK)
        terms = terms_of[:, here]
        load = [
            plane_of[pl.ds(8 * s, 8), here] * terms[c : c + 1] for s in range(13) for c in range(5)
        ]
        load.append(jnp.zeros((8, CHUNK), F32))
        load_hi, load_lo = split(jnp.concatenate(load, axis=0))
        got_hi = lax.dot_general(
            load_hi, wmat[pl.ds(0, 256), here], NT, preferred_element_type=F32
        )
        got_lo = lax.dot_general(
            load_lo, wmat[pl.ds(0, 128), here], NT, preferred_element_type=F32
        )
        dep[...] += got_hi[:, :128] + got_hi[:, 128:] + got_lo
        return 0

    lax.fori_loop(0, PARCELS // CHUNK, term_step, 0)
    lax.fori_loop(0, PARCELS // CHUNK // 2, load_step, 0)

    for copy in copies_z:
        copy.wait_recv()
    rimf[pl.ds(104, 24), :] = jnp.zeros((24, 128), F32)
    for s in range(13):
        sides = []
        for side in range(2):
            if s < 8:
                t = roll(zrecv[side, side_index(0, 0)], -16 * s - side)
            elif s < 10:
                dx = (-1, 1)[s - 8]
                t = roll(zrecv[side, side_index(dx, 0)], -(112, 0)[s - 8] - side)
            elif s < 12:
                dy = (-1, 1)[s - 10]
                t = spread_row(zrecv[side, side_index(0, dy)], (7, 0)[s - 10])
                t = skew(roll(t, -side), -16)
            else:
                t = zero8
                for j in range(4):
                    got = zrecv[side, side_index((-1, 1)[j // 2], (-1, 1)[j % 2])]
                    got = roll(got, -(112, 0)[j // 2] - side)
                    t = jnp.where(sub == j, spread_row(got, (7, 0)[j % 2]), t)
            zslot[side, pl.ds(8 * s, 8), :] = t
            sides.append(t)
        both = jnp.where(lane < 8, sides[0], roll(sides[1], 8))
        rimf[pl.ds(8 * s, 8), :] = jnp.where((lane < 16) & (low_lane < 5), both, 0.0)
    fields_hi, fields_lo = split(jnp.transpose(rimf[...])[:16])
    rim_left = jnp.concatenate(
        [
            jnp.concatenate([fields_hi, fields_hi], axis=1),
            jnp.concatenate([fields_lo, fields_lo], axis=1),
        ],
        axis=0,
    )

    def layer_step(n, _):
        here = pl.ds(pl.multiple_of(n * CHUNK, CHUNK), CHUNK)
        below, above, first, last = (edges[pl.ds(k, 1), here] for k in range(4))
        ends = jnp.dot(rim_left, pmat[:, here], preferred_element_type=F32)
        ends = ends[:16] + ends[16:]
        terms = terms_of[:, here] - factor[:, here] * (below * ends[:8] + above * ends[8:])
        for d in range(3):
            mo[d, :, here] = target[pl.ds(d, 1), here] - 0.5 * terms[d : d + 1]
        t = [terms[c : c + 1] for c in range(5)]
        lean = 3.0 * t[2]
        up = [t[4] + lean, t[0], t[1]]
        down = [t[4] - lean, t[0], t[1]]
        rows = [v * below for v in t] + [v * first for v in down]
        rows += [v * above for v in t] + [v * last for v in up]
        rows += [v * below for v in up] + [None] + [v * above for v in down] + [None]
        rows += [v * w for v in t for w in (last, first)]
        for k, row in enumerate(rows):
            if row is not None:
                left[pl.ds(k, 1), here] = row
        left_hi, left_lo = split(left[:, here])
        got_hi = lax.dot_general(left_hi, pmat[:, here], NT, preferred_element_type=F32)
        got_lo = lax.dot_general(
            left_lo, pmat[pl.ds(0, 128), here], NT, preferred_element_type=F32
        )
        rim[pl.ds(0, 48), :] += got_hi[:, :128] + got_hi[:, 128:] + got_lo
        return 0

    lax.fori_loop(0, PARCELS // CHUNK, layer_step, 0)

    rimf[...] = jnp.transpose(rim[...])
    low = zero8
    high = zero8
    ring = zero8
    for s in range(13):
        v = rimf[pl.ds(8 * s, 8), :]
        mine = group == s
        low = jnp.where(mine, roll(v, 8 * s), low)
        high = jnp.where(mine, roll(v, 8 * s - 8), high)
        ring = jnp.where(mine, roll(v, 8 * s - 16), ring)
    z2send[0] = low
    z2send[1] = high
    copies2 = exchange(1, z_moves(z2send, z2recv))

    lax.fori_loop(PARCELS // CHUNK // 2, PARCELS // CHUNK, load_step, 0)

    outer = (lane == 0) | (lane == 127)
    for s in range(13):
        v = rimf[pl.ds(8 * s, 8), :]
        for c in range(5):
            here = pl.ds(8 * (5 * s + c), 8)
            dep[here, :] = jnp.where(outer, roll(v, -25 - 2 * c), dep[here, :])

    def fill(send, blocks, singles, at):
        for n, block in enumerate(blocks):
            send[pl.ds(40 * n, 40), :] = block
        for n, (x, y) in enumerate(singles):
            s, r = place_of(x, y)
            send[pl.ds(at + 8 * n, 5), :] = dep[pl.ds(40 * s + r, 5, stride=8), :]
        send[pl.ds(at + 32, 8), :] = ring

    far = {1: (7, 8), -1: (0, -1)}
    for n, sign in enumerate((-1, 1)):
        a, b = far[sign]
        fill(
            x2send.at[n],
            [dep[pl.ds(40 * place_of(x, 0)[0], 40), :] for x in (a, b)],
            [(a, -1), (a, 8), (b, -1), (b, 8)],
            80,
        )
        for c in range(5):
            y2send[n, pl.ds(8 * c, 8), :] = dep[pl.ds(8 * c + a, 8, stride=40), :]
        y2send[n, pl.ds(40, 40), :] = dep[pl.ds(40 * place_of(0, b)[0], 40), :]
        fill(y2send.at[n], [], [(-1, a), (8, a), (-1, b), (8, b)], 80)
    for j, (sx, sy) in enumerate(SIGNS):
        fill(c2send.at[j], [], [(x, y) for x in far[sx] for y in far[sy]], 0)

    copies2 += exchange(
        1,
        corner_moves(c2send, c2recv)
        + [
            (y2send.at[1], y2recv.at[0], (0, 1, 0)),
            (y2send.at[0], y2recv.at[1], (0, -1, 0)),
            (x2send.at[1], x2recv.at[0], (1, 0, 0)),
            (x2send.at[0], x2recv.at[1], (-1, 0, 0)),
        ],
        18,
    )
    for copy in copies1 + copies_z + copies_b:
        copy.wait_send()
    for copy in copies_b:
        copy.wait_recv()
    for copy in copies2:
        copy.wait_recv()

    rings = {(0, 0): ring}
    for n, sign in enumerate((-1, 1)):
        rings[sign, 0] = x2recv[n, pl.ds(112, 8), :]
        rings[0, sign] = y2recv[n, pl.ds(112, 8), :]
    for j, (sx, sy) in enumerate(SIGNS):
        rings[-sx, -sy] = c2recv[j, pl.ds(32, 8), :]
    layers = []
    for side in range(2):
        acc = None
        for (dx, dy), ring_at in rings.items():
            t = z2recv[side, side_index(dx, dy)]
            t += jnp.where(low_lane >= 5, roll(ring_at, (5, 1)[side]), 0.0)
            xs = {0: range(-1, 9), -1: (-1, 0), 1: (7, 8)}[dx]
            ys = {0: range(-1, 9), -1: (-1, 0), 1: (7, 8)}[dy]
            singles = [(x, y) for x in xs for y in ys]
            if dx == 0 and dy == 0:
                acc = t
                continue
            if dy == 0:
                for x in xs:
                    s = place_of(x, 0)[0]
                    s_from = place_of(x - 8 * dx, 0)[0]
                    acc += jnp.where(group == s, roll(t, 8 * (s - s_from)), 0.0)
                singles = [(x, y) for (x, y) in singles if y in (-1, 8)]
            if dx == 0:
                row, s, s_from = (7, 10, 11) if dy == -1 else (0, 11, 10)
                rows = roll(skew(spread_row(t, row), -8), 8 * s)
                acc += jnp.where(group == s, rows, 0.0)
                rows = jnp.where(group == 0, roll(t, -8 * s_from), 0.0)
                rows = jnp.sum(skew(rows, 8), axis=0, keepdims=True)
                acc += jnp.where(sub == 7 - row, rows, 0.0)
                singles = [(x, y) for (x, y) in singles if x in (-1, 8)]
            for x, y in singles:
                s, r = place_of(x, y)
                s_from, r_from = place_of(x - 8 * dx, y - 8 * dy)
                got = spread_row(roll(t, 8 * (s - s_from)), r_from)
                acc += jnp.where((group == s) & (sub == r), got, 0.0)
        layers.append(acc)

    for s in range(13):
        for c in range(5):
            at = 8 * (5 * s + c)
            k = 8 * s + c
            v = dep[pl.ds(at, 8), :]
            v += jnp.where(lane == 0, roll(layers[0], -k), 0.0)
            v += jnp.where(lane == 127, roll(layers[1], 127 - k), 0.0)
            src[pl.ds(at, 8), :] = v
    def take(recv, singles, at):
        for n, (x, y) in enumerate(singles):
            s, r = place_of(x, y)
            src[pl.ds(40 * s + r, 5, stride=8), :] += recv[pl.ds(at + 8 * n, 5), :]

    near = {-1: (-1, 0), 1: (8, 7)}
    for n, sign in enumerate((-1, 1)):
        a, b = near[sign]
        for m, x in enumerate((a, b)):
            src[pl.ds(40 * place_of(x, 0)[0], 40), :] += x2recv[n, pl.ds(40 * m, 40), :]
        take(x2recv.at[n], [(a, -1), (a, 8), (b, -1), (b, 8)], 80)
        src[pl.ds(40 * place_of(0, a)[0], 40), :] += y2recv[n, pl.ds(0, 40), :]
        for c in range(5):
            src[pl.ds(8 * c + b, 8, stride=40), :] += y2recv[n, pl.ds(40 + 8 * c, 8), :]
        take(y2recv.at[n], [(-1, a), (8, a), (-1, b), (8, b)], 80)
    for j, (sx, sy) in enumerate(SIGNS):
        take(c2recv.at[j], [(x, y) for x in near[-sx] for y in near[-sy]], 0)

    def push_step(x, _):
        at = pl.multiple_of(x * 40, 8)
        to_row = pl.multiple_of(PITCH * (x + 1) + 8, 8)
        s = [src[pl.ds(at + 8 * c, 8), :] for c in range(5)]
        to[x] = gt[x] + s[3]
        vo[x] = gv[x] + s[4]
        for q in range(27):
            pop[q, pl.ds(to_row, 8), :] += push_of(q, s)
        return 0

    lax.fori_loop(0, 8, push_step, 0)
    s8, s9, s10, s11, s12 = (
        [src[pl.ds(8 * (5 * s + c), 8), :] for c in range(5)] for s in range(8, 13)
    )
    for k in range(9):
        pop[18 + k, pl.ds(8, 8), :] = xbrecv[0, k] + push_of(18 + k, s8)
        pop[k, pl.ds(PITCH * 9 + 8, 8), :] = xbrecv[1, k] + push_of(k, s9)
        q = Y_UP[k]
        pop[q, pl.ds(PITCH + 7, 8, stride=PITCH), :] = (
            ybrecv[0, pl.ds(8 * k, 8), :] + push_of(q, s10)
        )
        q = Y_DOWN[k]
        pop[q, pl.ds(PITCH + 16, 8, stride=PITCH), :] = (
            ybrecv[1, pl.ds(8 * k, 8), :] + push_of(q, s11)
        )
    for j, (sx, sy) in enumerate(SIGNS):
        row = PITCH * (0, 9)[j // 2] + (7, 16)[j % 2]
        for k in range(3):
            q = 9 * (sx + 1) + 3 * (sy + 1) + k
            total = crecv[j, pl.ds(5 + k, 1), :] + push_of(q, s12)[j : j + 1]
            pop[q, pl.ds(row, 1), :] = total

    number = lane - 5
    used = (number >= 0) & (number < 9)
    step_x = jnp.where(number < 3, -1.0, jnp.where(number < 6, 0.0, 1.0))
    third = jnp.where(number < 3, number, jnp.where(number < 6, number - 3, number - 6))
    step_y = jnp.where(third == 0, -1.0, jnp.where(third == 1, 0.0, 1.0))
    share = jnp.where(step_x == 0.0, 2.0 / 3.0, 1.0 / 6.0)
    share = share * jnp.where(step_y == 0.0, 2.0 / 3.0, 1.0 / 6.0)
    share = jnp.where(used, share * (1.0 / 6.0), 0.0)
    share_x = 3.0 * share * step_x
    share_y = 3.0 * share * step_y
    for side in range(2):
        for s in range(13):
            three = [
                jnp.broadcast_to(layers[side][:, 8 * s + v : 8 * s + v + 1], (8, 128))
                for v in (5, 6, 7)
            ]
            t = zslot[side, pl.ds(8 * s, 8), :]
            t = t + share * three[0] + share_x * three[1] + share_y * three[2]
            if s < 8:
                zcol[side, pl.ds(PITCH * (s + 1) + 8, 8), :] = t
            elif s < 10:
                zcol[side, pl.ds(PITCH * (0, 9)[s - 8] + 8, 8), :] = t
            elif s < 12:
                zcol[side, pl.ds(PITCH + (7, 16)[s - 10], 8, stride=PITCH), :] = t
            else:
                for j in range(4):
                    row = PITCH * (0, 9)[j // 2] + (7, 16)[j % 2]
                    zcol[side, pl.ds(row, 1), :] = t[j : j + 1]

    written = write([(to, to_out), (vo, vo_out), (mo, mo_out)], 0)
    for part in range(9):
        for q in range(3 * part, 3 * part + 3):
            ex, ey, ez = step_of(q)
            m = q // 3 + 5
            for x in range(8):
                row = PITCH * (x - ex + 1) + 8 - ey
                v = pop[q, pl.ds(row, 8), :]
                if ez == 1:
                    v = jnp.where(lane == 0, roll(zcol[0, pl.ds(row, 8), :], -m), roll(v, 1))
                elif ez == -1:
                    v = jnp.where(
                        lane == 127, roll(zcol[1, pl.ds(row, 8), :], 127 - m), roll(v, -1)
                    )
                staged[q, x] = v
        here = pl.ds(3 * part, 3)
        written += write([(staged.at[here], fo.at[here])], 3 + part)

    for copy in copies2:
        copy.wait_send()
    for copy in written:
        copy.wait()


def keep_kernel(a0, a1, a2, a3, b0, b1, b2, b3, t0, t1, t2, t3, sem):
    trips = []
    for part in range(3):
        here = pl.ds(9 * part, 9)
        trips.append((a0.at[here], t0.at[here], b0.at[here]))
    trips += [(a1, t1, b1), (a2, t2, b2), (a3, t3, b3)]
    copies = []
    for n, (a, t, _) in enumerate(trips):
        copy = pltpu.make_async_copy(a, t, sem.at[0, n])
        copy.start()
        copies.append(copy)
    outs = []
    for n, (_, t, b) in enumerate(trips):
        copies[n].wait()
        copy = pltpu.make_async_copy(t, b, sem.at[1, n])
        copy.start()
        outs.append(copy)
    for copy in outs:
        copy.wait()


def on_device(f, gt, gv, base, frac, vel, temp, rate, live):
    anywhere = pl.BlockSpec(memory_space=pl.ANY)

    def buffer(*shape, dtype=F32):
        return pltpu.VMEM(shape, dtype)

    results = (
        jax.ShapeDtypeStruct(f.shape, F32),
        jax.ShapeDtypeStruct(gt.shape, F32),
        jax.ShapeDtypeStruct(gv.shape, F32),
        jax.ShapeDtypeStruct((3, 1, PARCELS), F32),
    )
    inner = pl.pallas_call(
        gather_kernel,
        out_shape=results,
        in_specs=[anywhere] * 8 + [pl.BlockSpec(memory_space=pltpu.SMEM)],
        out_specs=[anywhere] * 4,
        scratch_shapes=[
            buffer(27, 10 * PITCH, 128),
            buffer(2, 10 * PITCH, 128),
            buffer(8, 8, 128),
            buffer(8, 8, 128),
            buffer(3, 1, PARCELS),
            buffer(27, 8, 8, 128),
            buffer(27, 8, 8, 128),
            buffer(8, 8, 128),
            buffer(8, 8, 128),
            buffer(3, 1, PARCELS, dtype=jnp.int32),
            buffer(3, 1, PARCELS),
            buffer(3, 1, PARCELS),
            buffer(1, PARCELS),
            buffer(1, PARCELS),
            buffer(528, 128),
            buffer(2, 40, 128),
            buffer(4, 8, 128),
            buffer(4, 8, 128),
            buffer(2, 8, 128),
            buffer(2, 9, 8, 128),
            buffer(2, 72, 128),
            buffer(2, 72, 128),
            buffer(2, 9, 8, 128),
            buffer(528, 384, dtype=BF16),
            buffer(384, PARCELS, dtype=BF16),
            buffer(256, PARCELS, dtype=BF16),
            buffer(128, PARCELS),
            buffer(8, PARCELS),
            buffer(8, PARCELS),
            buffer(8, PARCELS),
            buffer(8, PARCELS),
            buffer(8, PARCELS),
            buffer(48, PARCELS),
            buffer(528, 128),
            buffer(128, 128),
            buffer(2, 104, 128),
            buffer(128, 128),
            buffer(2, 120, 128),
            buffer(2, 120, 128),
            buffer(2, 120, 128),
            buffer(2, 120, 128),
            buffer(4, 40, 128),
            buffer(4, 40, 128),
            buffer(2, 8, 128),
            buffer(2, 9, 8, 128),
            buffer(528, 128),
            pltpu.SemaphoreType.DMA((8,)),
            pltpu.SemaphoreType.DMA((12,)),
            pltpu.SemaphoreType.DMA((2, 30)),
            pltpu.SemaphoreType.DMA((2, 30)),
        ],
        compiler_params=pltpu.CompilerParams(
            collective_id=0, has_side_effects=True, vmem_limit_bytes=56 * 1024 * 1024
        ),
    )(
        f,
        gt,
        gv,
        base.reshape(3, 1, PARCELS),
        frac.reshape(3, 1, PARCELS),
        vel.reshape(3, 1, PARCELS),
        temp.reshape(1, PARCELS),
        rate.reshape(1, PARCELS),
        live.reshape(1),
    )
    fo, to, vo, mo = pl.pallas_call(
        keep_kernel,
        out_shape=results,
        in_specs=[anywhere] * 4,
        out_specs=[anywhere] * 4,
        scratch_shapes=[
            buffer(*f.shape),
            buffer(*gt.shape),
            buffer(*gv.shape),
            buffer(3, 1, PARCELS),
            pltpu.SemaphoreType.DMA((2, 6)),
        ],
        compiler_params=pltpu.CompilerParams(vmem_limit_bytes=56 * 1024 * 1024),
    )(*inner)
    return fo, to, vo, mo.reshape(vel.shape)


def solution(mesh):
    placed = (
        P(None, "gx", "gy", "gz"),
        P("gx", "gy", "gz"),
        P("gx", "gy", "gz"),
        P(None, "gx", "gy", "gz", None),
        P(None, "gx", "gy", "gz", None),
        P(None, "gx", "gy", "gz", None),
        P("gx", "gy", "gz", None),
        P("gx", "gy", "gz", None),
        P("gx", "gy", "gz"),
    )
    return jax.shard_map(
        on_device,
        mesh=mesh,
        in_specs=placed,
        out_specs=(
            P(None, "gx", "gy", "gz"),
            P("gx", "gy", "gz"),
            P("gx", "gy", "gz"),
            P(None, "gx", "gy", "gz", None),
        ),
        check_vma=False,
    )
```

```python
import jax
import jax.numpy as jnp
from jax import lax
from jax.experimental import pallas as pl
from jax.experimental.pallas import tpu as pltpu
from jax.sharding import PartitionSpec as P

AXES = ("gx", "gy", "gz")
CHUNK = 2048
LOAD = 1024
PARCELS = 2048
PITCH = 24
F32 = jnp.float32
BF16 = jnp.bfloat16
MESH = pl.DeviceIdType.MESH
NT = (((1,), (1,)), ((), ()))


def step_of(q):
    return q // 9 - 1, q // 3 % 3 - 1, q % 3 - 1


def weight_of(q):
    value = 1.0
    for step in step_of(q):
        value = value * (2.0 / 3.0 if step == 0 else 1.0 / 6.0)
    return value


def roll(v, k):
    k = k % 128
    return pltpu.roll(v, k, 1) if k else v


def split(v):
    hi = v.astype(BF16)
    lo = (v - hi.astype(F32)).astype(BF16)
    return hi, lo


def side_index(dx, dy):
    return 3 * (dx + 1) + dy + 1


def place_of(x, y):
    if 0 <= x < 8:
        return (x, y) if 0 <= y < 8 else (10 if y < 0 else 11, x)
    if 0 <= y < 8:
        return 8 if x < 0 else 9, y
    return 12, 2 * (x > 0) + (y > 0)


SIGNS = [(1, 1), (1, -1), (-1, 1), (-1, -1)]
Y_UP = [9 * a + 6 + b for a in range(3) for b in range(3)]
Y_DOWN = [9 * a + b for a in range(3) for b in range(3)]


def push_of(q, s):
    push = s[4]
    e = step_of(q)
    for axis in range(3):
        if e[axis] == 1:
            push = push + 3.0 * s[axis]
        elif e[axis] == -1:
            push = push - 3.0 * s[axis]
    return weight_of(q) * push


def gather_kernel(
    f_in, gt_in, gv_in, base_in, frac_in, vel_in, temp_in, rate_in, live,
    fo, to_out, vo_out, mo_out,
    pop, zcol, to, vo, mo, staged,
    f, gt, gv, base, frac, vel, temp, rate,
    ext, ysend, csend, crecv, zsend, zrecv, ybsend, ybrecv, xbrecv,
    amat, wmat, pmat, plane_of, target, factor, sampled, edges, terms_of, left,
    dep, rim, zslot, rimf,
    x2send, x2recv, y2send, y2recv, c2send, c2recv, z2send, z2recv, zsum, src,
    in_sem, out_sem, send_sem, recv_sem,
):
    me = [lax.axis_index(a) for a in AXES]
    size = [lax.axis_size(a) for a in AXES]

    def device(d):
        return tuple(
            me[i] if d[i] == 0 else lax.rem(me[i] + (d[i] + size[i]), size[i]) for i in range(3)
        )

    around = [
        (dx, dy, dz)
        for dz in (-1, 1, 0)
        for dx in (-1, 1, 0)
        for dy in (-1, 1, 0)
        if (dx, dy, dz) != (0, 0, 0)
    ]
    around.sort(key=lambda d: -sum(map(abs, d)))
    barrier = pltpu.get_barrier_semaphore()
    for d in around:
        pl.semaphore_signal(barrier, inc=1, device_id=device(d), device_id_type=MESH)

    fetches = []
    for n, (a, b) in enumerate(
        [
            (f_in, f), (gt_in, gt), (gv_in, gv), (base_in, base), (frac_in, frac),
            (vel_in, vel), (temp_in, temp), (rate_in, rate),
        ]
    ):
        fetch = pltpu.make_async_copy(a, b, in_sem.at[n])
        fetch.start()
        fetches.append(fetch)

    def write(pairs, at):
        copies = []
        for n, (a, b) in enumerate(pairs):
            copy = pltpu.make_async_copy(a, b, out_sem.at[at + n])
            copy.start()
            copies.append(copy)
        return copies

    def exchange(phase, moves, at=0):
        copies = []
        for n, (a, b, d) in enumerate(moves, start=at):
            copy = pltpu.make_async_remote_copy(
                src_ref=a,
                dst_ref=b,
                send_sem=send_sem.at[phase, n],
                recv_sem=recv_sem.at[phase, n],
                device_id=device(d),
                device_id_type=MESH,
            )
            copy.start()
            copies.append(copy)
        return copies

    lane = lax.broadcasted_iota(jnp.int32, (8, 128), 1)
    sub = lax.broadcasted_iota(jnp.int32, (8, 128), 0)
    low_lane = lane & 7
    group = lane >> 3

    def skew(v, amount):
        for bit in range(3):
            v = jnp.where((sub >> bit) & 1 == 1, roll(v, amount << bit), v)
        return v

    def spread_row(v, row):
        return jnp.broadcast_to(v[row : row + 1], (8, 128))

    for fetch in fetches[:3]:
        fetch.wait()

    def moment_step(x, _):
        at = pl.multiple_of(x * 40, 8)
        to_row = pl.multiple_of(PITCH * (x + 1) + 8, 8)
        pops = [f[q, x] for q in range(27)]
        total = pops[0]
        for q in range(1, 27):
            total = total + pops[q]
        u = []
        for axis in range(3):
            up = None
            for q in range(27):
                e = step_of(q)[axis]
                if e == 1:
                    up = pops[q] if up is None else up + pops[q]
                elif e == -1:
                    up = -pops[q] if up is None else up - pops[q]
            u.append(up / total)
            ext[pl.ds(at + 8 * axis, 8), :] = u[axis]
        ext[pl.ds(at + 24, 8), :] = gt[x]
        ext[pl.ds(at + 32, 8), :] = gv[x]
        rest = 1.0 - 1.5 * (u[0] * u[0] + u[1] * u[1] + u[2] * u[2])
        for q in range(27):
            e = step_of(q)
            along = None
            for axis in range(3):
                if e[axis] != 0:
                    term = u[axis] if e[axis] == 1 else -u[axis]
                    along = term if along is None else along + term
            inner = rest if along is None else rest + along * (3.0 + 4.5 * along)
            equil = (1.25 * weight_of(q)) * total * inner
            pop[q, pl.ds(to_row, 8), :] = equil - 0.25 * pops[q]
        return 0

    lax.fori_loop(0, 8, moment_step, 0)

    for c in range(5):
        for side in range(2):
            ysend[side, pl.ds(8 * c, 8), :] = ext[pl.ds(8 * c + 7 * side, 8, stride=40), :]
    for k in range(9):
        ybsend[0, pl.ds(8 * k, 8), :] = pop[Y_DOWN[k], pl.ds(PITCH + 8, 8, stride=PITCH), :]
        ybsend[1, pl.ds(8 * k, 8), :] = pop[Y_UP[k], pl.ds(PITCH + 15, 8, stride=PITCH), :]
    for j, (sx, sy) in enumerate(SIGNS):
        x, y = 7 if sx == 1 else 0, 7 if sy == 1 else 0
        csend[j, pl.ds(0, 5), :] = ext[pl.ds(40 * x + y, 5, stride=8), :]
        for k in range(3):
            q = 9 * (sx + 1) + 3 * (sy + 1) + k
            csend[j, pl.ds(5 + k, 1), :] = pop[q, pl.ds(PITCH * (x + 1) + 8 + y, 1), :]

    def z_pack(x, carry):
        low, high = carry
        at = pl.multiple_of(x * 40, 8)
        row = pl.multiple_of(PITCH * (x + 1) + 8, 8)
        near_low = jnp.zeros((8, 128), F32)
        near_high = jnp.zeros((8, 128), F32)
        for v in range(14):
            if v < 5:
                t_low = t_high = roll(ext[pl.ds(at + 8 * v, 8), :], v + 1)
            else:
                t_low = roll(pop[3 * (v - 5), pl.ds(row, 8), :], v + 1)
                t_high = roll(pop[3 * (v - 5) + 2, pl.ds(row, 8), :], v + 1)
            near_low = jnp.where(lane == v + 1, t_low, near_low)
            near_high = jnp.where(lane == v, t_high, near_high)
        return (
            low + pltpu.roll(near_low, 16 * x, 1),
            high + pltpu.roll(near_high, 16 * x, 1),
        )

    zero8 = jnp.zeros((8, 128), F32)
    low, high = lax.fori_loop(0, 8, z_pack, (zero8, zero8))
    zsend[0] = low
    zsend[1] = high

    for fetch in fetches[3:]:
        fetch.wait()
    alive = live[0]

    def weight_step(n, _):
        first = pl.multiple_of(n * CHUNK, CHUNK)
        here = pl.ds(first, CHUNK)
        bx, by, bz = (base[d, :, here] for d in range(3))
        fx, fy, fz = (frac[d, :, here] for d in range(3))
        rows8 = lax.broadcasted_iota(jnp.int32, (8, CHUNK), 0)

        def hat(cells, b, fr):
            return jnp.where(cells == b, 1.0 - fr, jnp.where(cells == b + 1, fr, 0.0))

        wz_hi, wz_lo = split(hat(lax.broadcasted_iota(jnp.int32, (128, CHUNK), 0), bz, fz))
        wmat[pl.ds(0, 128), here] = wz_hi
        wmat[pl.ds(128, 128), here] = wz_lo
        wmat[pl.ds(256, 128), here] = wz_hi
        edges[pl.ds(0, 1), here] = jnp.where(bz == -1, 1.0 - fz, 0.0)
        edges[pl.ds(1, 1), here] = jnp.where(bz == 127, fz, 0.0)
        edges[pl.ds(2, 1), here] = hat(0, bz, fz)
        edges[pl.ds(3, 1), here] = hat(127, bz, fz)

        wx8 = hat(rows8, bx, fx)
        wy8 = hat(rows8, by, fy)
        x_low = jnp.where(bx == -1, 1.0 - fx, 0.0)
        x_high = jnp.where(bx == 7, fx, 0.0)
        y_low = jnp.where(by == -1, 1.0 - fy, 0.0)
        y_high = jnp.where(by == 7, fy, 0.0)
        plane = [wx8[x : x + 1] * wy8 for x in range(8)]
        plane += [x_low * wy8, x_high * wy8, y_low * wx8, y_high * wx8]
        edge = jnp.where(rows8 < 2, x_low, x_high) * jnp.where((rows8 & 1) == 0, y_low, y_high)
        plane.append(jnp.where(rows8 < 4, edge, 0.0))
        plane = jnp.concatenate(plane + [jnp.zeros((24, CHUNK), F32)], axis=0)
        plane_of[:, here] = plane
        plane_hi, plane_lo = split(plane)
        pmat[pl.ds(0, 128), here] = plane_hi
        pmat[pl.ds(128, 128), here] = plane_lo

        slot = lax.broadcasted_iota(jnp.int32, (1, CHUNK), 1) + first
        own_temp = temp[:, here]
        target[:, here] = jnp.concatenate(
            [vel[d, :, here] for d in range(3)]
            + [own_temp, 0.05 * jnp.exp(3.0 * (own_temp - 0.5)), jnp.zeros((3, CHUNK), F32)],
            axis=0,
        )
        scale = jnp.where(rows8 < 3, 2.0, jnp.where(rows8 < 5, 1.0, 0.0))
        factor[:, here] = jnp.where(slot < alive, rate[:, here], 0.0) * scale
        return 0


    def matrix_step(n, _):
        at = pl.multiple_of(n * 16, 16)
        hi, lo = split(ext[pl.ds(at, 16), :])
        amat[pl.ds(at, 16), pl.ds(0, 128)] = hi
        amat[pl.ds(at, 16), pl.ds(128, 128)] = hi
        amat[pl.ds(at, 16), pl.ds(256, 128)] = lo
        return 0

    pl.semaphore_wait(barrier, 26)

    def z_moves(send, recv):
        return [
            (
                send.at[(1 + dz) // 2],
                recv.at[(1 - dz) // 2, side_index(-dx, -dy)],
                (dx, dy, dz),
            )
            for (dx, dy, dz) in around
            if dz != 0
        ]

    def corner_moves(send, recv):
        return [(send.at[j], recv.at[j], (sx, sy, 0)) for j, (sx, sy) in enumerate(SIGNS)]

    copies1 = exchange(
        0,
        corner_moves(csend, crecv)
        + [
            (ysend.at[1], ext.at[pl.ds(400, 40)], (0, 1, 0)),
            (ysend.at[0], ext.at[pl.ds(440, 40)], (0, -1, 0)),
            (ext.at[pl.ds(280, 40)], ext.at[pl.ds(320, 40)], (1, 0, 0)),
            (ext.at[pl.ds(0, 40)], ext.at[pl.ds(360, 40)], (-1, 0, 0)),
        ],
    )
    copies_z = exchange(0, z_moves(zsend, zrecv), 8)
    copies_b = exchange(
        0,
        [
            (ybsend.at[1], ybrecv.at[0], (0, 1, 0)),
            (ybsend.at[0], ybrecv.at[1], (0, -1, 0)),
            (pop.at[pl.ds(18, 9), pl.ds(PITCH * 8 + 8, 8)], xbrecv.at[0], (1, 0, 0)),
            (pop.at[pl.ds(0, 9), pl.ds(PITCH + 8, 8)], xbrecv.at[1], (-1, 0, 0)),
        ],
        26,
    )

    lax.fori_loop(0, PARCELS // CHUNK, weight_step, 0)
    lax.fori_loop(0, 20, matrix_step, 0)

    def sample(first_slot, last_slot, along, here, off):
        sums = []
        for c in range(5):
            total = None
            for s in range(first_slot, last_slot):
                at = 8 * (5 * s + c) - off
                term = along[at : at + 8] * plane_of[pl.ds(8 * s, 8), here]
                total = term if total is None else total + term
            sums.append(jnp.sum(total, axis=0, keepdims=True))
        return jnp.concatenate(sums + [jnp.zeros((3, CHUNK), F32)], axis=0)

    def own_step(n, _):
        here = pl.ds(pl.multiple_of(n * CHUNK, CHUNK), CHUNK)
        along = jnp.dot(amat[pl.ds(0, 320), :], wmat[:, here], preferred_element_type=F32)
        sampled[:, here] = sample(0, 8, along, here, 0)
        return 0

    lax.fori_loop(0, PARCELS // CHUNK, own_step, 0)
    dep[...] = jnp.zeros_like(dep)
    rim[...] = jnp.zeros_like(rim)
    left[...] = jnp.zeros_like(left)

    for copy in copies1:
        copy.wait_recv()

    for j in range(4):
        ext[pl.ds(480 + j, 5, stride=8), :] = crecv[j, pl.ds(0, 5), :]
    for c in range(5):
        ext[pl.ds(480 + 8 * c + 4, 4), :] = jnp.zeros((4, 128), F32)
    ext[pl.ds(520, 8), :] = zero8

    lax.fori_loop(20, 33, matrix_step, 0)

    def term_step(n, _):
        here = pl.ds(pl.multiple_of(n * CHUNK, CHUNK), CHUNK)
        along = jnp.dot(amat[pl.ds(320, 208), :], wmat[:, here], preferred_element_type=F32)
        got = sampled[:, here] + sample(8, 13, along, here, 320)
        terms_of[:, here] = factor[:, here] * (target[:, here] - got)
        return 0

    def load_step(n, _):
        here = pl.ds(pl.multiple_of(n * LOAD, LOAD), LOAD)
        terms = terms_of[:, here]
        load = [
            plane_of[pl.ds(8 * s, 8), here] * terms[c : c + 1] for s in range(13) for c in range(5)
        ]
        load.append(jnp.zeros((8, LOAD), F32))
        load_hi, load_lo = split(jnp.concatenate(load, axis=0))
        got_hi = lax.dot_general(
            load_hi, wmat[pl.ds(0, 256), here], NT, preferred_element_type=F32
        )
        got_lo = lax.dot_general(
            load_lo, wmat[pl.ds(0, 128), here], NT, preferred_element_type=F32
        )
        dep[...] += got_hi[:, :128] + got_hi[:, 128:] + got_lo
        return 0

    lax.fori_loop(0, PARCELS // CHUNK, term_step, 0)
    lax.fori_loop(0, PARCELS // LOAD // 2, load_step, 0)

    for copy in copies_z:
        copy.wait_recv()
    rimf[pl.ds(104, 24), :] = jnp.zeros((24, 128), F32)
    for s in range(13):
        sides = []
        for side in range(2):
            if s < 8:
                t = roll(zrecv[side, side_index(0, 0)], -16 * s - side)
            elif s < 10:
                dx = (-1, 1)[s - 8]
                t = roll(zrecv[side, side_index(dx, 0)], -(112, 0)[s - 8] - side)
            elif s < 12:
                dy = (-1, 1)[s - 10]
                t = spread_row(zrecv[side, side_index(0, dy)], (7, 0)[s - 10])
                t = skew(roll(t, -side), -16)
            else:
                t = zero8
                for j in range(4):
                    got = zrecv[side, side_index((-1, 1)[j // 2], (-1, 1)[j % 2])]
                    got = roll(got, -(112, 0)[j // 2] - side)
                    t = jnp.where(sub == j, spread_row(got, (7, 0)[j % 2]), t)
            zslot[side, pl.ds(8 * s, 8), :] = t
            sides.append(t)
        both = jnp.where(lane < 8, sides[0], roll(sides[1], 8))
        rimf[pl.ds(8 * s, 8), :] = jnp.where((lane < 16) & (low_lane < 5), both, 0.0)
    fields_hi, fields_lo = split(jnp.transpose(rimf[...])[:16])
    rim_left = jnp.concatenate(
        [
            jnp.concatenate([fields_hi, fields_hi], axis=1),
            jnp.concatenate([fields_lo, fields_lo], axis=1),
        ],
        axis=0,
    )

    def layer_step(n, _):
        here = pl.ds(pl.multiple_of(n * CHUNK, CHUNK), CHUNK)
        below, above, first, last = (edges[pl.ds(k, 1), here] for k in range(4))
        ends = jnp.dot(rim_left, pmat[:, here], preferred_element_type=F32)
        ends = ends[:16] + ends[16:]
        terms = terms_of[:, here] - factor[:, here] * (below * ends[:8] + above * ends[8:])
        for d in range(3):
            mo[d, :, here] = target[pl.ds(d, 1), here] - 0.5 * terms[d : d + 1]
        left_hi, left_lo = split(
            jnp.concatenate([terms * w for w in (below, above, first, last)], axis=0)
        )
        got_hi = lax.dot_general(left_hi, pmat[:, here], NT, preferred_element_type=F32)
        got_lo = lax.dot_general(
            left_lo, pmat[pl.ds(0, 128), here], NT, preferred_element_type=F32
        )
        rim[pl.ds(0, 32), :] += got_hi[:, :128] + got_hi[:, 128:] + got_lo
        return 0

    lax.fori_loop(0, PARCELS // CHUNK, layer_step, 0)

    layer = [[rim[pl.ds(8 * k + c, 1), :] for c in range(5)] for k in range(4)]
    up = [[t[4] + 3.0 * t[2], t[0], t[1]] for t in layer]
    down = [[t[4] - 3.0 * t[2], t[0], t[1]] for t in layer]
    rows = layer[0] + down[2] + layer[1] + up[3] + up[0] + [None] + down[1] + [None]
    rows += [t for c in range(5) for t in (layer[3][c], layer[2][c])]
    for k, row in enumerate(rows):
        if row is not None:
            left[pl.ds(k, 1), :] = row
    rimf[...] = jnp.transpose(left[...])
    low = zero8
    high = zero8
    ring = zero8
    for s in range(13):
        v = rimf[pl.ds(8 * s, 8), :]
        mine = group == s
        low = jnp.where(mine, roll(v, 8 * s), low)
        high = jnp.where(mine, roll(v, 8 * s - 8), high)
        ring = jnp.where(mine, roll(v, 8 * s - 16), ring)
    z2send[0] = low
    z2send[1] = high
    copies2 = exchange(1, z_moves(z2send, z2recv))

    lax.fori_loop(PARCELS // LOAD // 2, PARCELS // LOAD, load_step, 0)

    outer = (lane == 0) | (lane == 127)
    for s in range(13):
        v = rimf[pl.ds(8 * s, 8), :]
        for c in range(5):
            here = pl.ds(8 * (5 * s + c), 8)
            dep[here, :] = jnp.where(outer, roll(v, -25 - 2 * c), dep[here, :])

    def fill(send, blocks, singles, at):
        for n, block in enumerate(blocks):
            send[pl.ds(40 * n, 40), :] = block
        for n, (x, y) in enumerate(singles):
            s, r = place_of(x, y)
            send[pl.ds(at + 8 * n, 5), :] = dep[pl.ds(40 * s + r, 5, stride=8), :]
        send[pl.ds(at + 32, 8), :] = ring

    far = {1: (7, 8), -1: (0, -1)}
    for n, sign in enumerate((-1, 1)):
        a, b = far[sign]
        fill(
            x2send.at[n],
            [dep[pl.ds(40 * place_of(x, 0)[0], 40), :] for x in (a, b)],
            [(a, -1), (a, 8), (b, -1), (b, 8)],
            80,
        )
        for c in range(5):
            y2send[n, pl.ds(8 * c, 8), :] = dep[pl.ds(8 * c + a, 8, stride=40), :]
        y2send[n, pl.ds(40, 40), :] = dep[pl.ds(40 * place_of(0, b)[0], 40), :]
        fill(y2send.at[n], [], [(-1, a), (8, a), (-1, b), (8, b)], 80)
    for j, (sx, sy) in enumerate(SIGNS):
        fill(c2send.at[j], [], [(x, y) for x in far[sx] for y in far[sy]], 0)

    copies2 += exchange(
        1,
        corner_moves(c2send, c2recv)
        + [
            (y2send.at[1], y2recv.at[0], (0, 1, 0)),
            (y2send.at[0], y2recv.at[1], (0, -1, 0)),
            (x2send.at[1], x2recv.at[0], (1, 0, 0)),
            (x2send.at[0], x2recv.at[1], (-1, 0, 0)),
        ],
        18,
    )
    for copy in copies1 + copies_z + copies_b:
        copy.wait_send()
    for copy in copies_b:
        copy.wait_recv()
    for copy in copies2:
        copy.wait_recv()

    rings = {(0, 0): ring}
    for n, sign in enumerate((-1, 1)):
        rings[sign, 0] = x2recv[n, pl.ds(112, 8), :]
        rings[0, sign] = y2recv[n, pl.ds(112, 8), :]
    for j, (sx, sy) in enumerate(SIGNS):
        rings[-sx, -sy] = c2recv[j, pl.ds(32, 8), :]
    for (dx, dy), ring_at in rings.items():
        n = side_index(dx, dy)
        for side in range(2):
            zsum[side, n] = z2recv[side, n] + jnp.where(
                low_lane >= 5, roll(ring_at, (5, 1)[side]), 0.0
            )
    layers = []
    for side in range(2):
        acc = zsum[side, side_index(0, 0)]
        by_shift = {}

        def move(shift, mask, v):
            v = jnp.where(mask, v, 0.0)
            by_shift[shift] = by_shift[shift] + v if shift in by_shift else v

        for dx, dy in rings:
            if dx == 0 and dy == 0:
                continue
            n = side_index(dx, dy)
            xs = {0: range(-1, 9), -1: (-1, 0), 1: (7, 8)}[dx]
            ys = {0: range(-1, 9), -1: (-1, 0), 1: (7, 8)}[dy]
            singles = [(x, y) for x in xs for y in ys]
            if dy == 0:
                for x in xs:
                    s = place_of(x, 0)[0]
                    s_from = place_of(x - 8 * dx, 0)[0]
                    move(s - s_from, group == s_from, zsum[side, n])
                singles = [(x, y) for (x, y) in singles if y in (-1, 8)]
            if dx == 0:
                row, s, s_from = (7, 10, 11) if dy == -1 else (0, 11, 10)
                line = jnp.broadcast_to(zsum[side, n, pl.ds(row, 1), :], (8, 128))
                move(s, group == 0, skew(line, -8))
                rows = jnp.where(group == 0, roll(zsum[side, n], -8 * s_from), 0.0)
                rows = jnp.sum(skew(rows, 8), axis=0, keepdims=True)
                acc += jnp.where(sub == 7 - row, rows, 0.0)
                singles = [(x, y) for (x, y) in singles if x in (-1, 8)]
            for x, y in singles:
                s, r = place_of(x, y)
                s_from, r_from = place_of(x - 8 * dx, y - 8 * dy)
                line = jnp.broadcast_to(zsum[side, n, pl.ds(r_from, 1), :], (8, 128))
                move(s - s_from, (group == s_from) & (sub == r), line)
        for shift, v in by_shift.items():
            acc += roll(v, 8 * shift)
        layers.append(acc)

    for s in range(13):
        for c in range(5):
            at = 8 * (5 * s + c)
            k = 8 * s + c
            v = dep[pl.ds(at, 8), :]
            v += jnp.where(lane == 0, roll(layers[0], -k), 0.0)
            v += jnp.where(lane == 127, roll(layers[1], 127 - k), 0.0)
            src[pl.ds(at, 8), :] = v
    def take(recv, singles, at):
        for n, (x, y) in enumerate(singles):
            s, r = place_of(x, y)
            src[pl.ds(40 * s + r, 5, stride=8), :] += recv[pl.ds(at + 8 * n, 5), :]

    near = {-1: (-1, 0), 1: (8, 7)}
    for n, sign in enumerate((-1, 1)):
        a, b = near[sign]
        for m, x in enumerate((a, b)):
            src[pl.ds(40 * place_of(x, 0)[0], 40), :] += x2recv[n, pl.ds(40 * m, 40), :]
        take(x2recv.at[n], [(a, -1), (a, 8), (b, -1), (b, 8)], 80)
        src[pl.ds(40 * place_of(0, a)[0], 40), :] += y2recv[n, pl.ds(0, 40), :]
        for c in range(5):
            src[pl.ds(8 * c + b, 8, stride=40), :] += y2recv[n, pl.ds(40 + 8 * c, 8), :]
        take(y2recv.at[n], [(-1, a), (8, a), (-1, b), (8, b)], 80)
    for j, (sx, sy) in enumerate(SIGNS):
        take(c2recv.at[j], [(x, y) for x in near[-sx] for y in near[-sy]], 0)

    def push_step(x, _):
        at = pl.multiple_of(x * 40, 8)
        to_row = pl.multiple_of(PITCH * (x + 1) + 8, 8)
        s = [src[pl.ds(at + 8 * c, 8), :] for c in range(5)]
        to[x] = gt[x] + s[3]
        vo[x] = gv[x] + s[4]
        for q in range(27):
            pop[q, pl.ds(to_row, 8), :] += push_of(q, s)
        return 0

    lax.fori_loop(0, 8, push_step, 0)
    s8, s9, s10, s11, s12 = (
        [src[pl.ds(8 * (5 * s + c), 8), :] for c in range(5)] for s in range(8, 13)
    )
    for k in range(9):
        pop[18 + k, pl.ds(8, 8), :] = xbrecv[0, k] + push_of(18 + k, s8)
        pop[k, pl.ds(PITCH * 9 + 8, 8), :] = xbrecv[1, k] + push_of(k, s9)
        q = Y_UP[k]
        pop[q, pl.ds(PITCH + 7, 8, stride=PITCH), :] = (
            ybrecv[0, pl.ds(8 * k, 8), :] + push_of(q, s10)
        )
        q = Y_DOWN[k]
        pop[q, pl.ds(PITCH + 16, 8, stride=PITCH), :] = (
            ybrecv[1, pl.ds(8 * k, 8), :] + push_of(q, s11)
        )
    for j, (sx, sy) in enumerate(SIGNS):
        row = PITCH * (0, 9)[j // 2] + (7, 16)[j % 2]
        for k in range(3):
            q = 9 * (sx + 1) + 3 * (sy + 1) + k
            total = crecv[j, pl.ds(5 + k, 1), :] + push_of(q, s12)[j : j + 1]
            pop[q, pl.ds(row, 1), :] = total

    number = lane - 5
    used = (number >= 0) & (number < 9)
    step_x = jnp.where(number < 3, -1.0, jnp.where(number < 6, 0.0, 1.0))
    third = jnp.where(number < 3, number, jnp.where(number < 6, number - 3, number - 6))
    step_y = jnp.where(third == 0, -1.0, jnp.where(third == 1, 0.0, 1.0))
    share = jnp.where(step_x == 0.0, 2.0 / 3.0, 1.0 / 6.0)
    share = share * jnp.where(step_y == 0.0, 2.0 / 3.0, 1.0 / 6.0)
    share = jnp.where(used, share * (1.0 / 6.0), 0.0)
    share_x = 3.0 * share * step_x
    share_y = 3.0 * share * step_y
    for side in range(2):
        for s in range(13):
            three = [
                jnp.broadcast_to(layers[side][:, 8 * s + v : 8 * s + v + 1], (8, 128))
                for v in (5, 6, 7)
            ]
            t = zslot[side, pl.ds(8 * s, 8), :]
            t = t + share * three[0] + share_x * three[1] + share_y * three[2]
            if s < 8:
                zcol[side, pl.ds(PITCH * (s + 1) + 8, 8), :] = t
            elif s < 10:
                zcol[side, pl.ds(PITCH * (0, 9)[s - 8] + 8, 8), :] = t
            elif s < 12:
                zcol[side, pl.ds(PITCH + (7, 16)[s - 10], 8, stride=PITCH), :] = t
            else:
                for j in range(4):
                    row = PITCH * (0, 9)[j // 2] + (7, 16)[j % 2]
                    zcol[side, pl.ds(row, 1), :] = t[j : j + 1]

    written = write([(to, to_out), (vo, vo_out), (mo, mo_out)], 0)
    for part in range(9):
        for q in range(3 * part, 3 * part + 3):
            ex, ey, ez = step_of(q)
            m = q // 3 + 5
            for x in range(8):
                row = PITCH * (x - ex + 1) + 8 - ey
                v = pop[q, pl.ds(row, 8), :]
                if ez == 1:
                    v = jnp.where(lane == 0, roll(zcol[0, pl.ds(row, 8), :], -m), roll(v, 1))
                elif ez == -1:
                    v = jnp.where(
                        lane == 127, roll(zcol[1, pl.ds(row, 8), :], 127 - m), roll(v, -1)
                    )
                staged[q, x] = v
        here = pl.ds(3 * part, 3)
        written += write([(staged.at[here], fo.at[here])], 3 + part)

    for copy in copies2:
        copy.wait_send()
    for copy in written:
        copy.wait()


def keep_kernel(a0, a1, a2, a3, b0, b1, b2, b3, t0, t1, t2, t3, sem):
    trips = []
    for part in range(3):
        here = pl.ds(9 * part, 9)
        trips.append((a0.at[here], t0.at[here], b0.at[here]))
    trips += [(a1, t1, b1), (a2, t2, b2), (a3, t3, b3)]
    copies = []
    for n, (a, t, _) in enumerate(trips):
        copy = pltpu.make_async_copy(a, t, sem.at[0, n])
        copy.start()
        copies.append(copy)
    outs = []
    for n, (_, t, b) in enumerate(trips):
        copies[n].wait()
        copy = pltpu.make_async_copy(t, b, sem.at[1, n])
        copy.start()
        outs.append(copy)
    for copy in outs:
        copy.wait()


def on_device(f, gt, gv, base, frac, vel, temp, rate, live):
    anywhere = pl.BlockSpec(memory_space=pl.ANY)

    def buffer(*shape, dtype=F32):
        return pltpu.VMEM(shape, dtype)

    results = (
        jax.ShapeDtypeStruct(f.shape, F32),
        jax.ShapeDtypeStruct(gt.shape, F32),
        jax.ShapeDtypeStruct(gv.shape, F32),
        jax.ShapeDtypeStruct((3, 1, PARCELS), F32),
    )
    inner = pl.pallas_call(
        gather_kernel,
        out_shape=results,
        in_specs=[anywhere] * 8 + [pl.BlockSpec(memory_space=pltpu.SMEM)],
        out_specs=[anywhere] * 4,
        scratch_shapes=[
            buffer(27, 10 * PITCH, 128),
            buffer(2, 10 * PITCH, 128),
            buffer(8, 8, 128),
            buffer(8, 8, 128),
            buffer(3, 1, PARCELS),
            buffer(27, 8, 8, 128),
            buffer(27, 8, 8, 128),
            buffer(8, 8, 128),
            buffer(8, 8, 128),
            buffer(3, 1, PARCELS, dtype=jnp.int32),
            buffer(3, 1, PARCELS),
            buffer(3, 1, PARCELS),
            buffer(1, PARCELS),
            buffer(1, PARCELS),
            buffer(528, 128),
            buffer(2, 40, 128),
            buffer(4, 8, 128),
            buffer(4, 8, 128),
            buffer(2, 8, 128),
            buffer(2, 9, 8, 128),
            buffer(2, 72, 128),
            buffer(2, 72, 128),
            buffer(2, 9, 8, 128),
            buffer(528, 384, dtype=BF16),
            buffer(384, PARCELS, dtype=BF16),
            buffer(256, PARCELS, dtype=BF16),
            buffer(128, PARCELS),
            buffer(8, PARCELS),
            buffer(8, PARCELS),
            buffer(8, PARCELS),
            buffer(8, PARCELS),
            buffer(8, PARCELS),
            buffer(128, 128),
            buffer(528, 128),
            buffer(128, 128),
            buffer(2, 104, 128),
            buffer(128, 128),
            buffer(2, 120, 128),
            buffer(2, 120, 128),
            buffer(2, 120, 128),
            buffer(2, 120, 128),
            buffer(4, 40, 128),
            buffer(4, 40, 128),
            buffer(2, 8, 128),
            buffer(2, 9, 8, 128),
            buffer(2, 9, 8, 128),
            buffer(528, 128),
            pltpu.SemaphoreType.DMA((8,)),
            pltpu.SemaphoreType.DMA((12,)),
            pltpu.SemaphoreType.DMA((2, 30)),
            pltpu.SemaphoreType.DMA((2, 30)),
        ],
        compiler_params=pltpu.CompilerParams(
            collective_id=0, has_side_effects=True, vmem_limit_bytes=56 * 1024 * 1024
        ),
    )(
        f,
        gt,
        gv,
        base.reshape(3, 1, PARCELS),
        frac.reshape(3, 1, PARCELS),
        vel.reshape(3, 1, PARCELS),
        temp.reshape(1, PARCELS),
        rate.reshape(1, PARCELS),
        live.reshape(1),
    )
    fo, to, vo, mo = pl.pallas_call(
        keep_kernel,
        out_shape=results,
        in_specs=[anywhere] * 4,
        out_specs=[anywhere] * 4,
        scratch_shapes=[
            buffer(*f.shape),
            buffer(*gt.shape),
            buffer(*gv.shape),
            buffer(3, 1, PARCELS),
            pltpu.SemaphoreType.DMA((2, 6)),
        ],
        compiler_params=pltpu.CompilerParams(vmem_limit_bytes=56 * 1024 * 1024),
    )(*inner)
    return fo, to, vo, mo.reshape(vel.shape)


def solution(mesh):
    placed = (
        P(None, "gx", "gy", "gz"),
        P("gx", "gy", "gz"),
        P("gx", "gy", "gz"),
        P(None, "gx", "gy", "gz", None),
        P(None, "gx", "gy", "gz", None),
        P(None, "gx", "gy", "gz", None),
        P("gx", "gy", "gz", None),
        P("gx", "gy", "gz", None),
        P("gx", "gy", "gz"),
    )
    return jax.shard_map(
        on_device,
        mesh=mesh,
        in_specs=placed,
        out_specs=(
            P(None, "gx", "gy", "gz"),
            P("gx", "gy", "gz"),
            P("gx", "gy", "gz"),
            P(None, "gx", "gy", "gz", None),
        ),
        check_vma=False,
    )
```

```python
import jax
import jax.numpy as jnp
from jax import lax
from jax.experimental import pallas as pl
from jax.experimental.pallas import tpu as pltpu
from jax.sharding import PartitionSpec as P

AXES = ("gx", "gy", "gz")
CHUNK = 2048
LOAD = 1024
PARCELS = 2048
PITCH = 24
F32 = jnp.float32
BF16 = jnp.bfloat16
MESH = pl.DeviceIdType.MESH
NT = (((1,), (1,)), ((), ()))


def step_of(q):
    return q // 9 - 1, q // 3 % 3 - 1, q % 3 - 1


def weight_of(q):
    value = 1.0
    for step in step_of(q):
        value = value * (2.0 / 3.0 if step == 0 else 1.0 / 6.0)
    return value


def roll(v, k):
    k = k % 128
    return pltpu.roll(v, k, 1) if k else v


def split(v):
    hi = v.astype(BF16)
    lo = (v - hi.astype(F32)).astype(BF16)
    return hi, lo


def side_index(dx, dy):
    return 3 * (dx + 1) + dy + 1


def place_of(x, y):
    if 0 <= x < 8:
        return (x, y) if 0 <= y < 8 else (10 if y < 0 else 11, x)
    if 0 <= y < 8:
        return 8 if x < 0 else 9, y
    return 12, 2 * (x > 0) + (y > 0)


SIGNS = [(1, 1), (1, -1), (-1, 1), (-1, -1)]
Y_UP = [9 * a + 6 + b for a in range(3) for b in range(3)]
Y_DOWN = [9 * a + b for a in range(3) for b in range(3)]


def push_of(q, s):
    push = s[4]
    e = step_of(q)
    for axis in range(3):
        if e[axis] == 1:
            push = push + 3.0 * s[axis]
        elif e[axis] == -1:
            push = push - 3.0 * s[axis]
    return weight_of(q) * push


def gather_kernel(
    f_in, gt_in, gv_in, base_in, frac_in, vel_in, temp_in, rate_in, live,
    fo, to_out, vo_out, mo_out,
    pop, zcol, to, vo, mo, staged,
    f, gt, gv, base, frac, vel, temp, rate,
    ext, ysend, csend, crecv, zsend, zrecv, ybsend, ybrecv, xbrecv,
    amat, wmat, pmat, plane_of, target, factor, sampled, edges, terms_of, left,
    dep, rim, zslot, rimf,
    x2send, x2recv, y2send, y2recv, c2send, c2recv, z2send, z2recv, zsum, src,
    in_sem, out_sem, send_sem, recv_sem,
):
    me = [lax.axis_index(a) for a in AXES]
    size = [lax.axis_size(a) for a in AXES]

    def device(d):
        return tuple(
            me[i] if d[i] == 0 else lax.rem(me[i] + (d[i] + size[i]), size[i]) for i in range(3)
        )

    around = [
        (dx, dy, dz)
        for dz in (-1, 1, 0)
        for dx in (-1, 1, 0)
        for dy in (-1, 1, 0)
        if (dx, dy, dz) != (0, 0, 0)
    ]
    around.sort(key=lambda d: -sum(map(abs, d)))
    barrier = pltpu.get_barrier_semaphore()
    for d in around:
        pl.semaphore_signal(barrier, inc=1, device_id=device(d), device_id_type=MESH)

    fetches = []
    for n, (a, b) in enumerate(
        [
            (f_in, f), (gt_in, gt), (gv_in, gv), (base_in, base), (frac_in, frac),
            (vel_in, vel), (temp_in, temp), (rate_in, rate),
        ]
    ):
        fetch = pltpu.make_async_copy(a, b, in_sem.at[n])
        fetch.start()
        fetches.append(fetch)

    def write(pairs, at):
        copies = []
        for n, (a, b) in enumerate(pairs):
            copy = pltpu.make_async_copy(a, b, out_sem.at[at + n])
            copy.start()
            copies.append(copy)
        return copies

    def exchange(phase, moves, at=0):
        copies = []
        for n, (a, b, d) in enumerate(moves, start=at):
            copy = pltpu.make_async_remote_copy(
                src_ref=a,
                dst_ref=b,
                send_sem=send_sem.at[phase, n],
                recv_sem=recv_sem.at[phase, n],
                device_id=device(d),
                device_id_type=MESH,
            )
            copy.start()
            copies.append(copy)
        return copies

    lane = lax.broadcasted_iota(jnp.int32, (8, 128), 1)
    sub = lax.broadcasted_iota(jnp.int32, (8, 128), 0)
    low_lane = lane & 7
    group = lane >> 3

    def skew(v, amount):
        for bit in range(3):
            v = jnp.where((sub >> bit) & 1 == 1, roll(v, amount << bit), v)
        return v

    def spread_row(v, row):
        return jnp.broadcast_to(v[row : row + 1], (8, 128))

    for fetch in fetches[:3]:
        fetch.wait()

    def moment_step(x, _):
        at = pl.multiple_of(x * 40, 8)
        to_row = pl.multiple_of(PITCH * (x + 1) + 8, 8)
        pops = [f[q, x] for q in range(27)]
        total = pops[0]
        for q in range(1, 27):
            total = total + pops[q]
        u = []
        for axis in range(3):
            up = None
            for q in range(27):
                e = step_of(q)[axis]
                if e == 1:
                    up = pops[q] if up is None else up + pops[q]
                elif e == -1:
                    up = -pops[q] if up is None else up - pops[q]
            u.append(up / total)
            ext[pl.ds(at + 8 * axis, 8), :] = u[axis]
        ext[pl.ds(at + 24, 8), :] = gt[x]
        ext[pl.ds(at + 32, 8), :] = gv[x]
        rest = 1.0 - 1.5 * (u[0] * u[0] + u[1] * u[1] + u[2] * u[2])
        for q in range(27):
            e = step_of(q)
            along = None
            for axis in range(3):
                if e[axis] != 0:
                    term = u[axis] if e[axis] == 1 else -u[axis]
                    along = term if along is None else along + term
            inner = rest if along is None else rest + along * (3.0 + 4.5 * along)
            equil = (1.25 * weight_of(q)) * total * inner
            pop[q, pl.ds(to_row, 8), :] = equil - 0.25 * pops[q]
        return 0

    lax.fori_loop(0, 8, moment_step, 0)

    for c in range(5):
        for side in range(2):
            ysend[side, pl.ds(8 * c, 8), :] = ext[pl.ds(8 * c + 7 * side, 8, stride=40), :]
    for k in range(9):
        ybsend[0, pl.ds(8 * k, 8), :] = pop[Y_DOWN[k], pl.ds(PITCH + 8, 8, stride=PITCH), :]
        ybsend[1, pl.ds(8 * k, 8), :] = pop[Y_UP[k], pl.ds(PITCH + 15, 8, stride=PITCH), :]
    for j, (sx, sy) in enumerate(SIGNS):
        x, y = 7 if sx == 1 else 0, 7 if sy == 1 else 0
        csend[j, pl.ds(0, 5), :] = ext[pl.ds(40 * x + y, 5, stride=8), :]
        for k in range(3):
            q = 9 * (sx + 1) + 3 * (sy + 1) + k
            csend[j, pl.ds(5 + k, 1), :] = pop[q, pl.ds(PITCH * (x + 1) + 8 + y, 1), :]

    def z_pack(x, carry):
        low, high = carry
        at = pl.multiple_of(x * 40, 8)
        row = pl.multiple_of(PITCH * (x + 1) + 8, 8)
        near_low = jnp.zeros((8, 128), F32)
        near_high = jnp.zeros((8, 128), F32)
        for v in range(14):
            if v < 5:
                t_low = t_high = roll(ext[pl.ds(at + 8 * v, 8), :], v + 1)
            else:
                t_low = roll(pop[3 * (v - 5), pl.ds(row, 8), :], v + 1)
                t_high = roll(pop[3 * (v - 5) + 2, pl.ds(row, 8), :], v + 1)
            near_low = jnp.where(lane == v + 1, t_low, near_low)
            near_high = jnp.where(lane == v, t_high, near_high)
        return (
            low + pltpu.roll(near_low, 16 * x, 1),
            high + pltpu.roll(near_high, 16 * x, 1),
        )

    zero8 = jnp.zeros((8, 128), F32)
    low, high = lax.fori_loop(0, 8, z_pack, (zero8, zero8))
    zsend[0] = low
    zsend[1] = high

    for fetch in fetches[3:]:
        fetch.wait()
    alive = live[0]

    def weight_step(n, _):
        first = pl.multiple_of(n * CHUNK, CHUNK)
        here = pl.ds(first, CHUNK)
        bx, by, bz = (base[d, :, here] for d in range(3))
        fx, fy, fz = (frac[d, :, here] for d in range(3))
        rows8 = lax.broadcasted_iota(jnp.int32, (8, CHUNK), 0)

        def hat(cells, b, fr):
            return jnp.where(cells == b, 1.0 - fr, jnp.where(cells == b + 1, fr, 0.0))

        wz_hi, wz_lo = split(hat(lax.broadcasted_iota(jnp.int32, (128, CHUNK), 0), bz, fz))
        wmat[pl.ds(0, 128), here] = wz_hi
        wmat[pl.ds(128, 128), here] = wz_lo
        wmat[pl.ds(256, 128), here] = wz_hi
        edges[pl.ds(0, 1), here] = jnp.where(bz == -1, 1.0 - fz, 0.0)
        edges[pl.ds(1, 1), here] = jnp.where(bz == 127, fz, 0.0)
        edges[pl.ds(2, 1), here] = hat(0, bz, fz)
        edges[pl.ds(3, 1), here] = hat(127, bz, fz)

        wx8 = hat(rows8, bx, fx)
        wy8 = hat(rows8, by, fy)
        x_low = jnp.where(bx == -1, 1.0 - fx, 0.0)
        x_high = jnp.where(bx == 7, fx, 0.0)
        y_low = jnp.where(by == -1, 1.0 - fy, 0.0)
        y_high = jnp.where(by == 7, fy, 0.0)
        plane = [wx8[x : x + 1] * wy8 for x in range(8)]
        plane += [x_low * wy8, x_high * wy8, y_low * wx8, y_high * wx8]
        edge = jnp.where(rows8 < 2, x_low, x_high) * jnp.where((rows8 & 1) == 0, y_low, y_high)
        plane.append(jnp.where(rows8 < 4, edge, 0.0))
        plane = jnp.concatenate(plane + [jnp.zeros((24, CHUNK), F32)], axis=0)
        plane_of[:, here] = plane
        plane_hi, plane_lo = split(plane)
        pmat[pl.ds(0, 128), here] = plane_hi
        pmat[pl.ds(128, 128), here] = plane_lo

        slot = lax.broadcasted_iota(jnp.int32, (1, CHUNK), 1) + first
        own_temp = temp[:, here]
        target[:, here] = jnp.concatenate(
            [vel[d, :, here] for d in range(3)]
            + [own_temp, 0.05 * jnp.exp(3.0 * (own_temp - 0.5)), jnp.zeros((3, CHUNK), F32)],
            axis=0,
        )
        scale = jnp.where(rows8 < 3, 2.0, jnp.where(rows8 < 5, 1.0, 0.0))
        factor[:, here] = jnp.where(slot < alive, rate[:, here], 0.0) * scale
        return 0


    def matrix_step(n, _):
        at = pl.multiple_of(n * 16, 16)
        hi, lo = split(ext[pl.ds(at, 16), :])
        amat[pl.ds(at, 16), pl.ds(0, 128)] = hi
        amat[pl.ds(at, 16), pl.ds(128, 128)] = hi
        amat[pl.ds(at, 16), pl.ds(256, 128)] = lo
        return 0

    pl.semaphore_wait(barrier, 26)

    def z_moves(send, recv):
        return [
            (
                send.at[(1 + dz) // 2],
                recv.at[(1 - dz) // 2, side_index(-dx, -dy)],
                (dx, dy, dz),
            )
            for (dx, dy, dz) in around
            if dz != 0
        ]

    def corner_moves(send, recv):
        return [(send.at[j], recv.at[j], (sx, sy, 0)) for j, (sx, sy) in enumerate(SIGNS)]

    copies1 = exchange(
        0,
        corner_moves(csend, crecv)
        + [
            (ysend.at[1], ext.at[pl.ds(400, 40)], (0, 1, 0)),
            (ysend.at[0], ext.at[pl.ds(440, 40)], (0, -1, 0)),
            (ext.at[pl.ds(280, 40)], ext.at[pl.ds(320, 40)], (1, 0, 0)),
            (ext.at[pl.ds(0, 40)], ext.at[pl.ds(360, 40)], (-1, 0, 0)),
        ],
    )
    copies_z = exchange(0, z_moves(zsend, zrecv), 8)
    copies_b = exchange(
        0,
        [
            (ybsend.at[1], ybrecv.at[0], (0, 1, 0)),
            (ybsend.at[0], ybrecv.at[1], (0, -1, 0)),
            (pop.at[pl.ds(18, 9), pl.ds(PITCH * 8 + 8, 8)], xbrecv.at[0], (1, 0, 0)),
            (pop.at[pl.ds(0, 9), pl.ds(PITCH + 8, 8)], xbrecv.at[1], (-1, 0, 0)),
        ],
        26,
    )

    lax.fori_loop(0, PARCELS // CHUNK, weight_step, 0)
    lax.fori_loop(0, 20, matrix_step, 0)

    def sample(first_slot, last_slot, along, here, off):
        sums = []
        for c in range(5):
            total = None
            for s in range(first_slot, last_slot):
                at = 8 * (5 * s + c) - off
                term = along[at : at + 8] * plane_of[pl.ds(8 * s, 8), here]
                total = term if total is None else total + term
            sums.append(jnp.sum(total, axis=0, keepdims=True))
        return jnp.concatenate(sums + [jnp.zeros((3, CHUNK), F32)], axis=0)

    def own_step(n, _):
        here = pl.ds(pl.multiple_of(n * CHUNK, CHUNK), CHUNK)
        along = jnp.dot(amat[pl.ds(0, 320), :], wmat[:, here], preferred_element_type=F32)
        sampled[:, here] = sample(0, 8, along, here, 0)
        return 0

    lax.fori_loop(0, PARCELS // CHUNK, own_step, 0)
    dep[...] = jnp.zeros_like(dep)
    rim[...] = jnp.zeros_like(rim)
    left[...] = jnp.zeros_like(left)

    for copy in copies1:
        copy.wait_recv()

    for j in range(4):
        ext[pl.ds(480 + j, 5, stride=8), :] = crecv[j, pl.ds(0, 5), :]
    for c in range(5):
        ext[pl.ds(480 + 8 * c + 4, 4), :] = jnp.zeros((4, 128), F32)
    ext[pl.ds(520, 8), :] = zero8

    lax.fori_loop(20, 33, matrix_step, 0)

    def term_step(n, _):
        here = pl.ds(pl.multiple_of(n * CHUNK, CHUNK), CHUNK)
        along = jnp.dot(amat[pl.ds(320, 208), :], wmat[:, here], preferred_element_type=F32)
        got = sampled[:, here] + sample(8, 13, along, here, 320)
        terms_of[:, here] = factor[:, here] * (target[:, here] - got)
        return 0

    def load_step(n, _):
        here = pl.ds(pl.multiple_of(n * LOAD, LOAD), LOAD)
        terms = terms_of[:, here]
        load = [
            plane_of[pl.ds(8 * s, 8), here] * terms[c : c + 1] for s in range(13) for c in range(5)
        ]
        load.append(jnp.zeros((8, LOAD), F32))
        load_hi, load_lo = split(jnp.concatenate(load, axis=0))
        got_hi = lax.dot_general(
            load_hi, wmat[pl.ds(0, 256), here], NT, preferred_element_type=F32
        )
        got_lo = lax.dot_general(
            load_lo, wmat[pl.ds(0, 128), here], NT, preferred_element_type=F32
        )
        dep[...] += got_hi[:, :128] + got_hi[:, 128:] + got_lo
        return 0

    lax.fori_loop(0, PARCELS // CHUNK, term_step, 0)
    lax.fori_loop(0, PARCELS // LOAD // 2, load_step, 0)

    for copy in copies_z:
        copy.wait_recv()
    rimf[pl.ds(104, 24), :] = jnp.zeros((24, 128), F32)
    for s in range(13):
        sides = []
        for side in range(2):
            if s < 8:
                t = roll(zrecv[side, side_index(0, 0)], -16 * s - side)
            elif s < 10:
                dx = (-1, 1)[s - 8]
                t = roll(zrecv[side, side_index(dx, 0)], -(112, 0)[s - 8] - side)
            elif s < 12:
                dy = (-1, 1)[s - 10]
                t = spread_row(zrecv[side, side_index(0, dy)], (7, 0)[s - 10])
                t = skew(roll(t, -side), -16)
            else:
                t = zero8
                for j in range(4):
                    got = zrecv[side, side_index((-1, 1)[j // 2], (-1, 1)[j % 2])]
                    got = roll(got, -(112, 0)[j // 2] - side)
                    t = jnp.where(sub == j, spread_row(got, (7, 0)[j % 2]), t)
            zslot[side, pl.ds(8 * s, 8), :] = t
            sides.append(t)
        both = jnp.where(lane < 8, sides[0], roll(sides[1], 8))
        rimf[pl.ds(8 * s, 8), :] = jnp.where((lane < 16) & (low_lane < 5), both, 0.0)
    fields_hi, fields_lo = split(jnp.transpose(rimf[...])[:16])
    rim_left = jnp.concatenate(
        [
            jnp.concatenate([fields_hi, fields_hi], axis=1),
            jnp.concatenate([fields_lo, fields_lo], axis=1),
        ],
        axis=0,
    )

    def layer_step(n, _):
        here = pl.ds(pl.multiple_of(n * CHUNK, CHUNK), CHUNK)
        below, above, first, last = (edges[pl.ds(k, 1), here] for k in range(4))
        ends = jnp.dot(rim_left, pmat[:, here], preferred_element_type=F32)
        ends = ends[:16] + ends[16:]
        terms = terms_of[:, here] - factor[:, here] * (below * ends[:8] + above * ends[8:])
        for d in range(3):
            mo[d, :, here] = target[pl.ds(d, 1), here] - 0.5 * terms[d : d + 1]
        left_hi, left_lo = split(
            jnp.concatenate([terms * w for w in (below, above, first, last)], axis=0)
        )
        got_hi = lax.dot_general(left_hi, pmat[:, here], NT, preferred_element_type=F32)
        got_lo = lax.dot_general(
            left_lo, pmat[pl.ds(0, 128), here], NT, preferred_element_type=F32
        )
        rim[pl.ds(0, 32), :] += got_hi[:, :128] + got_hi[:, 128:] + got_lo
        return 0

    lax.fori_loop(0, PARCELS // CHUNK, layer_step, 0)

    layer = [[rim[pl.ds(8 * k + c, 1), :] for c in range(5)] for k in range(4)]
    up = [[t[4] + 3.0 * t[2], t[0], t[1]] for t in layer]
    down = [[t[4] - 3.0 * t[2], t[0], t[1]] for t in layer]
    rows = layer[0] + down[2] + layer[1] + up[3] + up[0] + [None] + down[1] + [None]
    rows += [t for c in range(5) for t in (layer[3][c], layer[2][c])]
    for k, row in enumerate(rows):
        if row is not None:
            left[pl.ds(k, 1), :] = row
    rimf[...] = jnp.transpose(left[...])
    low = zero8
    high = zero8
    ring = zero8
    for s in range(13):
        v = rimf[pl.ds(8 * s, 8), :]
        mine = group == s
        low = jnp.where(mine, roll(v, 8 * s), low)
        high = jnp.where(mine, roll(v, 8 * s - 8), high)
        ring = jnp.where(mine, roll(v, 8 * s - 16), ring)
    z2send[0] = low
    z2send[1] = high
    copies2 = exchange(1, z_moves(z2send, z2recv))

    lax.fori_loop(PARCELS // LOAD // 2, PARCELS // LOAD, load_step, 0)

    outer = (lane == 0) | (lane == 127)
    for s in range(13):
        v = rimf[pl.ds(8 * s, 8), :]
        for c in range(5):
            here = pl.ds(8 * (5 * s + c), 8)
            dep[here, :] = jnp.where(outer, roll(v, -25 - 2 * c), dep[here, :])

    def fill(send, blocks, singles, at):
        for n, block in enumerate(blocks):
            send[pl.ds(40 * n, 40), :] = block
        for n, (x, y) in enumerate(singles):
            s, r = place_of(x, y)
            send[pl.ds(at + 8 * n, 5), :] = dep[pl.ds(40 * s + r, 5, stride=8), :]
        send[pl.ds(at + 32, 8), :] = ring

    far = {1: (7, 8), -1: (0, -1)}
    for n, sign in enumerate((-1, 1)):
        a, b = far[sign]
        fill(
            x2send.at[n],
            [dep[pl.ds(40 * place_of(x, 0)[0], 40), :] for x in (a, b)],
            [(a, -1), (a, 8), (b, -1), (b, 8)],
            80,
        )
        for c in range(5):
            y2send[n, pl.ds(8 * c, 8), :] = dep[pl.ds(8 * c + a, 8, stride=40), :]
        y2send[n, pl.ds(40, 40), :] = dep[pl.ds(40 * place_of(0, b)[0], 40), :]
        fill(y2send.at[n], [], [(-1, a), (8, a), (-1, b), (8, b)], 80)
    for j, (sx, sy) in enumerate(SIGNS):
        fill(c2send.at[j], [], [(x, y) for x in far[sx] for y in far[sy]], 0)

    copies2 += exchange(
        1,
        corner_moves(c2send, c2recv)
        + [
            (y2send.at[1], y2recv.at[0], (0, 1, 0)),
            (y2send.at[0], y2recv.at[1], (0, -1, 0)),
            (x2send.at[1], x2recv.at[0], (1, 0, 0)),
            (x2send.at[0], x2recv.at[1], (-1, 0, 0)),
        ],
        18,
    )
    for copy in copies1 + copies_z + copies_b:
        copy.wait_send()
    for copy in copies_b:
        copy.wait_recv()
    for copy in copies2:
        copy.wait_recv()

    rings = {(0, 0): ring}
    for n, sign in enumerate((-1, 1)):
        rings[sign, 0] = x2recv[n, pl.ds(112, 8), :]
        rings[0, sign] = y2recv[n, pl.ds(112, 8), :]
    for j, (sx, sy) in enumerate(SIGNS):
        rings[-sx, -sy] = c2recv[j, pl.ds(32, 8), :]
    for (dx, dy), ring_at in rings.items():
        n = side_index(dx, dy)
        for side in range(2):
            zsum[side, n] = z2recv[side, n] + jnp.where(
                low_lane >= 5, roll(ring_at, (5, 1)[side]), 0.0
            )
    layers = []
    for side in range(2):
        acc = zsum[side, side_index(0, 0)]
        by_shift = {}

        def move(shift, mask, v):
            v = jnp.where(mask, v, 0.0)
            by_shift[shift] = by_shift[shift] + v if shift in by_shift else v

        for dx, dy in rings:
            if dx == 0 and dy == 0:
                continue
            n = side_index(dx, dy)
            xs = {0: range(-1, 9), -1: (-1, 0), 1: (7, 8)}[dx]
            ys = {0: range(-1, 9), -1: (-1, 0), 1: (7, 8)}[dy]
            singles = [(x, y) for x in xs for y in ys]
            if dy == 0:
                for x in xs:
                    s = place_of(x, 0)[0]
                    s_from = place_of(x - 8 * dx, 0)[0]
                    move(s - s_from, group == s_from, zsum[side, n])
                singles = [(x, y) for (x, y) in singles if y in (-1, 8)]
            if dx == 0:
                row, s, s_from = (7, 10, 11) if dy == -1 else (0, 11, 10)
                line = jnp.broadcast_to(zsum[side, n, pl.ds(row, 1), :], (8, 128))
                move(s, group == 0, skew(line, -8))
                rows = jnp.where(group == 0, roll(zsum[side, n], -8 * s_from), 0.0)
                rows = jnp.sum(skew(rows, 8), axis=0, keepdims=True)
                acc += jnp.where(sub == 7 - row, rows, 0.0)
                singles = [(x, y) for (x, y) in singles if x in (-1, 8)]
            for x, y in singles:
                s, r = place_of(x, y)
                s_from, r_from = place_of(x - 8 * dx, y - 8 * dy)
                line = jnp.broadcast_to(zsum[side, n, pl.ds(r_from, 1), :], (8, 128))
                move(s - s_from, (group == s_from) & (sub == r), line)
        for shift, v in by_shift.items():
            acc += roll(v, 8 * shift)
        layers.append(acc)

    for s in range(13):
        for c in range(5):
            at = 8 * (5 * s + c)
            k = 8 * s + c
            v = dep[pl.ds(at, 8), :]
            v += jnp.where(lane == 0, roll(layers[0], -k), 0.0)
            v += jnp.where(lane == 127, roll(layers[1], 127 - k), 0.0)
            src[pl.ds(at, 8), :] = v
    def take(recv, singles, at):
        for n, (x, y) in enumerate(singles):
            s, r = place_of(x, y)
            src[pl.ds(40 * s + r, 5, stride=8), :] += recv[pl.ds(at + 8 * n, 5), :]

    near = {-1: (-1, 0), 1: (8, 7)}
    for n, sign in enumerate((-1, 1)):
        a, b = near[sign]
        for m, x in enumerate((a, b)):
            src[pl.ds(40 * place_of(x, 0)[0], 40), :] += x2recv[n, pl.ds(40 * m, 40), :]
        take(x2recv.at[n], [(a, -1), (a, 8), (b, -1), (b, 8)], 80)
        src[pl.ds(40 * place_of(0, a)[0], 40), :] += y2recv[n, pl.ds(0, 40), :]
        for c in range(5):
            src[pl.ds(8 * c + b, 8, stride=40), :] += y2recv[n, pl.ds(40 + 8 * c, 8), :]
        take(y2recv.at[n], [(-1, a), (8, a), (-1, b), (8, b)], 80)
    for j, (sx, sy) in enumerate(SIGNS):
        take(c2recv.at[j], [(x, y) for x in near[-sx] for y in near[-sy]], 0)

    def push_step(x, _):
        at = pl.multiple_of(x * 40, 8)
        to_row = pl.multiple_of(PITCH * (x + 1) + 8, 8)
        s = [src[pl.ds(at + 8 * c, 8), :] for c in range(5)]
        to[x] = gt[x] + s[3]
        vo[x] = gv[x] + s[4]
        for q in range(27):
            pop[q, pl.ds(to_row, 8), :] += push_of(q, s)
        return 0

    lax.fori_loop(0, 8, push_step, 0)
    s8, s9, s10, s11, s12 = (
        [src[pl.ds(8 * (5 * s + c), 8), :] for c in range(5)] for s in range(8, 13)
    )
    for k in range(9):
        pop[18 + k, pl.ds(8, 8), :] = xbrecv[0, k] + push_of(18 + k, s8)
        pop[k, pl.ds(PITCH * 9 + 8, 8), :] = xbrecv[1, k] + push_of(k, s9)
        q = Y_UP[k]
        pop[q, pl.ds(PITCH + 7, 8, stride=PITCH), :] = (
            ybrecv[0, pl.ds(8 * k, 8), :] + push_of(q, s10)
        )
        q = Y_DOWN[k]
        pop[q, pl.ds(PITCH + 16, 8, stride=PITCH), :] = (
            ybrecv[1, pl.ds(8 * k, 8), :] + push_of(q, s11)
        )
    for j, (sx, sy) in enumerate(SIGNS):
        row = PITCH * (0, 9)[j // 2] + (7, 16)[j % 2]
        for k in range(3):
            q = 9 * (sx + 1) + 3 * (sy + 1) + k
            total = crecv[j, pl.ds(5 + k, 1), :] + push_of(q, s12)[j : j + 1]
            pop[q, pl.ds(row, 1), :] = total

    written = write([(to, to_out), (vo, vo_out), (mo, mo_out)], 0)

    def run(ez):
        for m in range(9):
            q = 3 * m + 1 + ez
            ex, ey, _ = step_of(q)
            for x in range(8):
                row = PITCH * (x - ex + 1) + 8 - ey
                v = pop[q, pl.ds(row, 8), :]
                if ez == 1:
                    end = roll(zcol[0, pl.ds(row, 8), :], -m - 5)
                    v = jnp.where(lane == 0, end, roll(v, 1))
                elif ez == -1:
                    end = roll(zcol[1, pl.ds(row, 8), :], 122 - m)
                    v = jnp.where(lane == 127, end, roll(v, -1))
                staged[q, x] = v
            written.extend(write([(staged.at[q], fo.at[q])], 3 + q))

    run(0)

    number = lane - 5
    used = (number >= 0) & (number < 9)
    step_x = jnp.where(number < 3, -1.0, jnp.where(number < 6, 0.0, 1.0))
    third = jnp.where(number < 3, number, jnp.where(number < 6, number - 3, number - 6))
    step_y = jnp.where(third == 0, -1.0, jnp.where(third == 1, 0.0, 1.0))
    share = jnp.where(step_x == 0.0, 2.0 / 3.0, 1.0 / 6.0)
    share = share * jnp.where(step_y == 0.0, 2.0 / 3.0, 1.0 / 6.0)
    share = jnp.where(used, share * (1.0 / 6.0), 0.0)
    share_x = 3.0 * share * step_x
    share_y = 3.0 * share * step_y
    for side in range(2):
        for s in range(13):
            three = [
                jnp.broadcast_to(layers[side][:, 8 * s + v : 8 * s + v + 1], (8, 128))
                for v in (5, 6, 7)
            ]
            t = zslot[side, pl.ds(8 * s, 8), :]
            t = t + share * three[0] + share_x * three[1] + share_y * three[2]
            if s < 8:
                zcol[side, pl.ds(PITCH * (s + 1) + 8, 8), :] = t
            elif s < 10:
                zcol[side, pl.ds(PITCH * (0, 9)[s - 8] + 8, 8), :] = t
            elif s < 12:
                zcol[side, pl.ds(PITCH + (7, 16)[s - 10], 8, stride=PITCH), :] = t
            else:
                for j in range(4):
                    row = PITCH * (0, 9)[j // 2] + (7, 16)[j % 2]
                    zcol[side, pl.ds(row, 1), :] = t[j : j + 1]

    run(1)
    run(-1)

    for copy in copies2:
        copy.wait_send()
    for copy in written:
        copy.wait()


def keep_kernel(a0, a1, a2, a3, b0, b1, b2, b3, t0, t1, t2, t3, sem):
    trips = []
    for part in range(3):
        here = pl.ds(9 * part, 9)
        trips.append((a0.at[here], t0.at[here], b0.at[here]))
    trips += [(a1, t1, b1), (a2, t2, b2), (a3, t3, b3)]
    copies = []
    for n, (a, t, _) in enumerate(trips):
        copy = pltpu.make_async_copy(a, t, sem.at[0, n])
        copy.start()
        copies.append(copy)
    outs = []
    for n, (_, t, b) in enumerate(trips):
        copies[n].wait()
        copy = pltpu.make_async_copy(t, b, sem.at[1, n])
        copy.start()
        outs.append(copy)
    for copy in outs:
        copy.wait()


def on_device(f, gt, gv, base, frac, vel, temp, rate, live):
    anywhere = pl.BlockSpec(memory_space=pl.ANY)

    def buffer(*shape, dtype=F32):
        return pltpu.VMEM(shape, dtype)

    results = (
        jax.ShapeDtypeStruct(f.shape, F32),
        jax.ShapeDtypeStruct(gt.shape, F32),
        jax.ShapeDtypeStruct(gv.shape, F32),
        jax.ShapeDtypeStruct((3, 1, PARCELS), F32),
    )
    inner = pl.pallas_call(
        gather_kernel,
        out_shape=results,
        in_specs=[anywhere] * 8 + [pl.BlockSpec(memory_space=pltpu.SMEM)],
        out_specs=[anywhere] * 4,
        scratch_shapes=[
            buffer(27, 10 * PITCH, 128),
            buffer(2, 10 * PITCH, 128),
            buffer(8, 8, 128),
            buffer(8, 8, 128),
            buffer(3, 1, PARCELS),
            buffer(27, 8, 8, 128),
            buffer(27, 8, 8, 128),
            buffer(8, 8, 128),
            buffer(8, 8, 128),
            buffer(3, 1, PARCELS, dtype=jnp.int32),
            buffer(3, 1, PARCELS),
            buffer(3, 1, PARCELS),
            buffer(1, PARCELS),
            buffer(1, PARCELS),
            buffer(528, 128),
            buffer(2, 40, 128),
            buffer(4, 8, 128),
            buffer(4, 8, 128),
            buffer(2, 8, 128),
            buffer(2, 9, 8, 128),
            buffer(2, 72, 128),
            buffer(2, 72, 128),
            buffer(2, 9, 8, 128),
            buffer(528, 384, dtype=BF16),
            buffer(384, PARCELS, dtype=BF16),
            buffer(256, PARCELS, dtype=BF16),
            buffer(128, PARCELS),
            buffer(8, PARCELS),
            buffer(8, PARCELS),
            buffer(8, PARCELS),
            buffer(8, PARCELS),
            buffer(8, PARCELS),
            buffer(128, 128),
            buffer(528, 128),
            buffer(128, 128),
            buffer(2, 104, 128),
            buffer(128, 128),
            buffer(2, 120, 128),
            buffer(2, 120, 128),
            buffer(2, 120, 128),
            buffer(2, 120, 128),
            buffer(4, 40, 128),
            buffer(4, 40, 128),
            buffer(2, 8, 128),
            buffer(2, 9, 8, 128),
            buffer(2, 9, 8, 128),
            buffer(528, 128),
            pltpu.SemaphoreType.DMA((8,)),
            pltpu.SemaphoreType.DMA((30,)),
            pltpu.SemaphoreType.DMA((2, 30)),
            pltpu.SemaphoreType.DMA((2, 30)),
        ],
        compiler_params=pltpu.CompilerParams(
            collective_id=0, has_side_effects=True, vmem_limit_bytes=56 * 1024 * 1024
        ),
    )(
        f,
        gt,
        gv,
        base.reshape(3, 1, PARCELS),
        frac.reshape(3, 1, PARCELS),
        vel.reshape(3, 1, PARCELS),
        temp.reshape(1, PARCELS),
        rate.reshape(1, PARCELS),
        live.reshape(1),
    )
    fo, to, vo, mo = pl.pallas_call(
        keep_kernel,
        out_shape=results,
        in_specs=[anywhere] * 4,
        out_specs=[anywhere] * 4,
        scratch_shapes=[
            buffer(*f.shape),
            buffer(*gt.shape),
            buffer(*gv.shape),
            buffer(3, 1, PARCELS),
            pltpu.SemaphoreType.DMA((2, 6)),
        ],
        compiler_params=pltpu.CompilerParams(vmem_limit_bytes=56 * 1024 * 1024),
    )(*inner)
    return fo, to, vo, mo.reshape(vel.shape)


def solution(mesh):
    placed = (
        P(None, "gx", "gy", "gz"),
        P("gx", "gy", "gz"),
        P("gx", "gy", "gz"),
        P(None, "gx", "gy", "gz", None),
        P(None, "gx", "gy", "gz", None),
        P(None, "gx", "gy", "gz", None),
        P("gx", "gy", "gz", None),
        P("gx", "gy", "gz", None),
        P("gx", "gy", "gz"),
    )
    return jax.shard_map(
        on_device,
        mesh=mesh,
        in_specs=placed,
        out_specs=(
            P(None, "gx", "gy", "gz"),
            P("gx", "gy", "gz"),
            P("gx", "gy", "gz"),
            P(None, "gx", "gy", "gz", None),
        ),
        check_vma=False,
    )
```
